32 devices in a mesh: dp: 8 (over z, x), mp: 4 (over y, core).
Axes of the slice: x: 2, y: 2, z: 4, core: 2. Of those that a mesh axis runs over, the one named last changes fastest.
Arguments:
- image: bfloat16 [16, 16, 64, 2048], P(None, 'mp', 'dp'), may hold values from -6 to 6
- text: bfloat16 [16, 1024, 768], P('dp'), may hold values from -6 to 6
- cotangent: bfloat16 [16, 1024, 768], P('dp'), may hold values from -6 to 6
- segments: int32 [16, 1024], P('dp'), may hold values from 0 to 3, never falling along the last dimension, each value on 1 to 512 neighbouring positions
- boxes: int32 [16, 2, 1024], P('dp'), may hold values from 0 to 31
- reduce_weight: float32 [2048, 512], P(('dp', 'mp')), may hold values from -0.125 to 0.125
- reduce_weight_rows: float32 [2048], P(('dp', 'mp')), may hold values from 163.84 to 1228.8
- reduce_weight_cols: float32 [512], replicated, may hold values from 163.84 to 1228.8
- spatial_weight: float32 [4608, 512], P(('dp', 'mp')), may hold values from -0.09375 to 0.09375
- spatial_weight_rows: float32 [4608], P(('dp', 'mp')), may hold values from 163.84 to 1228.8
- spatial_weight_cols: float32 [512], replicated, may hold values from 163.84 to 1228.8
- expand_weight: float32 [512, 2048], P(('dp', 'mp')), may hold values from -0.25 to 0.25
- expand_weight_rows: float32 [512], P(('dp', 'mp')), may hold values from 163.84 to 1228.8
- expand_weight_cols: float32 [2048], replicated, may hold values from 163.84 to 1228.8
- visual_proj: float32 [2048, 768], P(('dp', 'mp')), may hold values from -0.125 to 0.125
- visual_proj_rows: float32 [2048], P(('dp', 'mp')), may hold values from 1638.4 to 12288
- visual_proj_cols: float32 [768], replicated, may hold values from 1638.4 to 12288
- attn_in: float32 [2, 3, 768, 768], P(None, None, 'dp', 'mp'), may hold values from -0.21875 to 0.21875
- attn_in_rows: float32 [2, 3, 768], P(None, None, 'dp'), may hold values from 491.52 to 3686.4
- attn_in_cols: float32 [2, 3, 768], P(None, None, 'mp'), may hold values from 491.52 to 3686.4
- attn_out: float32 [2, 768, 768], P(None, 'mp', 'dp'), may hold values from -1.25 to 1.25
- attn_out_rows: float32 [2, 768], P(None, 'mp'), may hold values from 32.768 to 245.76
- attn_out_cols: float32 [2, 768], P(None, 'dp'), may hold values from 32.768 to 245.76
- ffn_up: float32 [768, 3072], P('dp', 'mp'), may hold values from -0.21875 to 0.21875
- ffn_up_rows: float32 [768], P('dp'), may hold values from 819.2 to 6144
- ffn_up_cols: float32 [3072], P('mp'), may hold values from 819.2 to 6144
- ffn_down: float32 [3072, 768], P('mp', 'dp'), may hold values from -0.109375 to 0.109375
- ffn_down_rows: float32 [3072], P('mp'), may hold values from 1310.72 to 9830.4
- ffn_down_cols: float32 [768], P('dp'), may hold values from 1310.72 to 9830.4
- norm_params: float32 [5, 768], replicated, may hold values from 0.1 to 1.9
- norm_moment: float32 [5, 768], replicated, may hold values from 3276.8 to 24576
- up_bias: float32 [3072], replicated, may hold values from -1.8 to 1.8
- up_moment: float32 [3072], replicated, may hold values from 819.2 to 6144
- tables: float32 [2, 33, 12], replicated, may hold values from -4 to 4
- table_moment: float32 [2, 33, 12], replicated, may hold values from 327.68 to 2457.6
Outputs:
- out: bfloat16 [16, 1024, 768], P('dp')
- grad_text: float32 [16, 1024, 768], P('dp', 'mp')
- grad_image: float32 [16, 16, 64, 2048], P(None, 'mp', 'dp')
- reduce_weight_grad: float32 [2048, 512], P(('dp', 'mp'))
- reduce_weight_next: float32 [2048, 512], P(('dp', 'mp'))
- reduce_weight_rows_next: float32 [2048], P(('dp', 'mp'))
- reduce_weight_cols_next: float32 [512], replicated
- reduce_weight_low: bfloat16 [2048, 512], P(('dp', 'mp'))
- spatial_weight_grad: float32 [4608, 512], P(('dp', 'mp'))
- spatial_weight_next: float32 [4608, 512], P(('dp', 'mp'))
- spatial_weight_rows_next: float32 [4608], P(('dp', 'mp'))
- spatial_weight_cols_next: float32 [512], replicated
- spatial_weight_low: bfloat16 [4608, 512], P(('dp', 'mp'))
- expand_weight_grad: float32 [512, 2048], P(('dp', 'mp'))
- expand_weight_next: float32 [512, 2048], P(('dp', 'mp'))
- expand_weight_rows_next: float32 [512], P(('dp', 'mp'))
- expand_weight_cols_next: float32 [2048], replicated
- expand_weight_low: bfloat16 [512, 2048], P(('dp', 'mp'))
- visual_proj_grad: float32 [2048, 768], P(('dp', 'mp'))
- visual_proj_next: float32 [2048, 768], P(('dp', 'mp'))
- visual_proj_rows_next: float32 [2048], P(('dp', 'mp'))
- visual_proj_cols_next: float32 [768], replicated
- visual_proj_low: bfloat16 [2048, 768], P(('dp', 'mp'))
- attn_in_grad: float32 [2, 3, 768, 768], P(None, None, 'dp', 'mp')
- attn_in_next: float32 [2, 3, 768, 768], P(None, None, 'dp', 'mp')
- attn_in_rows_next: float32 [2, 3, 768], P(None, None, 'dp')
- attn_in_cols_next: float32 [2, 3, 768], P(None, None, 'mp')
- attn_in_low: bfloat16 [2, 3, 768, 768], P(None, None, 'dp', 'mp')
- attn_out_grad: float32 [2, 768, 768], P(None, 'mp', 'dp')
- attn_out_next: float32 [2, 768, 768], P(None, 'mp', 'dp')
- attn_out_rows_next: float32 [2, 768], P(None, 'mp')
- attn_out_cols_next: float32 [2, 768], P(None, 'dp')
- attn_out_low: bfloat16 [2, 768, 768], P(None, 'mp', 'dp')
- ffn_up_grad: float32 [768, 3072], P('dp', 'mp')
- ffn_up_next: float32 [768, 3072], P('dp', 'mp')
- ffn_up_rows_next: float32 [768], P('dp')
- ffn_up_cols_next: float32 [3072], P('mp')
- ffn_up_low: bfloat16 [768, 3072], P('dp', 'mp')
- ffn_down_grad: float32 [3072, 768], P('mp', 'dp')
- ffn_down_next: float32 [3072, 768], P('mp', 'dp')
- ffn_down_rows_next: float32 [3072], P('mp')
- ffn_down_cols_next: float32 [768], P('dp')
- ffn_down_low: bfloat16 [3072, 768], P('mp', 'dp')
- norm_grad: float32 [5, 768], replicated
- norm_moment_next: float32 [5, 768], replicated
- norm_next: float32 [5, 768], replicated
- up_grad: float32 [3072], replicated
- up_moment_next: float32 [3072], replicated
- up_next: float32 [3072], replicated
- table_grad: float32 [2, 33, 12], replicated
- table_moment_next: float32 [2, 33, 12], replicated
- table_next: float32 [2, 33, 12], replicated
The draws below stay inside these ranges and needn't reach their ends.
Inputs may be any that keep to these rules, and one draw needn't show every extreme that they name: `segments`: within a page the segment id never falls.
All inputs are finite; a program needn't handle non-finite values.
Results may differ from the reference program's by a relative error of at most 0.025.
Values may be sent and summed in bfloat16 or wider, within the bound.
No kernel may reach another device: no remote copies, remote signals or barrier semaphores. Data moves between devices by JAX's collectives and lax.ppermute only.
A program may use at most 256 MiB of HBM per device.

```python
import math
from functools import partial
import jax
import jax.numpy as jnp
import numpy as np
from jax import lax

D = 768
HEADS = 12
FF = 3072
CIN = 2048
CMID = 512
IMG_H = 64
IMG_W = 16
NB = 32
RREL = 16
SEGS = 4
STEP = 5
PAGE_LEN = 1024
PAGES = 16


def touch_ends(entries, stream_key, smallest, largest):
    shape = entries.shape
    spot = [jax.random.randint(jax.random.fold_in(stream_key, axis), (), 0, shape[axis]) for axis in range(len(shape))]
    entries = entries.at[tuple(spot)].set(smallest)
    longest = shape.index(max(shape))
    spot[longest] = (spot[longest] + 1) % shape[longest]
    return entries.at[tuple(spot)].set(largest)


def block_levels(own_key, shape, pieces, low, top_value):
    gain = 1.0
    for position, parts in pieces:
        draws = jax.random.uniform(jax.random.fold_in(jax.random.fold_in(own_key, 6), position), (parts,), jnp.float32, low / len(pieces), top_value / len(pieces))
        gain = gain * jnp.repeat(jnp.exp(draws), shape[position] // parts).reshape((-1,) + (1,) * (len(shape) - 1 - position))
    return gain


def split_up(count, total, limit, lean):
    weights = [(1 << 20) // math.isqrt(standing ** lean) + 1 for standing in range(2, count + 1)]
    rest, holding = total - limit - (count - 1), [1] * (count - 1)
    while rest > 0:
        free = [i for i in range(count - 1) if holding[i] < limit]
        pool, left = sum([weights[i] for i in free]), rest
        for i in free:
            more = min(limit - holding[i], max(1, left * weights[i] // pool), rest)
            holding[i] = holding[i] + more
            rest = rest - more
    return np.array([limit] + holding)


def uneven(key, amount, total, limit, lean):
    if amount == 2:
        one = jax.random.randint(key, (), max(1, total - limit), min(limit, total - 1) + 1)
        return jnp.stack([one, total - one])
    tallies = jnp.asarray(split_up(amount, total, limit, lean), jnp.int32)
    couples = (amount - 1) // 2
    source_of, receiver = tallies[1:1 + 2 * couples:2], tallies[2:2 + 2 * couples:2]
    room = jnp.minimum(source_of - 1, limit - receiver)
    passed = jax.random.randint(jax.random.fold_in(key, 1), (couples,), 0, 1 << 20) % (room + 1)
    tallies = tallies.at[1:1 + 2 * couples:2].set(source_of - passed).at[2:2 + 2 * couples:2].set(receiver + passed)
    return tallies[jax.random.permutation(jax.random.fold_in(key, 2), amount)]


def gaussian(rng, dims, width, reach, cuts=(), kind=jnp.bfloat16):
    level = block_levels(rng, dims, cuts, -0.22, 0.18) if cuts else 1.0
    result = jax.random.normal(rng, dims, jnp.float32) * width * level
    return jnp.minimum(jnp.maximum(result, -reach), reach).astype(kind)


def setup_inputs(seed: int = 0) -> dict:
    splits = jax.random.split(jax.random.key(seed), 36)
    return {
        "image": gaussian(splits[0], (PAGES, IMG_W, IMG_H, CIN), 1.0, 6.0, ((1, 4), (2, 8))),
        "text": gaussian(splits[1], (PAGES, PAGE_LEN, D), 1.0, 6.0, ((0, 8),)),
        "cotangent": gaussian(splits[2], (PAGES, PAGE_LEN, D), 1.0, 6.0, ((0, 8),)),
        "segments": jax.vmap(lambda own: jnp.searchsorted(jnp.cumsum(uneven(own, SEGS, PAGE_LEN, PAGE_LEN // 2, 0)), jnp.arange(PAGE_LEN), side="right"))(jax.random.split(splits[3], PAGES)).reshape((PAGES, PAGE_LEN)).astype(jnp.int32),
        "boxes": touch_ends(jax.random.randint(splits[4], (PAGES, 2, PAGE_LEN), 0, NB), jax.random.fold_in(splits[4], 1), 0, NB - 1).astype(jnp.int32),
        "reduce_weight": gaussian(splits[5], (CIN, CMID), CIN ** -0.5, 0.125, ((0, 32),), jnp.float32),
        "reduce_weight_rows": jnp.clip(jnp.exp(math.log(1228.8) - 2.014903 * jax.random.uniform(splits[6], (CIN,), jnp.float32) ** block_levels(splits[6], (CIN,), ((0, 32),), -0.2, 0.2)), 163.84, 1228.8),
        "reduce_weight_cols": jnp.clip(jnp.exp(jax.random.uniform(splits[7], (CMID,), jnp.float32, math.log(163.84), math.log(1228.8))), 163.84, 1228.8),
        "spatial_weight": gaussian(splits[8], (9 * CMID, CMID), (9 * CMID) ** -0.5, 0.09375, ((0, 32),), jnp.float32),
        "spatial_weight_rows": jnp.clip(jnp.exp(math.log(1228.8) - 2.014903 * jax.random.uniform(splits[9], (9 * CMID,), jnp.float32) ** block_levels(splits[9], (9 * CMID,), ((0, 32),), -0.2, 0.2)), 163.84, 1228.8),
        "spatial_weight_cols": jnp.clip(jnp.exp(jax.random.uniform(splits[10], (CMID,), jnp.float32, math.log(163.84), math.log(1228.8))), 163.84, 1228.8),
        "expand_weight": gaussian(splits[11], (CMID, CIN), CMID ** -0.5, 0.25, ((0, 32),), jnp.float32),
        "expand_weight_rows": jnp.clip(jnp.exp(math.log(1228.8) - 2.014903 * jax.random.uniform(splits[12], (CMID,), jnp.float32) ** block_levels(splits[12], (CMID,), ((0, 32),), -0.2, 0.2)), 163.84, 1228.8),
        "expand_weight_cols": jnp.clip(jnp.exp(jax.random.uniform(splits[13], (CIN,), jnp.float32, math.log(163.84), math.log(1228.8))), 163.84, 1228.8),
        "visual_proj": gaussian(splits[14], (CIN, D), CIN ** -0.5, 0.125, ((0, 32),), jnp.float32),
        "visual_proj_rows": jnp.clip(jnp.exp(math.log(12288.0) - 2.014903 * jax.random.uniform(splits[15], (CIN,), jnp.float32) ** block_levels(splits[15], (CIN,), ((0, 32),), -0.2, 0.2)), 1638.4, 12288.0),
        "visual_proj_cols": jnp.clip(jnp.exp(jax.random.uniform(splits[16], (D,), jnp.float32, math.log(1638.4), math.log(12288.0))), 1638.4, 12288.0),
        "attn_in": gaussian(splits[17], (2, 3, D, D), D ** -0.5, 0.21875, ((2, 8), (3, 4)), jnp.float32),
        "attn_in_rows": jnp.clip(jnp.exp(math.log(3686.4) - 2.014903 * jax.random.uniform(splits[18], (2, 3, D), jnp.float32) ** block_levels(splits[18], (2, 3, D), ((2, 8),), -0.2, 0.2)), 491.52, 3686.4),
        "attn_in_cols": jnp.clip(jnp.exp(math.log(3686.4) - 2.014903 * jax.random.uniform(splits[19], (2, 3, D), jnp.float32) ** block_levels(splits[19], (2, 3, D), ((2, 4),), -0.2, 0.2)), 491.52, 3686.4),
        "attn_out": gaussian(splits[20], (2, D, D), (max(D // 32, 8)) ** -0.5, 1.25, ((1, 4), (2, 8)), jnp.float32),
        "attn_out_rows": jnp.clip(jnp.exp(math.log(245.76) - 2.014903 * jax.random.uniform(splits[21], (2, D), jnp.float32) ** block_levels(splits[21], (2, D), ((1, 4),), -0.2, 0.2)), 32.768, 245.76),
        "attn_out_cols": jnp.clip(jnp.exp(math.log(245.76) - 2.014903 * jax.random.uniform(splits[22], (2, D), jnp.float32) ** block_levels(splits[22], (2, D), ((1, 8),), -0.2, 0.2)), 32.768, 245.76),
        "ffn_up": gaussian(splits[23], (D, FF), D ** -0.5, 0.21875, ((0, 8), (1, 4)), jnp.float32),
        "ffn_up_rows": jnp.clip(jnp.exp(math.log(6144.0) - 2.014903 * jax.random.uniform(splits[24], (D,), jnp.float32) ** block_levels(splits[24], (D,), ((0, 8),), -0.2, 0.2)), 819.2, 6144.0),
        "ffn_up_cols": jnp.clip(jnp.exp(math.log(6144.0) - 2.014903 * jax.random.uniform(splits[25], (FF,), jnp.float32) ** block_levels(splits[25], (FF,), ((0, 4),), -0.2, 0.2)), 819.2, 6144.0),
        "ffn_down": gaussian(splits[26], (FF, D), FF ** -0.5, 0.109375, ((0, 4), (1, 8)), jnp.float32),
        "ffn_down_rows": jnp.clip(jnp.exp(math.log(9830.4) - 2.014903 * jax.random.uniform(splits[27], (FF,), jnp.float32) ** block_levels(splits[27], (FF,), ((0, 4),), -0.2, 0.2)), 1310.72, 9830.4),
        "ffn_down_cols": jnp.clip(jnp.exp(math.log(9830.4) - 2.014903 * jax.random.uniform(splits[28], (D,), jnp.float32) ** block_levels(splits[28], (D,), ((0, 8),), -0.2, 0.2)), 1310.72, 9830.4),
        "norm_params": jnp.clip(1.0 + 0.18 * jax.random.normal(splits[29], (5, D), jnp.float32), 0.1, 1.9),
        "norm_moment": jnp.clip(jnp.exp(jax.random.uniform(splits[30], (5, D), jnp.float32, math.log(3276.8), math.log(24576.0))), 3276.8, 24576.0),
        "up_bias": gaussian(splits[31], (FF,), 0.3, 1.8, (), jnp.float32),
        "up_moment": jnp.clip(jnp.exp(jax.random.uniform(splits[32], (FF,), jnp.float32, math.log(819.2), math.log(6144.0))), 819.2, 6144.0),
        "tables": gaussian(splits[33], (2, 2 * RREL + 1, HEADS), 0.7, 4.0, (), jnp.float32),
        "table_moment": jnp.clip(jnp.exp(jax.random.uniform(splits[34], (2, 2 * RREL + 1, HEADS), jnp.float32, math.log(327.68), math.log(2457.6))), 327.68, 2457.6),
    }


NEGATIVE = -1000000000.0
NORM_EPS = 1e-05
RELATIVE = 0.5
RATE_FLOOR = 0.001
PRECISE = lax.Precision.HIGHEST
FORWARD_TAPS = tuple(((shift_col, shift_row) for shift_col in range(3) for shift_row in range(3)))

@jax.custom_vjp
def low(v):
    return lax.optimization_barrier(v.astype(jnp.bfloat16)).astype(jnp.float32)

@jax.custom_vjp
def low_back(v):
    return v

def low_keep(v):
    return (low(v), None)

def low_pass(kept, grad):
    return (grad,)

def back_keep(v):
    return (v, None)

def back_low(kept, grad):
    return (low(grad),)
low.defvjp(low_keep, low_pass)
low_back.defvjp(back_keep, back_low)

def smooth(values):
    return jax.nn.gelu(values, approximate=True)

def layer_norm(values, norm_gain, norm_shift):
    centre = values - lax.optimization_barrier(jnp.mean(values, axis=-1, keepdims=True))
    spread = lax.optimization_barrier(jnp.mean(centre * centre, axis=-1, keepdims=True))
    return centre * lax.rsqrt(spread + NORM_EPS) * norm_gain + norm_shift

def relative_select(buckets, reach_max):
    offsets = jnp.arange(buckets, dtype=jnp.int32)[None, :] - jnp.arange(buckets, dtype=jnp.int32)[:, None]
    clipped = jnp.clip(offsets, -reach_max, reach_max) + reach_max
    return (clipped[:, :, None] == jnp.arange(2 * reach_max + 1, dtype=jnp.int32)[None, None, :]).astype(jnp.float32)

def box_onehot(boxes_page, buckets):
    levels = jnp.arange(buckets, dtype=jnp.int32)[None, :]
    across_hot = (boxes_page[0][:, None] == levels).astype(jnp.float32)
    down_hot = (boxes_page[1][:, None] == levels).astype(jnp.float32)
    return jnp.concatenate([across_hot, down_hot], axis=1)

def bias_block(rows_hot, keys_hot, span_tables, buckets):
    first_part = jnp.einsum('qa,hab->hqb', rows_hot[:, :buckets], span_tables[0], precision=PRECISE)
    second_part = jnp.einsum('qa,hab->hqb', rows_hot[:, buckets:], span_tables[1], precision=PRECISE)
    joined = jnp.concatenate([first_part, second_part], axis=-1)
    return jnp.einsum('hqc,kc->hqk', joined, keys_hot, precision=PRECISE)

def attend_block(block_rows, block_index, queries, key_rows, values, onehot, segment_row, span_tables):
    block_start = block_index * block_rows
    rows_hot = lax.dynamic_slice_in_dim(onehot, block_start, block_rows, 0)
    same_page = lax.dynamic_slice_in_dim(segment_row, block_start, block_rows, 0)[:, None] == segment_row[None, :]
    query_block = lax.dynamic_slice_in_dim(queries, block_start, block_rows, 0)
    scaling = queries.shape[-1] ** (-0.5)
    scores = jnp.einsum('qhd,khd->hqk', query_block, key_rows, precision=PRECISE) * scaling
    scores = scores + bias_block(rows_hot, onehot, span_tables, onehot.shape[1] // 2)
    scores = low_back(jnp.where(same_page[None], scores, NEGATIVE))
    weights = low(jax.nn.softmax(scores, axis=-1))
    return jnp.einsum('hqk,khd->qhd', weights, values, precision=PRECISE)

def page_attention(text_page, visual_page, segment_row, boxes_page, in_weights, out_weights, span_tables):
    length, model_width = text_page.shape
    head_count = span_tables.shape[1]
    head_size = model_width // head_count
    block_rows = min(512, length)
    onehot = box_onehot(boxes_page, span_tables.shape[2])
    checked = jax.checkpoint(partial(attend_block, block_rows))
    mixtures = []
    for stream, source in enumerate((text_page, visual_page)):
        projected = [low(low_back(jnp.dot(source, in_weights[stream, member], precision=PRECISE, preferred_element_type=jnp.float32))).reshape(length, head_count, head_size) for member in range(3)]

        def run_block(block_index):
            return checked(block_index, projected[0], projected[1], projected[2], onehot, segment_row, span_tables)
        gathered = lax.map(run_block, jnp.arange(length // block_rows, dtype=jnp.int32))
        attended = low(low_back(gathered.reshape(length, model_width)))
        mixtures.append(jnp.dot(attended, out_weights[stream], precision=PRECISE, preferred_element_type=jnp.float32))
    return mixtures[0] + mixtures[1]

def bottleneck(image_float, reduce_low, spatial_low, expand_low):
    channels = spatial_low.shape[1]
    across = image_float.shape[1]
    downward = image_float.shape[2]
    reduced = low_back(jnp.einsum('pwhc,cd->pwhd', image_float, reduce_low, precision=PRECISE))
    hidden_one = low(smooth(reduced))
    padded = jnp.pad(hidden_one, ((0, 0), (1, 1), (1, 1), (0, 0)))
    mixed_sum = jnp.zeros(hidden_one.shape, jnp.float32)
    for tap_index, (from_col, from_row) in enumerate(FORWARD_TAPS):
        window = padded[:, from_col:from_col + across, from_row:from_row + downward, :]
        tap_weight = spatial_low[tap_index * channels:(tap_index + 1) * channels]
        mixed_sum = mixed_sum + jnp.einsum('pwhc,cd->pwhd', window, tap_weight, precision=PRECISE)
    convolved = low_back(mixed_sum)
    hidden_two = low(smooth(convolved))
    expanded = low_back(jnp.einsum('pwhc,cd->pwhd', hidden_two, expand_low, precision=PRECISE))
    return smooth(image_float + expanded)

def factored_update(weight, gradient, rows_old, cols_old):
    decay_rate = 1.0 - STEP ** (-0.8)
    squares = gradient * gradient
    rows_next = decay_rate * rows_old + (1.0 - decay_rate) * lax.optimization_barrier(jnp.mean(squares, axis=-1))
    cols_next = decay_rate * cols_old + (1.0 - decay_rate) * lax.optimization_barrier(jnp.mean(squares, axis=-2))
    row_mean = lax.optimization_barrier(jnp.mean(rows_next, axis=-1))
    second = rows_next[..., :, None] * cols_next[..., None, :] / row_mean[..., None, None]
    step_rate = RELATIVE * jnp.maximum(RATE_FLOOR, jnp.sqrt(lax.optimization_barrier(jnp.mean(weight * weight, axis=(-2, -1)))))
    weight_next = weight - step_rate[..., None, None] * (gradient * lax.rsqrt(second))
    return (gradient, weight_next, rows_next, cols_next, weight_next.astype(jnp.bfloat16))

def moment_step(parameter, gradient, moment, reduce_axes):
    decay_rate = 1.0 - STEP ** (-0.8)
    moment_next = decay_rate * moment + (1.0 - decay_rate) * gradient * gradient
    rms_value = jnp.sqrt(lax.optimization_barrier(jnp.mean(parameter * parameter, axis=reduce_axes, keepdims=True)))
    return (gradient, moment_next, parameter - RELATIVE * jnp.maximum(RATE_FLOOR, rms_value) * gradient * lax.rsqrt(moment_next))

def reference(image, text, cotangent, segments, boxes, reduce_weight, reduce_weight_rows, reduce_weight_cols, spatial_weight, spatial_weight_rows, spatial_weight_cols, expand_weight, expand_weight_rows, expand_weight_cols, visual_proj, visual_proj_rows, visual_proj_cols, attn_in, attn_in_rows, attn_in_cols, attn_out, attn_out_rows, attn_out_cols, ffn_up, ffn_up_rows, ffn_up_cols, ffn_down, ffn_down_rows, ffn_down_cols, norm_params, norm_moment, up_bias, up_moment, tables, table_moment):
    bucket_select = relative_select(NB, RREL)

    def forward(image_float, text_float, norm_table, bias_up, span_source, reduce_float, spatial_float, expand_float, proj_float, in_float, out_float, up_float, down_float):
        reduce_low = low(reduce_float)
        spatial_low = low(spatial_float)
        expand_low = low(expand_float)
        proj_low = low(proj_float)
        in_low = low(in_float)
        out_low = low(out_float)
        up_low = low(up_float)
        down_low = low(down_float)
        feature = bottleneck(image_float, reduce_low, spatial_low, expand_low)
        visual = low(low_back(jnp.einsum('pwhc,cd->pwhd', low(feature), proj_low, precision=PRECISE))).reshape(text_float.shape)
        span_tables = jnp.einsum('abr,trh->thab', bucket_select, span_source, precision=PRECISE)

        def one_page(page_items):
            return page_attention(page_items[0], page_items[1], page_items[2], page_items[3], in_low, out_low, span_tables)
        attention = low_back(lax.map(one_page, (text_float, visual, segments, boxes)))
        first_sum = text_float + visual + attention
        normed = layer_norm(first_sum, norm_table[0], norm_table[1])
        hidden_pre = low_back(jnp.einsum('pld,df->plf', low(normed), up_low, precision=PRECISE) + bias_up)
        hidden = low(smooth(hidden_pre))
        down_out = low_back(jnp.einsum('plf,fd->pld', hidden, down_low, precision=PRECISE) + norm_table[4])
        return layer_norm(normed + down_out, norm_table[2], norm_table[3])
    primal, pull = jax.vjp(forward, image.astype(jnp.float32), text.astype(jnp.float32), norm_params, up_bias, tables, reduce_weight, spatial_weight, expand_weight, visual_proj, attn_in, attn_out, ffn_up, ffn_down)
    grads = pull(cotangent.astype(jnp.float32))
    reduce_parts = factored_update(reduce_weight, grads[5], reduce_weight_rows, reduce_weight_cols)
    spatial_parts = factored_update(spatial_weight, grads[6], spatial_weight_rows, spatial_weight_cols)
    expand_parts = factored_update(expand_weight, grads[7], expand_weight_rows, expand_weight_cols)
    proj_parts = factored_update(visual_proj, grads[8], visual_proj_rows, visual_proj_cols)
    in_parts = factored_update(attn_in, grads[9], attn_in_rows, attn_in_cols)
    out_parts = factored_update(attn_out, grads[10], attn_out_rows, attn_out_cols)
    up_parts = factored_update(ffn_up, grads[11], ffn_up_rows, ffn_up_cols)
    down_parts = factored_update(ffn_down, grads[12], ffn_down_rows, ffn_down_cols)
    norm_parts = moment_step(norm_params, grads[2], norm_moment, (1,))
    bias_parts = moment_step(up_bias, grads[3], up_moment, (0,))
    table_parts = moment_step(tables, grads[4], table_moment, (1, 2))
    return (primal.astype(jnp.bfloat16), grads[1], grads[0], reduce_parts[0], reduce_parts[1], reduce_parts[2], reduce_parts[3], reduce_parts[4], spatial_parts[0], spatial_parts[1], spatial_parts[2], spatial_parts[3], spatial_parts[4], expand_parts[0], expand_parts[1], expand_parts[2], expand_parts[3], expand_parts[4], proj_parts[0], proj_parts[1], proj_parts[2], proj_parts[3], proj_parts[4], in_parts[0], in_parts[1], in_parts[2], in_parts[3], in_parts[4], out_parts[0], out_parts[1], out_parts[2], out_parts[3], out_parts[4], up_parts[0], up_parts[1], up_parts[2], up_parts[3], up_parts[4], down_parts[0], down_parts[1], down_parts[2], down_parts[3], down_parts[4], norm_parts[0], norm_parts[1], norm_parts[2], bias_parts[0], bias_parts[1], bias_parts[2], table_parts[0], table_parts[1], table_parts[2])
```

```python
import functools

import jax
import jax.numpy as jnp
from jax import lax
from jax.experimental import pallas as pl
from jax.experimental.pallas import tpu as pltpu
from jax.sharding import Mesh
from jax.sharding import PartitionSpec as P

NB = 32
STEP = 5
NEGATIVE = -1000000000.0
SAFE = 2.0e8
NT = (((1,), (1,)), ((), ()))
NN = (((1,), (0,)), ((), ()))


def mm(a, b, dims=NN):
    return lax.dot_general(a, b, dims, preferred_element_type=jnp.float32)


def column(head, kind, group, size):
    return ((head // group * 3 + kind) * group + head % group) * size


def stage_heads(p_ref, kx_ref, tab_ref, q_scr, k_scr, heads, group, size):
    kx = kx_ref[...]
    for h in range(heads):
        first, second = column(h, 0, group, size), column(h, 1, group, size)
        mixed = mm(kx, tab_ref[h]).astype(jnp.bfloat16)
        q_scr[h, :, : 256 - size] = mixed[:, : 256 - size]
        q_scr[h, :, 256 - size :] = p_ref[:, first : first + size] * jnp.bfloat16(size**-0.5)
        k_scr[h, :, :128] = kx
        k_scr[h, :, 128 : 256 - size] = kx[:, : 128 - size]
        k_scr[h, :, 256 - size :] = p_ref[:, second : second + size]


def bound_ok(q_scr, k_scr, heads, size):
    big_q, big_k = 0.0, 0.0
    for h in range(heads):
        big_q = jnp.maximum(big_q, jnp.max(jnp.abs(q_scr[h, :, 256 - size :].astype(jnp.float32))))
        big_k = jnp.maximum(big_k, jnp.max(jnp.abs(k_scr[h, :, 256 - size :].astype(jnp.float32))))
    return big_q * big_k * size < SAFE


def window(win_ref, chunk, safe, length, tile):
    start = jnp.where(safe, win_ref[0, chunk], 0)
    count = jnp.where(safe, win_ref[1, chunk], length // tile)
    return pl.multiple_of(start, 128), count


def masked(safe, scores_scr, row, tile, seg_col, seg_row):
    @pl.when(jnp.logical_not(safe))
    def _():
        scores_scr[pl.ds(row, tile), :] = jnp.where(
            seg_col == seg_row, scores_scr[pl.ds(row, tile), :], NEGATIVE
        )


def forward_kernel(
    win_ref, p_ref, kx_ref, tab_ref, segc_ref, segr_ref, o_ref, lse_ref,
    q_scr, k_scr, vt_scr, s_scr, ot_scr, *, heads, group, size, chunk_rows, tile,
):
    length = kx_ref.shape[0]
    stage_heads(p_ref, kx_ref, tab_ref, q_scr, k_scr, heads, group, size)
    for h in range(heads):
        third = column(h, 2, group, size)
        vt_scr[h] = p_ref[:, third : third + size].astype(jnp.float32).T.astype(jnp.bfloat16)
    safe = bound_ok(q_scr, k_scr, heads, size)
    lse_ref[...] = jnp.zeros_like(lse_ref)

    def one_chunk(item, _):
        h, c = item // (length // chunk_rows), item % (length // chunk_rows)
        start, count = window(win_ref, c, safe, length, tile)
        first = pl.multiple_of(c * chunk_rows, chunk_rows)
        q = q_scr[h, pl.ds(first, chunk_rows), :]
        seg_row = segr_ref[:, pl.ds(first, chunk_rows)]

        def score(t, top):
            row = pl.multiple_of(t * tile, tile)
            src = pl.multiple_of(start + t * tile, 128)
            s_scr[pl.ds(row, tile), :] = mm(k_scr[h, pl.ds(src, tile), :], q, NT)
            masked(safe, s_scr, row, tile, segc_ref[pl.ds(src, tile), :1], seg_row)
            s = s_scr[pl.ds(row, tile), :]
            return jnp.maximum(top, jnp.max(s.reshape(tile // 8, 8, chunk_rows), axis=0))

        top = lax.fori_loop(0, count, score, jnp.full((8, chunk_rows), -3.0e38, jnp.float32))
        top = jnp.max(top, axis=0, keepdims=True)

        def mix(t, carry):
            total, out = carry
            row = pl.multiple_of(t * tile, tile)
            src = pl.multiple_of(start + t * tile, 128)
            p = jnp.exp(s_scr[pl.ds(row, tile), :] - top)
            total = total + jnp.sum(p.reshape(tile // 8, 8, chunk_rows), axis=0)
            out = out + mm(vt_scr[h, :, pl.ds(src, tile)], p.astype(jnp.bfloat16))
            return total, out

        total, out = lax.fori_loop(
            0, count, mix,
            (jnp.zeros((8, chunk_rows), jnp.float32), jnp.zeros((size, chunk_rows), jnp.float32)),
        )
        total = jnp.sum(total, axis=0, keepdims=True)
        lse_ref[pl.ds(h, 1), pl.ds(first, chunk_rows)] = top + jnp.log(total)
        ot_scr[h, :, pl.ds(first, chunk_rows)] = out / total
        return 0

    lax.fori_loop(0, heads * (length // chunk_rows), one_chunk, 0)
    for h in range(heads):
        o_ref[:, h * size : (h + 1) * size] = ot_scr[h].T.astype(jnp.bfloat16)


def backward_kernel(
    win_ref, p_ref, kx_ref, tab_ref, segc_ref, segr_ref, o_ref, lse_ref, g_ref, d_ref, span_ref,
    q_scr, k_scr, kt_scr, v_scr, g_scr, dk_scr, dv_scr, dq_scr, dl_scr, s_scr,
    *, heads, group, size, chunk_rows, tile, offset,
):
    length = kx_ref.shape[0]
    stage_heads(p_ref, kx_ref, tab_ref, q_scr, k_scr, heads, group, size)
    safe = bound_ok(q_scr, k_scr, heads, size)
    for h in range(heads):
        third = column(h, 2, group, size)
        kt_scr[h] = k_scr[h, :, 128:].astype(jnp.float32).T.astype(jnp.bfloat16)
        v_scr[h] = p_ref[:, third : third + size]
        g = g_ref[:, offset + h * size : offset + (h + 1) * size]
        g_scr[h] = g
        o = o_ref[:, h * size : (h + 1) * size]
        mixed = g.astype(jnp.float32) * o.astype(jnp.float32)
        dl_scr[pl.ds(h, 1), :] = jnp.sum(mixed.T, axis=0, keepdims=True)
    dk_scr[...] = jnp.zeros_like(dk_scr)
    dv_scr[...] = jnp.zeros_like(dv_scr)

    def one_chunk(item, _):
        h, c = item // (length // chunk_rows), item % (length // chunk_rows)
        start, count = window(win_ref, c, safe, length, tile)
        first = pl.multiple_of(c * chunk_rows, chunk_rows)
        q = q_scr[h, pl.ds(first, chunk_rows), :]
        q_own = q_scr[h, pl.ds(first, chunk_rows), 256 - size :]
        g = g_scr[h, pl.ds(first, chunk_rows), :]
        seg_row = segr_ref[:, pl.ds(first, chunk_rows)]
        lse = lse_ref[pl.ds(h, 1), pl.ds(first, chunk_rows)]
        delta = dl_scr[pl.ds(h, 1), pl.ds(first, chunk_rows)]

        def step(t, acc):
            src = pl.multiple_of(start + t * tile, 128)
            s_scr[...] = mm(k_scr[h, pl.ds(src, tile), :], q, NT)
            masked(safe, s_scr, 0, tile, segc_ref[pl.ds(src, tile), :1], seg_row)
            p = jnp.exp(s_scr[...] - lse)
            dp = mm(v_scr[h, pl.ds(src, tile), :], g, NT)
            ds = (p * (dp - delta)).astype(jnp.bfloat16)
            dv_scr[h, pl.ds(src, tile), :] += mm(p.astype(jnp.bfloat16), g)
            dk_scr[h, pl.ds(src, tile), :] += mm(ds, q_own)
            return acc + mm(kt_scr[h, :, pl.ds(src, tile)], ds)

        acc = lax.fori_loop(0, count, step, jnp.zeros((128, chunk_rows), jnp.float32))
        dq_scr[h, :, pl.ds(first, chunk_rows)] = acc
        return 0

    lax.fori_loop(0, heads * (length // chunk_rows), one_chunk, 0)
    for h in range(heads):
        first, second, third = (column(h, kind, group, size) for kind in range(3))
        d_ref[:, first : first + size] = (
            (dq_scr[h, 128 - size :, :] * size**-0.5).T.astype(jnp.bfloat16)
        )
        d_ref[:, second : second + size] = dk_scr[h].astype(jnp.bfloat16)
        d_ref[:, third : third + size] = dv_scr[h].astype(jnp.bfloat16)
        thr = dq_scr[h, : 128 - size, :]
        upper = thr.astype(jnp.bfloat16)
        lower = (thr - upper.astype(jnp.float32)).astype(jnp.bfloat16)
        span_ref[h] = mm(upper, kx_ref[...]) + mm(lower, kx_ref[...])


CHUNK = 256
TILE = 256
VMEM = pltpu.VMEM


def attend_forward(proj, around, size, group):
    length, total = proj.shape
    heads = total // (3 * size)
    full = pl.BlockSpec(memory_space=pltpu.VMEM)
    return pl.pallas_call(
        functools.partial(
            forward_kernel, heads=heads, group=group, size=size, chunk_rows=CHUNK, tile=TILE
        ),
        in_specs=[pl.BlockSpec(memory_space=pltpu.SMEM)] + [full] * 5,
        out_specs=[full, full],
        out_shape=[
            jax.ShapeDtypeStruct((length, heads * size), jnp.bfloat16),
            jax.ShapeDtypeStruct((8, length), jnp.float32),
        ],
        scratch_shapes=[
            VMEM((heads, length, 256), jnp.bfloat16),
            VMEM((heads, length, 256), jnp.bfloat16),
            VMEM((heads, size, length), jnp.bfloat16),
            VMEM((length, CHUNK), jnp.float32),
            VMEM((heads, size, length), jnp.float32),
        ],
        compiler_params=pltpu.CompilerParams(vmem_limit_bytes=48 * 1024 * 1024),
        cost_estimate=pl.CostEstimate(
            flops=heads * length * length * 512,
            bytes_accessed=length * total * 4,
            transcendentals=heads * length * length,
        ),
    )(around[0], proj, *around[1:])


def attend_backward(proj, around, out, lse, grads, stream, size, group):
    length, total = proj.shape
    heads = total // (3 * size)
    full = pl.BlockSpec(memory_space=pltpu.VMEM)
    return pl.pallas_call(
        functools.partial(
            backward_kernel, heads=heads, group=group, size=size, chunk_rows=CHUNK, tile=TILE,
            offset=stream * heads * size,
        ),
        in_specs=[pl.BlockSpec(memory_space=pltpu.SMEM)] + [full] * 8,
        out_specs=[full, full],
        out_shape=[
            jax.ShapeDtypeStruct((length, total), jnp.bfloat16),
            jax.ShapeDtypeStruct((heads, 128 - size, 128), jnp.float32),
        ],
        scratch_shapes=[
            VMEM((heads, length, 256), jnp.bfloat16),
            VMEM((heads, length, 256), jnp.bfloat16),
            VMEM((heads, 128, length), jnp.bfloat16),
            VMEM((heads, length, size), jnp.bfloat16),
            VMEM((heads, length, size), jnp.bfloat16),
            VMEM((heads, length, size), jnp.float32),
            VMEM((heads, length, size), jnp.float32),
            VMEM((heads, 128, length), jnp.float32),
            VMEM((8, length), jnp.float32),
            VMEM((TILE, CHUNK), jnp.float32),
        ],
        compiler_params=pltpu.CompilerParams(vmem_limit_bytes=56 * 1024 * 1024),
        cost_estimate=pl.CostEstimate(
            flops=heads * length * length * 1280,
            bytes_accessed=length * total * 8,
            transcendentals=heads * length * length,
        ),
    )(around[0], proj, *around[1:], out, lse, grads)


def attention_windows(segment_row, chunk_rows, tile):
    length = segment_row.shape[0]
    heads_of = segment_row[::chunk_rows]
    tails_of = segment_row[chunk_rows - 1 :: chunk_rows]
    low = jnp.sum((segment_row[None, :] < heads_of[:, None]).astype(jnp.int32), axis=1)
    high = jnp.sum((segment_row[None, :] <= tails_of[:, None]).astype(jnp.int32), axis=1)
    start = low // 128 * 128
    count = (high - start + tile - 1) // tile
    start = jnp.minimum(start, length - count * tile)
    return jnp.stack([start, count]).astype(jnp.int32)


def attention_tables(span_tables):
    _, heads, buckets, _ = span_tables.shape
    upper = lax.reduce_precision(span_tables, 8, 7)
    lower = (span_tables - upper).astype(jnp.bfloat16)
    def diag(t):
        z = jnp.zeros_like(t[0])
        return jnp.concatenate([jnp.concatenate([t[0], z], 2), jnp.concatenate([z, t[1]], 2)], 1)
    hi, lo = diag(upper.astype(jnp.bfloat16)), diag(lower)
    level = jnp.arange(64)
    away = jnp.where((level[:, None] != level[None, :]), NEGATIVE, 0.0)
    segs = jnp.where((level[:, None] < 4) & (level[None, :] < 4), away, 0.0).astype(jnp.bfloat16)
    segs = jnp.broadcast_to(segs[None], (heads, 64, 64))
    zero = jnp.zeros((heads, 64, 64), jnp.bfloat16)
    top = jnp.concatenate([hi, zero, lo, zero], 2)
    bottom = jnp.concatenate([zero, segs, zero, zero], 2)
    return jnp.concatenate([top, bottom], 1)


def token_marks(boxes_page, segment_row, buckets):
    levels = jnp.arange(buckets, dtype=jnp.int32)[None, :]
    kinds = jnp.arange(64, dtype=jnp.int32)[None, :]
    return jnp.concatenate(
        [boxes_page[0][:, None] == levels, boxes_page[1][:, None] == levels, segment_row[:, None] == kinds],
        axis=1,
    ).astype(jnp.bfloat16)


NORM_EPS = 1e-05
RELATIVE = 0.5
RATE_FLOOR = 0.001
PRECISE = lax.Precision.HIGHEST
LOW = jnp.bfloat16
WIDE = jnp.float32
AXES = ("dz", "dx", "my", "core")
DP = ("dz", "dx")
MP = ("my", "core")
CHIPS = ("dz", "dx", "my")
OWNERS = ("my", "dz", "dx")
FORWARD_TAPS = tuple((col, row) for col in range(3) for row in range(3))
BACKWARD_TAPS = tuple((2 - col, 2 - row) for col in range(3) for row in range(3))


def swap(values, axis, reach):
    count = lax.axis_size(axis)
    return lax.ppermute(values, axis, [(i, i ^ reach) for i in range(count)])


def bits_of(axis):
    reach, found = lax.axis_size(axis) // 2, []
    while reach:
        found.append((axis, reach))
        reach //= 2
    return found


def bits(axes):
    return [bit for axis in axes for bit in bits_of(axis)]


def side(bit):
    return lax.axis_index(bit[0]) // bit[1] % 2


def gather_tree(shard, order, owners):
    places = bits(owners)
    steps = [bit for axis in order for bit in reversed(bits_of(axis))]
    sides = [side(place) for place in places]
    rest = [0] * shard.ndim

    def corner(done, other=None):
        return [
            0 if place in done else (1 - mine if place == other else mine)
            for place, mine in zip(places, sides)
        ] + rest

    held = shard.reshape((1,) * len(places) + shard.shape)
    whole = jnp.zeros((2,) * len(places) + shard.shape, shard.dtype)
    whole = lax.dynamic_update_slice(whole, held, corner(()))
    done = []
    for bit in steps:
        whole = lax.dynamic_update_slice(whole, swap(held, *bit), corner(done, bit))
        done.append(bit)
        sizes = [2 if place in done else 1 for place in places] + list(shard.shape)
        held = lax.dynamic_slice(whole, corner(done), sizes)
    return whole.reshape((2 ** len(places) * shard.shape[0],) + shard.shape[1:])


def scatter_tree(blocks, order, live, wide=True):
    live = list(live)
    steps = [bit for axis in order for bit in bits_of(axis)]
    for number, bit in enumerate(steps):
        place = live.index(bit)
        half = blocks.shape[place] // 2
        mine = side(bit)
        sent = lax.dynamic_slice_in_dim(blocks, (1 - mine) * half, half, place)
        kept = lax.dynamic_slice_in_dim(blocks, mine * half, half, place)
        blocks = kept.astype(WIDE) + swap(sent, *bit).astype(WIDE)
        if number < len(steps) - 1:
            blocks = blocks.astype(LOW)
    return blocks


def scatter_rows(blocks, order, owners):
    live = bits(owners)
    split = blocks.reshape((2,) * len(live) + (-1,) + blocks.shape[1:])
    summed = scatter_tree(split, order, live + [None] * blocks.ndim)
    return summed.reshape(summed.shape[len(live) :])


def total_over(values, axes):
    for bit in bits(axes):
        values = values + swap(values, *bit)
    return values


def by_side(bit, own, other, axis):
    return jnp.where(
        side(bit) == 0, jnp.stack([own, other], axis), jnp.stack([other, own], axis)
    )


def from_both(own):
    both = by_side(("core", 1), own, swap(own, "core", 1), 1)
    return both.reshape((-1,) + own.shape[2:])


def add_both(partial, quarter):
    parts = partial.reshape((-1, 2, quarter) + partial.shape[1:])
    core = lax.axis_index("core")
    sent = lax.dynamic_index_in_dim(parts, 1 - core, 1, keepdims=False)
    kept = lax.dynamic_index_in_dim(parts, core, 1, keepdims=False)
    return (kept + swap(sent.astype(LOW), "core", 1).astype(WIDE)).reshape(
        (-1,) + partial.shape[1:]
    )


def extended(cells, sides, width):
    for axis, dim in sides:
        count = lax.axis_size(axis)
        ends = count - 1
        head = lax.slice_in_dim(cells, 0, width, axis=dim)
        tail = lax.slice_in_dim(cells, cells.shape[dim] - width, cells.shape[dim], axis=dim)
        cells = jnp.concatenate(
            [
                lax.ppermute(tail, axis, [(i, i + 1) for i in range(ends)]),
                cells,
                lax.ppermute(head, axis, [(i + 1, i) for i in range(ends)]),
            ],
            axis=dim,
        )
    return cells


def smooth(values):
    return jax.nn.gelu(values, approximate=True)


def smooth_back(values, upstream):
    return jax.vjp(smooth, values)[1](upstream)[0]


def layer_norm(values, norm_gain, norm_shift):
    centre = values - jnp.mean(values, axis=-1, keepdims=True)
    spread = jnp.mean(centre * centre, axis=-1, keepdims=True)
    return centre * lax.rsqrt(spread + NORM_EPS) * norm_gain + norm_shift


def relative_select(buckets, reach_max):
    offsets = (
        jnp.arange(buckets, dtype=jnp.int32)[None, :]
        - jnp.arange(buckets, dtype=jnp.int32)[:, None]
    )
    clipped = jnp.clip(offsets, -reach_max, reach_max) + reach_max
    return (
        clipped[:, :, None] == jnp.arange(2 * reach_max + 1, dtype=jnp.int32)[None, None, :]
    ).astype(WIDE)


def stacked_taps(padded, across, downward, anchors):
    return jnp.concatenate(
        [
            padded[:, from_col : from_col + across, from_row : from_row + downward, :]
            for from_col, from_row in anchors
        ],
        axis=-1,
    )


def dot(left, right, dims="nn"):
    first = 0 if dims[0] == "t" else 1
    second = 1 if dims[1] == "t" else 0
    return lax.dot_general(
        left, right, (((first,), (second,)), ((), ())), preferred_element_type=WIDE
    )


def factored_step(weight, gradient, rows_old, cols_old, row_piece, col_piece, row_mean, weight_mean, sizes):
    decay_rate = 1.0 - STEP ** (-0.8)
    rows_next = decay_rate * rows_old + (1.0 - decay_rate) * row_piece / sizes[1]
    cols_next = decay_rate * cols_old + (1.0 - decay_rate) * col_piece / sizes[0]
    second = rows_next[..., :, None] * cols_next[..., None, :] / row_mean[..., None, None]
    step_rate = RELATIVE * jnp.maximum(RATE_FLOOR, jnp.sqrt(weight_mean))
    weight_next = weight - step_rate[..., None, None] * (gradient * lax.rsqrt(second))
    return (gradient, weight_next, rows_next, cols_next, weight_next.astype(LOW))


def moment_step(parameter, gradient, moment, reduce_axes):
    decay_rate = 1.0 - STEP ** (-0.8)
    moment_next = decay_rate * moment + (1.0 - decay_rate) * gradient * gradient
    rms_value = jnp.sqrt(jnp.mean(parameter * parameter, axis=reduce_axes, keepdims=True))
    return (
        gradient,
        moment_next,
        parameter
        - RELATIVE * jnp.maximum(RATE_FLOOR, rms_value) * gradient * lax.rsqrt(moment_next),
    )


def pack(parts):
    return jnp.concatenate([part.reshape(-1) for part in parts])


def unpack(flat, like):
    found, cursor = [], 0
    for part in like:
        found.append(flat[cursor : cursor + part.size].reshape(part.shape))
        cursor += part.size
    return found


def on_device(
    image, text, cotangent, segments, boxes,
    reduce_weight, reduce_weight_rows, reduce_weight_cols,
    spatial_weight, spatial_weight_rows, spatial_weight_cols,
    expand_weight, expand_weight_rows, expand_weight_cols,
    visual_proj, visual_proj_rows, visual_proj_cols,
    attn_in, attn_in_rows, attn_in_cols,
    attn_out, attn_out_rows, attn_out_cols,
    ffn_up, ffn_up_rows, ffn_up_cols,
    ffn_down, ffn_down_rows, ffn_down_cols,
    norm_params, norm_moment, up_bias, up_moment, tables, table_moment,
):
    dp_count = lax.axis_size(DP)
    pair = lax.axis_size("my")
    mp_count = 2 * pair
    my, core = lax.axis_index("my"), lax.axis_index("core")
    mp_index = lax.axis_index(MP)
    length, width = text.shape[1:]
    quarter = length // mp_count
    heads = tables.shape[2]
    size = width // heads
    group = heads // mp_count
    part = group * size
    units = ffn_up.shape[1]
    pages, across, down, channels = image.shape
    middle = spatial_weight.shape[1]

    layer_in = jnp.concatenate(
        [
            attn_in.astype(LOW).transpose(2, 0, 1, 3).reshape(attn_in.shape[2], -1),
            attn_out.astype(LOW).transpose(2, 0, 1).reshape(attn_out.shape[2], -1),
        ],
        axis=1,
    )
    layer_ffn = jnp.concatenate([ffn_up.astype(LOW), ffn_down.astype(LOW).T], axis=1)
    attn_whole = lax.all_gather(layer_in, OWNERS, axis=0, tiled=True).reshape(pair, width, -1)
    ffn_whole = lax.all_gather(layer_ffn, OWNERS, axis=0, tiled=True).reshape(pair, width, -1)
    reduce_low = reduce_weight.astype(LOW)
    reduce_half = reduce_low.shape[0] // 2
    middle_cut = spatial_weight.shape[0] // 2
    side_low = jnp.concatenate(
        [expand_weight.astype(LOW).reshape(-1, middle), visual_proj.astype(LOW)], axis=1
    )
    weight_reduce = gather_tree(reduce_low, ("dz", "dx", "my", "core"), AXES)
    weight_spatial = gather_tree(spatial_weight.astype(LOW), ("dz", "my", "dx", "core"), AXES)
    side_whole = gather_tree(side_low, ("dz", "dx", "my", "core"), AXES)
    weight_expand = side_whole[:, :middle].reshape(middle, channels)
    weight_proj = side_whole[:, middle:]

    bucket_select = relative_select(NB, (tables.shape[1] - 1) // 2)
    own_tables = tables.reshape(tables.shape[:2] + (pair, 2, group))
    own_tables = lax.dynamic_index_in_dim(own_tables, core, 3, keepdims=False).reshape(
        tables.shape[:2] + (pair * group,)
    )
    span_tables = jnp.einsum("abr,trh->thab", bucket_select, own_tables, precision=PRECISE)
    head_tables = attention_tables(span_tables)
    page_segments = lax.dynamic_index_in_dim(segments, my, 0, keepdims=False)
    page_boxes = lax.dynamic_index_in_dim(boxes, my, 0, keepdims=False)
    marks = token_marks(page_boxes, page_segments, NB)
    windows = attention_windows(page_segments, CHUNK, TILE)
    segment_cols = jnp.broadcast_to(page_segments[:, None], (length, 128))
    around = (windows, marks, head_tables, segment_cols, page_segments[None])
    text_page = lax.dynamic_index_in_dim(text, my, 0, keepdims=False)
    upstream_page = lax.dynamic_index_in_dim(cotangent, my, 0, keepdims=False)

    def own_tokens(page):
        split = page.reshape(pair, 2, quarter, width)
        return lax.dynamic_index_in_dim(split, core, 1, keepdims=False).reshape(-1, width)

    weight_in = [
        attn_whole[:, :, stream * 3 * part : (stream + 1) * 3 * part]
        .transpose(1, 0, 2)
        .reshape(width, pair * 3 * part)
        for stream in range(2)
    ]
    weight_out = (
        attn_whole[:, :, 6 * part :]
        .reshape(pair, width, 2, part)
        .transpose(1, 2, 0, 3)
        .reshape(width, 2 * pair * part)
    )
    weight_up = [ffn_whole[y, :, :units] for y in range(pair)]
    weight_down = [ffn_whole[y, :, units:] for y in range(pair)]

    reduced = jnp.einsum("pwhc,cd->pwhd", image, weight_reduce, preferred_element_type=WIDE)
    hidden_one = smooth(reduced).astype(LOW)
    padded = extended(hidden_one, ((DP, 2), (MP, 1)), 1)
    tap_stack = stacked_taps(padded, across, down, FORWARD_TAPS)
    convolved = jnp.einsum("pwhk,kd->pwhd", tap_stack, weight_spatial, preferred_element_type=WIDE)
    hidden_two = smooth(convolved).astype(LOW)
    expanded = jnp.einsum("pwhc,cd->pwhd", hidden_two, weight_expand, preferred_element_type=WIDE)
    summed_pre = image.astype(WIDE) + expanded
    feature_low = smooth(summed_pre).astype(LOW)
    visual_rows = jnp.einsum(
        "pwhc,cd->pwhd", feature_low, weight_proj, preferred_element_type=WIDE
    ).astype(LOW)
    visual_own = lax.all_to_all(visual_rows, CHIPS, split_axis=0, concat_axis=0, tiled=True)
    visual_own = (
        visual_own.reshape(dp_count, pair, across, down, width)
        .transpose(1, 2, 0, 3, 4)
        .reshape(pair, quarter, width)
    )
    visual_page = from_both(visual_own)

    sources = (text_page, visual_page)
    projected, attended, logs = [], [], []
    for stream in range(2):
        projected.append(dot(sources[stream], weight_in[stream]).astype(LOW))
        mixed, log_sum = attend_forward(projected[stream], around, size, group)
        attended.append(mixed)
        logs.append(log_sum)
    attended_both = jnp.concatenate(attended, axis=1)
    attention = add_both(dot(attended_both, weight_out, "nt"), quarter)
    first_sum = (
        own_tokens(text_page).astype(WIDE) + visual_own.reshape(-1, width).astype(WIDE) + attention
    )
    normed, first_pull = jax.vjp(layer_norm, first_sum, norm_params[0], norm_params[1])
    normed_low = from_both(normed.astype(LOW).reshape(pair, quarter, width))
    own_bias = lax.dynamic_index_in_dim(up_bias.reshape(pair, 2, units), core, 1, keepdims=False)
    hidden_pre = [dot(normed_low, weight_up[y]) + own_bias[y] for y in range(pair)]
    hidden_low = [smooth(pre).astype(LOW) for pre in hidden_pre]
    down_part = sum(dot(hidden_low[y], weight_down[y], "nt") for y in range(pair))
    second_sum = normed + (add_both(down_part, quarter) + norm_params[4])
    final_out, second_pull = jax.vjp(layer_norm, second_sum, norm_params[2], norm_params[3])
    out_low = final_out.astype(LOW)
    out_pages = by_side(("my", 1), out_low, swap(out_low, "my", 1), 0)
    out_pages = out_pages.reshape(pair, pair, quarter, width)
    out_pages = by_side(("core", 1), out_pages, swap(out_pages, "core", 1), 2)
    out_local = out_pages.reshape(text.shape)

    second_grad, gain_two, shift_two = second_pull(own_tokens(upstream_page).astype(WIDE))
    down_own = second_grad.astype(LOW)
    down_bias_grad = jnp.sum(down_own.astype(WIDE), axis=0)
    down_low = from_both(down_own.reshape(pair, quarter, width))
    hidden_grad_low = [
        smooth_back(hidden_pre[y], dot(down_low, weight_down[y])).astype(LOW) for y in range(pair)
    ]
    normed_part = sum(dot(hidden_grad_low[y], weight_up[y], "nt") for y in range(pair))
    up_part = jnp.stack([jnp.sum(part_low.astype(WIDE), axis=0) for part_low in hidden_grad_low])
    grad_down = jnp.concatenate([dot(down_low, hidden_low[y], "tn").astype(LOW) for y in range(pair)])
    grad_up = jnp.concatenate(
        [dot(normed_low, hidden_grad_low[y], "tn").astype(LOW) for y in range(pair)]
    )
    down_shard = scatter_rows(grad_down, ("my", "dx", "dz"), OWNERS)
    up_shard = scatter_rows(grad_up, ("dx", "my", "dz"), OWNERS)
    normed_grad = second_grad + add_both(normed_part, quarter)
    first_grad, gain_one, shift_one = first_pull(normed_grad)
    norm_part = jnp.stack([gain_one, shift_one, gain_two, shift_two, down_bias_grad])
    attention_low = from_both(first_grad.astype(LOW).reshape(pair, quarter, width))
    head_grads = dot(attention_low, weight_out).astype(LOW)
    grad_out = dot(attention_low, attended_both, "tn").astype(LOW)
    projected_grads, span_grads = [], []
    for stream in range(2):
        own_grads, span_part = attend_backward(
            projected[stream], around, attended[stream], logs[stream], head_grads, stream, size, group
        )
        projected_grads.append(own_grads)
        span_grads.append(span_part)
    source_own = [
        add_both(dot(projected_grads[stream], weight_in[stream], "nt"), quarter)
        for stream in range(2)
    ]
    visual_low = (first_grad + source_own[1]).astype(LOW)
    text_back = (first_grad + source_own[0]).reshape(pair, quarter, width)
    text_sent = lax.dynamic_index_in_dim(text_back, 1 - my, 0, keepdims=False)
    text_kept = lax.dynamic_index_in_dim(text_back, my, 0, keepdims=False)
    text_grad_local = by_side(
        ("my", 1), text_kept, swap(text_sent.astype(LOW), "my", 1).astype(WIDE), 0
    )
    visual_sent = (
        visual_low.reshape(pair, across, dp_count, down, width)
        .transpose(2, 0, 1, 3, 4)
        .reshape(pages, across, down, width)
    )
    visual_grad = lax.all_to_all(visual_sent, CHIPS, split_axis=0, concat_axis=0, tiled=True)
    grad_in = [
        dot(sources[stream], projected_grads[stream], "tn").astype(LOW).reshape(width, pair, 3 * part)
        for stream in range(2)
    ]
    grad_attn = jnp.concatenate(
        grad_in + [grad_out.reshape(width, 2, pair, part)[:, s] for s in range(2)], axis=2
    ).transpose(1, 0, 2)
    attn_cut = grad_attn.shape[2] // 2
    attn_shard = jnp.concatenate(
        [
            scatter_rows(
                grad_attn[:, :, :attn_cut].reshape(-1, attn_cut), ("my", "dx", "dz"), OWNERS
            ),
            scatter_rows(
                grad_attn[:, :, attn_cut:].reshape(-1, attn_cut), ("dx", "my", "dz"), OWNERS
            ),
        ],
        axis=1,
    )

    grad_proj = jnp.einsum("pwhc,pwhd->cd", feature_low, visual_grad, preferred_element_type=WIDE)
    feature_grad = jnp.einsum("pwhd,cd->pwhc", visual_grad, weight_proj, preferred_element_type=WIDE)
    pre_grad = smooth_back(summed_pre, feature_grad)
    expanded_low = pre_grad.astype(LOW)
    grad_expand = jnp.einsum("pwhc,pwhd->cd", hidden_two, expanded_low, preferred_element_type=WIDE)
    conv_grad = smooth_back(
        convolved,
        jnp.einsum("pwhd,cd->pwhc", expanded_low, weight_expand, preferred_element_type=WIDE),
    ).astype(LOW)
    back_padded = extended(conv_grad, ((DP, 2), (MP, 1)), 1)
    back_taps = stacked_taps(back_padded, across, down, BACKWARD_TAPS).reshape(
        conv_grad.shape[:3] + (9, middle)
    )
    reduced_grad = smooth_back(
        reduced,
        jnp.einsum(
            "pwhko,kio->pwhi",
            back_taps,
            weight_spatial.reshape(9, middle, middle),
            preferred_element_type=WIDE,
        ),
    ).astype(LOW)
    grad_spatial = jnp.einsum("pwhk,pwhd->kd", tap_stack, conv_grad, preferred_element_type=WIDE)
    grad_reduce = jnp.einsum("pwhc,pwhd->cd", image, reduced_grad, preferred_element_type=WIDE)
    image_grad_local = pre_grad + jnp.einsum(
        "pwhd,cd->pwhc", reduced_grad, weight_reduce, preferred_element_type=WIDE
    )
    grad_side = jnp.concatenate(
        [grad_expand.astype(LOW).reshape(-1, middle), grad_proj.astype(LOW)], axis=1
    )
    side_shard = scatter_rows(grad_side, ("core", "my", "dx", "dz"), AXES)
    spatial_shard = scatter_rows(grad_spatial.astype(LOW), ("core", "dx", "my", "dz"), AXES)
    reduce_shard = scatter_rows(grad_reduce.astype(LOW), ("core", "my", "dx", "dz"), AXES)
    expand_shard = side_shard[:, :middle].reshape(expand_weight.shape)
    proj_shard = side_shard[:, middle:]

    in_shard = attn_shard[:, : 6 * part].reshape(-1, 2, 3, part).transpose(1, 2, 0, 3)
    out_shard = attn_shard[:, 6 * part :].reshape(-1, 2, part).transpose(1, 2, 0)
    down_shard = down_shard.T
    image_sets = (
        (reduce_weight, reduce_shard, reduce_weight_rows, reduce_weight_cols),
        (spatial_weight, spatial_shard, spatial_weight_rows, spatial_weight_cols),
        (expand_weight, expand_shard, expand_weight_rows, expand_weight_cols),
        (visual_proj, proj_shard, visual_proj_rows, visual_proj_cols),
    )
    layer_sets = (
        (attn_in, in_shard, attn_in_rows, attn_in_cols, dp_count, mp_count, True),
        (attn_out, out_shard, attn_out_rows, attn_out_cols, mp_count, dp_count, False),
        (ffn_up, up_shard, ffn_up_rows, ffn_up_cols, dp_count, mp_count, True),
        (ffn_down, down_shard, ffn_down_rows, ffn_down_cols, mp_count, dp_count, False),
    )
    weight_squares = [jnp.sum(entry[0] * entry[0], axis=(-2, -1)) for entry in image_sets + layer_sets]
    rows_before = [jnp.sum(entry[2], axis=-1) for entry in image_sets] + [
        jnp.sum(entry[2], axis=-1) / (entry[5]) for entry in layer_sets
    ]
    early = weight_squares + rows_before
    early_sums = unpack(total_over(pack(early), AXES), early)
    weight_squares, rows_before = early_sums[:8], early_sums[8:]

    row_parts = [jnp.sum(entry[1] * entry[1], axis=-1) for entry in layer_sets]
    col_parts = [jnp.sum(entry[1] * entry[1], axis=-2) for entry in layer_sets]
    over_dp = [(cols if entry[6] else rows) for rows, cols, entry in zip(row_parts, col_parts, layer_sets)]
    over_mp = [(rows if entry[6] else cols) for rows, cols, entry in zip(row_parts, col_parts, layer_sets)]
    dp_sums = unpack(total_over(pack(over_dp), DP), over_dp)
    mp_sums = unpack(total_over(pack(over_mp), MP), over_mp)
    squares_total = [jnp.sum(rows, axis=-1) for rows in row_parts]
    span_sum = span_grads[0] + span_grads[1]
    span_sum = jnp.stack([span_sum[:, :NB, :NB], span_sum[:, NB : 2 * NB, NB : 2 * NB]])
    table_part = jnp.einsum("abr,thba->trh", bucket_select, span_sum, precision=PRECISE)
    table_term = jnp.zeros(tables.shape[:2] + (pair, 2, group), WIDE)
    table_term = lax.dynamic_update_slice(
        table_term, table_part.reshape(tables.shape[:2] + (pair, 1, group)), (0, 0, 0, core, 0)
    ).reshape(tables.shape)
    up_term = lax.dynamic_update_slice(
        jnp.zeros((pair, 2, units), WIDE), up_part[:, None], (0, core, 0)
    ).reshape(up_bias.shape)
    middle_terms = [norm_part, up_term, table_term] + squares_total
    middle_sums = unpack(total_over(pack(middle_terms), AXES), middle_terms)
    norm_gradient, up_gradient, table_gradient = middle_sums[:3]
    squares_total = middle_sums[3:]
    late = [jnp.sum(entry[1] * entry[1], axis=-2) for entry in image_sets]
    image_cols = unpack(total_over(pack(late), AXES), late)

    decay_rate = 1.0 - STEP ** (-0.8)
    results = []
    for number, (weight, gradient, rows_old, cols_old) in enumerate(image_sets):
        sizes = (weight.shape[0] * dp_count * mp_count, weight.shape[1])
        rows_sum = jnp.sum(gradient * gradient, axis=-1)
        mean = (
            decay_rate * rows_before[number]
            + (1.0 - decay_rate) * jnp.sum(image_cols[number], axis=-1) / sizes[1]
        ) / sizes[0]
        results.append(
            factored_step(
                weight, gradient, rows_old, cols_old, rows_sum, image_cols[number], mean,
                weight_squares[number] / (sizes[0] * sizes[1]), sizes,
            )
        )
    for number, (weight, gradient, rows_old, cols_old, row_split, col_split, flag) in enumerate(layer_sets):
        sizes = (weight.shape[-2] * row_split, weight.shape[-1] * col_split)
        rows_sum = mp_sums[number] if flag else dp_sums[number]
        cols_sum = dp_sums[number] if flag else mp_sums[number]
        mean = (
            decay_rate * rows_before[4 + number]
            + (1.0 - decay_rate) * squares_total[number] / sizes[1]
        ) / sizes[0]
        results.append(
            factored_step(
                weight, gradient, rows_old, cols_old, rows_sum, cols_sum, mean,
                weight_squares[4 + number] / (sizes[0] * sizes[1]), sizes,
            )
        )
    norm_parts = moment_step(norm_params, norm_gradient, norm_moment, (1,))
    bias_parts = moment_step(up_bias, up_gradient, up_moment, (0,))
    table_parts = moment_step(tables, table_gradient, table_moment, (1, 2))
    flat = [value for result in results for value in result]
    return (
        (out_local, text_grad_local, image_grad_local)
        + tuple(flat)
        + norm_parts
        + bias_parts
        + table_parts
    )


def solution(mesh):
    whole = mesh.shape["dp"], mesh.shape["mp"]
    devices = mesh.devices.reshape(whole[0] // 2, 2, whole[1] // 2, 2)
    flat, rows, none = P(AXES, None), P(AXES), P()
    image_weight_in = (flat, rows, none)
    image_weight_out = (flat, flat, rows, none, flat)
    in_spec, in_rows, in_cols = P(None, None, DP, MP), P(None, None, DP), P(None, None, MP)
    out_spec, out_rows, out_cols = P(None, MP, DP), P(None, MP), P(None, DP)
    up_spec, up_rows, up_cols = P(DP, MP), P(DP), P(MP)
    down_spec, down_rows, down_cols = P(MP, DP), P(MP), P(DP)
    placed = (
        (P(None, MP, DP, None), P(DP, None, None), P(DP, None, None), P(DP, None), P(DP, None, None))
        + image_weight_in * 4
        + (in_spec, in_rows, in_cols, out_spec, out_rows, out_cols)
        + (up_spec, up_rows, up_cols, down_spec, down_rows, down_cols)
        + (none,) * 6
    )
    given = (
        (P(DP, None, None), P(DP, MP, None), P(None, MP, DP, None))
        + image_weight_out * 4
        + (in_spec, in_spec, in_rows, in_cols, in_spec)
        + (out_spec, out_spec, out_rows, out_cols, out_spec)
        + (up_spec, up_spec, up_rows, up_cols, up_spec)
        + (down_spec, down_spec, down_rows, down_cols, down_spec)
        + (none,) * 9
    )
    return jax.shard_map(
        on_device, mesh=Mesh(devices, AXES), in_specs=placed, out_specs=given, check_vma=False
    )
```

```python
import functools

import jax
import jax.numpy as jnp
from jax import lax
from jax.experimental import pallas as pl
from jax.experimental.pallas import tpu as pltpu
from jax.sharding import Mesh
from jax.sharding import PartitionSpec as P

NB = 32
STEP = 5
NEGATIVE = -1000000000.0
SAFE = 2.0e8
NT = (((1,), (1,)), ((), ()))
NN = (((1,), (0,)), ((), ()))


def mm(a, b, dims=NN):
    return lax.dot_general(a, b, dims, preferred_element_type=jnp.float32)


def column(refs, head, kind, group, size):
    start = (kind * group + head % group) * size
    return refs[head // group].at[:, start : start + size]


def stage_heads(p_refs, kx_ref, tab_ref, q_scr, k_scr, heads, group, size):
    kx = kx_ref[...]
    for h in range(heads):
        mixed = mm(kx, tab_ref[h]).astype(jnp.bfloat16)
        q_scr[h, :, : 256 - size] = mixed[:, : 256 - size]
        q_scr[h, :, 256 - size :] = column(p_refs, h, 0, group, size)[...] * jnp.bfloat16(size**-0.5)
        k_scr[h, :, :128] = kx
        k_scr[h, :, 128 : 256 - size] = kx[:, : 128 - size]
        k_scr[h, :, 256 - size :] = column(p_refs, h, 1, group, size)[...]


def bound_ok(q_scr, k_scr, heads, size):
    big_q, big_k = 0.0, 0.0
    for h in range(heads):
        big_q = jnp.maximum(big_q, jnp.max(jnp.abs(q_scr[h, :, 256 - size :].astype(jnp.float32))))
        big_k = jnp.maximum(big_k, jnp.max(jnp.abs(k_scr[h, :, 256 - size :].astype(jnp.float32))))
    return big_q * big_k * size < SAFE


def window(win_ref, chunk, exact, length, tile):
    if exact:
        return 0, length // tile
    return pl.multiple_of(win_ref[0, chunk], 128), win_ref[1, chunk]


def sweep(count, tile, body, carry):
    carry = lax.fori_loop(0, count // 2, lambda t, c: body(t * 2 * tile, 2 * tile, c), carry)
    return lax.fori_loop(
        0, count % 2, lambda t, c: body(count // 2 * 2 * tile, tile, c), carry
    )


def forward_kernel(*refs, heads, group, size, chunk_rows, tile, beside):
    p_refs = refs[: heads // group]
    (
        win_ref, kx_ref, tab_ref, segc_ref, segr_ref, o_ref, lse_ref,
        q_scr, k_scr, vt_scr, s_scr, ot_scr,
    ) = refs[heads // group :]
    length = kx_ref.shape[0]
    chunks = length // chunk_rows
    stage_heads(p_refs, kx_ref, tab_ref, q_scr, k_scr, heads, group, size)
    for h in range(heads):
        values = column(p_refs, h, 2, group, size)[...]
        vt_scr[h] = values.astype(jnp.float32).T.astype(jnp.bfloat16)
    safe = bound_ok(q_scr, k_scr, heads, size)
    lse_ref[...] = jnp.zeros_like(lse_ref)

    def run(exact):
        def one_chunk(item, _):
            lead, c = (0, item) if beside == heads else (item // chunks * beside, item % chunks)
            start, count = window(win_ref, c, exact, length, tile)
            first = pl.multiple_of(c * chunk_rows, chunk_rows)
            queries = pl.ds(first, chunk_rows)

            def score(at, tile, tops):
                row = pl.multiple_of(at, 128)
                src = pl.multiple_of(start + at, 128)
                found = []
                for u in range(beside):
                    s = mm(k_scr[lead + u, pl.ds(src, tile), :], q_scr[lead + u, queries, :], NT)
                    if exact:
                        s = jnp.where(segc_ref[pl.ds(src, tile), :1] == segr_ref[:, queries], s, NEGATIVE)
                    s_scr[u, pl.ds(row, tile), :] = s
                    found.append(
                        jnp.maximum(tops[u], jnp.max(s.reshape(tile // 8, 8, chunk_rows), axis=0))
                    )
                return tuple(found)

            tops = sweep(
                count, tile, score, (jnp.full((8, chunk_rows), -3.0e38, jnp.float32),) * beside
            )
            tops = [jnp.max(top, axis=0, keepdims=True) for top in tops]
            ot_scr[pl.ds(lead, beside), :, queries] = jnp.zeros((beside, size, chunk_rows), jnp.float32)

            def mix(at, tile, totals):
                row = pl.multiple_of(at, 128)
                src = pl.multiple_of(start + at, 128)
                found = []
                for u in range(beside):
                    p = jnp.exp(s_scr[u, pl.ds(row, tile), :] - tops[u])
                    found.append(totals[u] + jnp.sum(p.reshape(tile // 8, 8, chunk_rows), axis=0))
                    ot_scr[lead + u, :, queries] += mm(
                        vt_scr[lead + u, :, pl.ds(src, tile)], p.astype(jnp.bfloat16)
                    )
                return tuple(found)

            totals = sweep(
                count, tile, mix, (jnp.zeros((8, chunk_rows), jnp.float32),) * beside
            )
            for u in range(beside):
                total = jnp.sum(totals[u], axis=0, keepdims=True)
                lse_ref[pl.ds(lead + u, 1), queries] = tops[u] + jnp.log(total)
                ot_scr[lead + u, :, queries] = ot_scr[lead + u, :, queries] / total
            return 0

        lax.fori_loop(0, heads // beside * chunks, one_chunk, 0)

    pl.when(safe)(functools.partial(run, False))
    pl.when(jnp.logical_not(safe))(functools.partial(run, True))
    for h in range(heads):
        o_ref[:, h * size : (h + 1) * size] = ot_scr[h].T.astype(jnp.bfloat16)


def backward_kernel(*refs, heads, group, size, chunk_rows, tile, offset, beside):
    groups = heads // group
    p_refs, refs = refs[:groups], refs[groups:]
    win_ref, kx_ref, tab_ref, segc_ref, segr_ref, o_ref, lse_ref, g_ref = refs[:8]
    d_refs, span_ref = refs[8 : 8 + groups], refs[8 + groups]
    q_scr, k_scr, kt_scr, v_scr, g_scr, dk_scr, dv_scr, dq_scr, dl_scr = refs[9 + groups :]
    length = kx_ref.shape[0]
    chunks = length // chunk_rows
    stage_heads(p_refs, kx_ref, tab_ref, q_scr, k_scr, heads, group, size)
    safe = bound_ok(q_scr, k_scr, heads, size)
    for h in range(heads):
        kt_scr[h] = k_scr[h, :, 128:].astype(jnp.float32).T.astype(jnp.bfloat16)
        v_scr[h] = column(p_refs, h, 2, group, size)[...]
        g = g_ref[:, offset + h * size : offset + (h + 1) * size]
        g_scr[h] = g
        o = o_ref[:, h * size : (h + 1) * size]
        mixed = g.astype(jnp.float32) * o.astype(jnp.float32)
        dl_scr[pl.ds(h, 1), :] = jnp.sum(mixed.T, axis=0, keepdims=True)
    dk_scr[...] = jnp.zeros_like(dk_scr)
    dv_scr[...] = jnp.zeros_like(dv_scr)
    dq_scr[...] = jnp.zeros_like(dq_scr)

    def run(exact):
        def one_chunk(item, _):
            lead, c = (0, item) if beside == heads else (item // chunks * beside, item % chunks)
            start, count = window(win_ref, c, exact, length, tile)
            first = pl.multiple_of(c * chunk_rows, chunk_rows)
            queries = pl.ds(first, chunk_rows)

            def step(at, tile, _):
                keys = pl.ds(pl.multiple_of(start + at, 128), tile)
                for u in range(beside):
                    h = lead + u
                    g = g_scr[h, queries, :]
                    s = mm(k_scr[h, keys, :], q_scr[h, queries, :], NT)
                    if exact:
                        s = jnp.where(segc_ref[keys, :1] == segr_ref[:, queries], s, NEGATIVE)
                    p = jnp.exp(s - lse_ref[pl.ds(h, 1), queries])
                    dp = mm(v_scr[h, keys, :], g, NT)
                    ds = (p * (dp - dl_scr[pl.ds(h, 1), queries])).astype(jnp.bfloat16)
                    dv_scr[h, keys, :] += mm(p.astype(jnp.bfloat16), g)
                    dk_scr[h, keys, :] += mm(ds, q_scr[h, queries, 256 - size :])
                    dq_scr[h, :, queries] += mm(kt_scr[h, :, keys], ds)
                return 0

            return sweep(count, tile, step, 0)

        lax.fori_loop(0, heads // beside * chunks, one_chunk, 0)

    pl.when(safe)(functools.partial(run, False))
    pl.when(jnp.logical_not(safe))(functools.partial(run, True))
    for h in range(heads):
        own, keys, values = (column(d_refs, h, kind, group, size) for kind in range(3))
        own[...] = (dq_scr[h, 128 - size :, :] * size**-0.5).T.astype(jnp.bfloat16)
        keys[...] = dk_scr[h].astype(jnp.bfloat16)
        values[...] = dv_scr[h].astype(jnp.bfloat16)
        thr = dq_scr[h, : 128 - size, :]
        upper = thr.astype(jnp.bfloat16)
        lower = (thr - upper.astype(jnp.float32)).astype(jnp.bfloat16)
        span_ref[h] = mm(upper, kx_ref[...]) + mm(lower, kx_ref[...])


CHUNK = 256
TILE = 256
VMEM = pltpu.VMEM


def attend_forward(proj, around, size):
    length, total = proj[0].shape
    group = total // (3 * size)
    heads = len(proj) * group
    full = pl.BlockSpec(memory_space=pltpu.VMEM)
    return pl.pallas_call(
        functools.partial(
            forward_kernel, heads=heads, group=group, size=size, chunk_rows=CHUNK, tile=TILE,
            beside=heads,
        ),
        in_specs=[full] * len(proj) + [pl.BlockSpec(memory_space=pltpu.SMEM)] + [full] * 4,
        out_specs=[full, full],
        out_shape=[
            jax.ShapeDtypeStruct((length, heads * size), jnp.bfloat16),
            jax.ShapeDtypeStruct((8, length), jnp.float32),
        ],
        scratch_shapes=[
            VMEM((heads, length, 256), jnp.bfloat16),
            VMEM((heads, length, 256), jnp.bfloat16),
            VMEM((heads, size, length), jnp.bfloat16),
            VMEM((heads, length, CHUNK), jnp.float32),
            VMEM((heads, size, length), jnp.float32),
        ],
        compiler_params=pltpu.CompilerParams(vmem_limit_bytes=48 * 1024 * 1024),
        cost_estimate=pl.CostEstimate(flops=0, bytes_accessed=0, transcendentals=0),
    )(*proj, *around)


def attend_backward(proj, around, out, lse, grads, stream, size):
    length, total = proj[0].shape
    group = total // (3 * size)
    heads = len(proj) * group
    full = pl.BlockSpec(memory_space=pltpu.VMEM)
    found = pl.pallas_call(
        functools.partial(
            backward_kernel, heads=heads, group=group, size=size, chunk_rows=CHUNK, tile=TILE,
            offset=stream * heads * size, beside=heads,
        ),
        in_specs=[full] * len(proj) + [pl.BlockSpec(memory_space=pltpu.SMEM)] + [full] * 7,
        out_specs=[full] * (len(proj) + 1),
        out_shape=[jax.ShapeDtypeStruct((length, total), jnp.bfloat16)] * len(proj)
        + [jax.ShapeDtypeStruct((heads, 128 - size, 128), jnp.float32)],
        scratch_shapes=[
            VMEM((heads, length, 256), jnp.bfloat16),
            VMEM((heads, length, 256), jnp.bfloat16),
            VMEM((heads, 128, length), jnp.bfloat16),
            VMEM((heads, length, size), jnp.bfloat16),
            VMEM((heads, length, size), jnp.bfloat16),
            VMEM((heads, length, size), jnp.float32),
            VMEM((heads, length, size), jnp.float32),
            VMEM((heads, 128, length), jnp.float32),
            VMEM((8, length), jnp.float32),
        ],
        compiler_params=pltpu.CompilerParams(vmem_limit_bytes=56 * 1024 * 1024),
        cost_estimate=pl.CostEstimate(flops=0, bytes_accessed=0, transcendentals=0),
    )(*proj, *around, out, lse, grads)
    return found[:-1], found[-1]


def attention_windows(segment_row, chunk_rows, tile):
    length = segment_row.shape[0]
    heads_of = segment_row[::chunk_rows]
    tails_of = segment_row[chunk_rows - 1 :: chunk_rows]
    low = jnp.sum((segment_row[None, :] < heads_of[:, None]).astype(jnp.int32), axis=1)
    high = jnp.sum((segment_row[None, :] <= tails_of[:, None]).astype(jnp.int32), axis=1)
    start = low // 128 * 128
    count = (high - start + tile - 1) // tile
    start = jnp.minimum(start, length - count * tile)
    return jnp.stack([start, count]).astype(jnp.int32)


def attention_tables(span_tables):
    _, heads, buckets, _ = span_tables.shape
    upper = lax.reduce_precision(span_tables, 8, 7)
    lower = (span_tables - upper).astype(jnp.bfloat16)
    def diag(t):
        z = jnp.zeros_like(t[0])
        return jnp.concatenate([jnp.concatenate([t[0], z], 2), jnp.concatenate([z, t[1]], 2)], 1)
    hi, lo = diag(upper.astype(jnp.bfloat16)), diag(lower)
    level = jnp.arange(64)
    away = jnp.where((level[:, None] != level[None, :]), NEGATIVE, 0.0)
    segs = jnp.where((level[:, None] < 4) & (level[None, :] < 4), away, 0.0).astype(jnp.bfloat16)
    segs = jnp.broadcast_to(segs[None], (heads, 64, 64))
    zero = jnp.zeros((heads, 64, 64), jnp.bfloat16)
    top = jnp.concatenate([hi, zero, lo, zero], 2)
    bottom = jnp.concatenate([zero, segs, zero, zero], 2)
    return jnp.concatenate([top, bottom], 1)


def token_marks(boxes_page, segment_row, buckets):
    levels = jnp.arange(buckets, dtype=jnp.int32)[None, :]
    kinds = jnp.arange(64, dtype=jnp.int32)[None, :]
    return jnp.concatenate(
        [boxes_page[0][:, None] == levels, boxes_page[1][:, None] == levels, segment_row[:, None] == kinds],
        axis=1,
    ).astype(jnp.bfloat16)


NORM_EPS = 1e-05
RELATIVE = 0.5
RATE_FLOOR = 0.001
PRECISE = lax.Precision.HIGHEST
LOW = jnp.bfloat16
WIDE = jnp.float32
AXES = ("dz", "dx", "my", "core")
DP = ("dz", "dx")
MP = ("my", "core")
CHIPS = ("dz", "dx", "my")
OWNERS = ("my", "dz", "dx")
FORWARD_TAPS = tuple((col, row) for col in range(3) for row in range(3))
BACKWARD_TAPS = tuple((2 - col, 2 - row) for col in range(3) for row in range(3))


def swap(values, axis, reach):
    count = lax.axis_size(axis)
    return lax.ppermute(values, axis, [(i, i ^ reach) for i in range(count)])


def exchange(values, flips):
    if len({axis for axis, _ in flips}) == 1:
        return swap(values, flips[0][0], sum(reach for _, reach in flips))
    (one, far), (two, near) = flips
    count = lax.axis_size(two)
    pairs = [
        (i * count + k, (i ^ far) * count + (k ^ near))
        for i in range(lax.axis_size(one))
        for k in range(count)
    ]
    return lax.ppermute(values, (one, two), pairs)


def bits_of(axis):
    reach, found = lax.axis_size(axis) // 2, []
    while reach:
        found.append((axis, reach))
        reach //= 2
    return found


def bits(axes):
    return [bit for axis in axes for bit in bits_of(axis)]


def rounds_of(order):
    found = []
    for axes in order:
        places = bits(axes)
        found += [tuple(places[n : n + 2]) for n in range(0, len(places), 2)]
    return found


def flips_of(group):
    return [(bit,) for bit in group] + ([group] if len(group) == 2 else [])


def side(bit):
    return lax.axis_index(bit[0]) // bit[1] % 2


def tie(values, *after):
    if not after:
        return values
    return lax.optimization_barrier((values,) + after)[0]


class Gather:
    def __init__(self, shard, order, owners):
        self.places = bits(owners)
        self.rounds = rounds_of(order)[::-1]
        self.sides = [side(place) for place in self.places]
        self.shape = shard.shape
        self.done = []
        self.held = shard.reshape((1,) * len(self.places) + shard.shape)
        whole = jnp.zeros((2,) * len(self.places) + shard.shape, shard.dtype)
        self.whole = lax.dynamic_update_slice(whole, self.held, self.corner())

    def corner(self, flips=()):
        return [
            0 if place in self.done else (1 - mine if place in flips else mine)
            for place, mine in zip(self.places, self.sides)
        ] + [0] * len(self.shape)

    def step(self, before=(), fill=()):
        group = self.rounds.pop()
        sent = tie(self.held, *before)
        arrived = []
        for flips in flips_of(group):
            got = tie(exchange(sent, flips), *fill)
            self.whole = lax.dynamic_update_slice(self.whole, got, self.corner(flips))
            arrived.append(got)
        self.done += group
        if self.rounds:
            sizes = [2 if place in self.done else 1 for place in self.places] + list(self.shape)
            self.held = lax.dynamic_slice(self.whole, self.corner(), sizes)
        return tuple(arrived)

    def value(self):
        return self.whole.reshape((-1,) + self.shape[1:])


class Scatter:
    def __init__(self, blocks, order, owners, axis=0):
        self.live = bits(owners)
        self.count = len(self.live)
        self.rounds = rounds_of(order)[::-1]
        self.parts = [value.reshape((2,) * self.count + (-1,) + value.shape[1:]) for value in blocks]
        self.axis = self.count + axis
        self.held = None
        self.busy = False

    def pick(self, group, flips):
        def cut(value):
            for bit in group:
                mine = side(bit)
                place = 1 - mine if bit in flips else mine
                value = lax.dynamic_slice_in_dim(value, place, 1, self.live.index(bit))
            return value

        if self.held is None:
            return jnp.concatenate([cut(value) for value in self.parts], axis=self.axis)
        return sum(cut(value).astype(WIDE) for value in self.held).astype(LOW)

    def send(self, *after):
        group = self.rounds.pop()
        self.flying = tuple(
            exchange(tie(self.pick(group, flips), *after), flips) for flips in flips_of(group)
        )
        self.kept = self.pick(group, ())
        for bit in group:
            self.live[self.live.index(bit)] = None
        self.busy = True
        return self

    def take(self, *after):
        if self.busy:
            flying = lax.optimization_barrier(self.flying + after)[: len(self.flying)]
            self.held = [self.kept] + list(flying)
            self.busy = False
        return self

    def step(self, *after):
        self.take(*after)
        return self.send() if self.rounds else self

    def land(self, values):
        found = lax.optimization_barrier((values,) + self.flying)
        self.held = [self.kept] + list(found[1:])
        self.busy = False
        if self.rounds:
            self.send()
        return found[0]

    def value(self):
        total = sum(value.astype(WIDE) for value in self.held)
        return total.reshape(total.shape[self.count :])


def total_over(values, axes):
    for bit in bits(axes):
        values = values + swap(values, *bit)
    return values


def by_side(bit, own, other, axis):
    return jnp.where(
        side(bit) == 0, jnp.stack([own, other], axis), jnp.stack([other, own], axis)
    )


def own_quarters(page, quarter):
    parts = page.reshape((-1, 2, quarter) + page.shape[1:])
    own = lax.dynamic_index_in_dim(parts, lax.axis_index("core"), 1, keepdims=False)
    return own.reshape((-1,) + page.shape[1:])


def add_both(partial, quarter, *after):
    parts = partial.reshape((-1, 2, quarter) + partial.shape[1:])
    core = lax.axis_index("core")
    sent = lax.dynamic_index_in_dim(parts, 1 - core, 1, keepdims=False)
    kept = lax.dynamic_index_in_dim(parts, core, 1, keepdims=False)
    got = tie(swap(sent.astype(LOW), "core", 1), *after)
    return (kept + got.astype(WIDE)).reshape((-1,) + partial.shape[1:])


def extended(cells, sides, width):
    for axis, dim in sides:
        count = lax.axis_size(axis)
        ends = count - 1
        head = lax.slice_in_dim(cells, 0, width, axis=dim)
        tail = lax.slice_in_dim(cells, cells.shape[dim] - width, cells.shape[dim], axis=dim)
        cells = jnp.concatenate(
            [
                lax.ppermute(tail, axis, [(i, i + 1) for i in range(ends)]),
                cells,
                lax.ppermute(head, axis, [(i + 1, i) for i in range(ends)]),
            ],
            axis=dim,
        )
    return cells


def smooth(values):
    return jax.nn.gelu(values, approximate=True)


def smooth_back(values, upstream):
    return jax.vjp(smooth, values)[1](upstream)[0]


def row_mean(values):
    return jnp.mean(values, axis=-1, keepdims=True)


def first_norm_kernel(text_ref, visual_ref, mine_ref, other_ref, params_ref, hat_ref, scale_ref, low_ref):
    first = text_ref[...].astype(WIDE) + visual_ref[...].astype(WIDE)
    first = first + (mine_ref[...].astype(WIDE) + other_ref[...].astype(WIDE))
    centre = first - row_mean(first)
    scale = lax.rsqrt(row_mean(centre * centre) + NORM_EPS)
    hat = centre * scale
    hat_ref[...] = hat
    scale_ref[...] = scale
    low_ref[...] = (hat * params_ref[0:1, :] + params_ref[1:2, :]).astype(LOW)


def second_norm_kernel(hat_ref, mine_ref, other_ref, upstream_ref, params_ref, out_ref, grad_ref, low_ref, sums_ref):
    normed = hat_ref[...] * params_ref[0:1, :] + params_ref[1:2, :]
    down = mine_ref[...].astype(WIDE) + other_ref[...].astype(WIDE)
    second = normed + (down + params_ref[4:5, :])
    centre = second - row_mean(second)
    scale = lax.rsqrt(row_mean(centre * centre) + NORM_EPS)
    hat = centre * scale
    out_ref[...] = (hat * params_ref[2:3, :] + params_ref[3:4, :]).astype(LOW)
    upstream = upstream_ref[...].astype(WIDE)
    inner = upstream * params_ref[2:3, :]
    grad = scale * (inner - row_mean(inner) - hat * row_mean(inner * hat))
    grad_ref[...] = grad
    low = grad.astype(LOW)
    low_ref[...] = low
    sums_ref[0:1, :] += jnp.sum(upstream * hat, axis=0, keepdims=True)
    sums_ref[1:2, :] += jnp.sum(upstream, axis=0, keepdims=True)
    sums_ref[2:3, :] += jnp.sum(low.astype(WIDE), axis=0, keepdims=True)


def first_back_kernel(grad_ref, mine_ref, other_ref, hat_ref, scale_ref, params_ref, first_ref, low_ref, sums_ref):
    upstream = grad_ref[...] + (mine_ref[...].astype(WIDE) + other_ref[...].astype(WIDE))
    hat = hat_ref[...]
    inner = upstream * params_ref[0:1, :]
    grad = scale_ref[...] * (inner - row_mean(inner) - hat * row_mean(inner * hat))
    first_ref[...] = grad
    low_ref[...] = grad.astype(LOW)
    sums_ref[0:1, :] += jnp.sum(upstream * hat, axis=0, keepdims=True)
    sums_ref[1:2, :] += jnp.sum(upstream, axis=0, keepdims=True)


def row_kernel(kernel, rows, given, made):
    length = given[0].shape[0]
    shapes = [value.shape for value in given] + [shape for shape, _ in made]

    def body(*refs):
        def block(number, _):
            here = pl.ds(pl.multiple_of(number * rows, rows), rows)
            kernel(*(ref.at[here] if shape[0] == length else ref for ref, shape in zip(refs, shapes)))
            return 0

        for ref, shape in zip(refs[len(given) :], shapes[len(given) :]):
            if shape[0] != length:
                ref[...] = jnp.zeros_like(ref)
        lax.fori_loop(0, length // rows, block, 0)

    whole = pl.BlockSpec(memory_space=pltpu.VMEM)
    return pl.pallas_call(
        body,
        in_specs=[whole] * len(given),
        out_specs=[whole] * len(made),
        out_shape=[jax.ShapeDtypeStruct(shape, kind) for shape, kind in made],
        compiler_params=pltpu.CompilerParams(vmem_limit_bytes=32 * 1024 * 1024),
        cost_estimate=pl.CostEstimate(flops=0, bytes_accessed=0, transcendentals=0),
    )(*given)


def relative_select(buckets, reach_max):
    offsets = (
        jnp.arange(buckets, dtype=jnp.int32)[None, :]
        - jnp.arange(buckets, dtype=jnp.int32)[:, None]
    )
    clipped = jnp.clip(offsets, -reach_max, reach_max) + reach_max
    return (
        clipped[:, :, None] == jnp.arange(2 * reach_max + 1, dtype=jnp.int32)[None, None, :]
    ).astype(WIDE)


def stacked_taps(padded, across, downward, anchors):
    return jnp.concatenate(
        [
            padded[:, from_col : from_col + across, from_row : from_row + downward, :]
            for from_col, from_row in anchors
        ],
        axis=-1,
    )


def dot(left, right, dims="nn"):
    first = 0 if dims[0] == "t" else 1
    second = 1 if dims[1] == "t" else 0
    return lax.dot_general(
        left, right, (((first,), (second,)), ((), ())), preferred_element_type=WIDE
    )


def factored_step(weight, gradient, rows_old, cols_old, row_piece, col_piece, row_mean, weight_mean, sizes):
    decay_rate = 1.0 - STEP ** (-0.8)
    rows_next = decay_rate * rows_old + (1.0 - decay_rate) * row_piece / sizes[1]
    cols_next = decay_rate * cols_old + (1.0 - decay_rate) * col_piece / sizes[0]
    second = rows_next[..., :, None] * cols_next[..., None, :] / row_mean[..., None, None]
    step_rate = RELATIVE * jnp.maximum(RATE_FLOOR, jnp.sqrt(weight_mean))
    weight_next = weight - step_rate[..., None, None] * (gradient * lax.rsqrt(second))
    return (gradient, weight_next, rows_next, cols_next, weight_next.astype(LOW))


def moment_step(parameter, gradient, moment, reduce_axes):
    decay_rate = 1.0 - STEP ** (-0.8)
    moment_next = decay_rate * moment + (1.0 - decay_rate) * gradient * gradient
    rms_value = jnp.sqrt(jnp.mean(parameter * parameter, axis=reduce_axes, keepdims=True))
    return (
        gradient,
        moment_next,
        parameter
        - RELATIVE * jnp.maximum(RATE_FLOOR, rms_value) * gradient * lax.rsqrt(moment_next),
    )


def pack(parts):
    flat = [part.reshape(-1) for part in parts]
    return jnp.concatenate(
        [jnp.pad(part, (0, -part.size % 1024)).reshape(-1, 8, 128) for part in flat]
    )


def unpack(packed, like):
    found, cursor = [], 0
    for part in like:
        tiles = -(-part.size // 1024)
        flat = packed[cursor : cursor + tiles].reshape(-1)
        found.append(flat[: part.size].reshape(part.shape))
        cursor += tiles
    return found


def join(parts):
    return jnp.concatenate([part.reshape(-1) for part in parts])


def split(flat, like):
    found, cursor = [], 0
    for part in like:
        found.append(flat[cursor : cursor + part.size].reshape(part.shape))
        cursor += part.size
    return found


def on_device(
    image, text, cotangent, segments, boxes,
    reduce_weight, reduce_weight_rows, reduce_weight_cols,
    spatial_weight, spatial_weight_rows, spatial_weight_cols,
    expand_weight, expand_weight_rows, expand_weight_cols,
    visual_proj, visual_proj_rows, visual_proj_cols,
    attn_in, attn_in_rows, attn_in_cols,
    attn_out, attn_out_rows, attn_out_cols,
    ffn_up, ffn_up_rows, ffn_up_cols,
    ffn_down, ffn_down_rows, ffn_down_cols,
    norm_params, norm_moment, up_bias, up_moment, tables, table_moment,
):
    dp_count = lax.axis_size(DP)
    pair = lax.axis_size("my")
    mp_count = 2 * pair
    my, core = lax.axis_index("my"), lax.axis_index("core")
    mp_index = lax.axis_index(MP)
    length, width = text.shape[1:]
    quarter = length // mp_count
    heads = tables.shape[2]
    size = width // heads
    group = heads // mp_count
    part = group * size
    units = ffn_up.shape[1]
    pages, across, down, channels = image.shape
    middle = spatial_weight.shape[1]

    flat_in = attn_in.astype(LOW).transpose(2, 0, 1, 3).reshape(attn_in.shape[2], 2, 3 * part)
    flat_out = attn_out.astype(LOW).transpose(2, 0, 1)
    layer_in = [
        jnp.concatenate([flat_in[:, stream], flat_out[:, stream]], axis=1) for stream in range(2)
    ]
    layer_ffn = jnp.concatenate([ffn_up.astype(LOW), ffn_down.astype(LOW).T], axis=1)
    base = visual_proj.shape[0]
    spatial_low = spatial_weight.astype(LOW)
    blocks, extra = divmod(spatial_low.shape[0], base)
    section_low = [spatial_low[n * base : (n + 1) * base] for n in range(blocks)]
    section_low.append(spatial_low[blocks * base :].reshape(base, -1))
    section_low.append(expand_weight.astype(LOW).reshape(base, middle))
    section_low.append(visual_proj.astype(LOW))
    section_low.append(reduce_weight.astype(LOW))
    section_low = jnp.concatenate(section_low, axis=1)
    section_whole = lax.all_gather(section_low, AXES, axis=0, tiled=True)
    ffn_whole = lax.all_gather(layer_ffn, OWNERS, axis=0, tiled=True).reshape(pair, width, -1)
    old_weights = (reduce_weight, spatial_weight, expand_weight, visual_proj, attn_in, attn_out, ffn_up, ffn_down)
    old_rows = (
        reduce_weight_rows, spatial_weight_rows, expand_weight_rows, visual_proj_rows,
        attn_in_rows, attn_out_rows, ffn_up_rows, ffn_down_rows,
    )
    copies = (1, 1, 1, 1, mp_count, dp_count, mp_count, dp_count)
    halves = [Gather(half, (("dz",), ("dx", "my")), OWNERS) for half in layer_in]
    while len(halves[0].rounds) > 1:
        for half in halves:
            half.step()
    old_parts = [jnp.sum(weight * weight, axis=(-2, -1)) for weight in old_weights]
    old_parts += [jnp.sum(rows, axis=-1) / times for rows, times in zip(old_rows, copies)]
    old_sums = join(old_parts)

    section_whole = section_whole.reshape(dp_count * mp_count, base, -1)
    ends = [blocks * middle, extra * middle // base, middle, width, middle]
    ends = [sum(ends[: n + 1]) for n in range(len(ends))]
    weight_reduce = section_whole[:, :, ends[3] :].reshape(channels, middle)
    halves[0].step()
    first_wait = (halves[0].whole, old_sums)
    reduced = jnp.einsum(
        "pwhc,cd->pwhd",
        tie(image, *first_wait),
        weight_reduce,
        preferred_element_type=WIDE,
    )
    hidden_one = smooth(reduced).astype(LOW)
    beside = extended(hidden_one, ((DP, 2),), 1)
    section_whole = tie(section_whole, hidden_one)
    weight_spatial = [section_whole[:, :, n * middle : (n + 1) * middle] for n in range(blocks)]
    weight_spatial.append(
        section_whole[:, :, ends[0] : ends[1]].reshape(dp_count * mp_count, extra, middle)
    )
    weight_spatial = jnp.concatenate(weight_spatial, axis=1).reshape(-1, middle)
    weight_expand = section_whole[:, :, ends[1] : ends[2]].reshape(middle, channels)
    weight_proj = section_whole[:, :, ends[2] : ends[3]].reshape(channels, width)
    padded = extended(beside, ((MP, 1),), 1)
    tap_stack = stacked_taps(tie(padded, weight_spatial), across, down, FORWARD_TAPS)
    convolved = jnp.einsum("pwhk,kd->pwhd", tap_stack, weight_spatial, preferred_element_type=WIDE)
    hidden_two = smooth(convolved).astype(LOW)
    expanded = jnp.einsum("pwhc,cd->pwhd", hidden_two, weight_expand, preferred_element_type=WIDE)
    summed_pre = image.astype(WIDE) + expanded
    feature_low = smooth(summed_pre).astype(LOW)
    visual_rows = jnp.einsum(
        "pwhc,cd->pwhd", feature_low, weight_proj, preferred_element_type=WIDE
    ).astype(LOW)
    attn_text = halves[0].value().reshape(pair, width, 4 * part)

    bucket_select = relative_select(NB, (tables.shape[1] - 1) // 2)
    own_tables = tables.reshape(tables.shape[:2] + (pair, 2, group))
    own_tables = lax.dynamic_index_in_dim(own_tables, core, 3, keepdims=False).reshape(
        tables.shape[:2] + (pair * group,)
    )
    span_tables = jnp.einsum("abr,trh->thab", bucket_select, own_tables, precision=PRECISE)
    head_tables = attention_tables(span_tables)
    page_segments = lax.dynamic_index_in_dim(segments, my, 0, keepdims=False)
    page_boxes = lax.dynamic_index_in_dim(boxes, my, 0, keepdims=False)
    marks = token_marks(page_boxes, page_segments, NB)
    windows = attention_windows(page_segments, CHUNK, TILE)
    segment_cols = jnp.broadcast_to(page_segments[:, None], (length, 128))
    around = (windows, marks, head_tables, segment_cols, page_segments[None])
    text_page = lax.dynamic_index_in_dim(text, my, 0, keepdims=False)
    upstream_page = lax.dynamic_index_in_dim(cotangent, my, 0, keepdims=False)

    weight_up = [ffn_whole[y, :, :units] for y in range(pair)]
    weight_down = [ffn_whole[y, :, units:] for y in range(pair)]

    visual_own = lax.all_to_all(visual_rows, CHIPS, split_axis=0, concat_axis=0, tiled=True)

    text_source = tie(text_page, visual_rows)
    weight_in = [[attn_text[y, :, : 3 * part] for y in range(pair)]]
    projected_text = [dot(text_source, weight).astype(LOW) for weight in weight_in[0]]
    attended_text, logs_text = attend_forward(projected_text, around, size)
    halves[1].step((), (attended_text,))
    attn_visual = halves[1].value().reshape(pair, width, 4 * part)
    weight_in.append([attn_visual[y, :, : 3 * part] for y in range(pair)])
    weight_out = jnp.concatenate(
        [whole[y, :, 3 * part :] for whole in (attn_text, attn_visual) for y in range(pair)], axis=1
    )
    visual_own = (
        tie(visual_own, attended_text)
        .reshape(dp_count, pair, across, down, width)
        .transpose(1, 2, 0, 3, 4)
        .reshape(pair, quarter, width)
    )
    visual_page = by_side(("core", 1), visual_own, swap(visual_own, "core", 1), 1)
    visual_page = visual_page.reshape(length, width)
    projected_visual = [dot(visual_page, weight).astype(LOW) for weight in weight_in[1]]
    attended_visual, logs_visual = attend_forward(projected_visual, around, size)
    attended = jnp.concatenate([attended_text, attended_visual], axis=1)
    attention = dot(attended, weight_out, "nt").astype(LOW)
    hat_one, scale_one, normed_low = row_kernel(
        first_norm_kernel,
        256,
        (text_page, visual_page, attention, swap(attention, "core", 1), norm_params),
        (((length, width), WIDE), ((length, 1), WIDE), ((length, width), LOW)),
    )
    own_bias = lax.dynamic_index_in_dim(up_bias.reshape(pair, 2, units), core, 1, keepdims=False)
    hidden_pre = [dot(normed_low, weight_up[y]) + own_bias[y] for y in range(pair)]
    hidden_low = [smooth(pre).astype(LOW) for pre in hidden_pre]
    down_part = sum(dot(hidden_low[y], weight_down[y], "nt") for y in range(pair)).astype(LOW)
    out_page, second_grad, down_low, second_sums = row_kernel(
        second_norm_kernel,
        256,
        (hat_one, down_part, swap(down_part, "core", 1), upstream_page, norm_params),
        (((length, width), LOW), ((length, width), WIDE), ((length, width), LOW), ((8, width), WIDE)),
    )

    out_own = own_quarters(out_page, quarter).reshape(pair, quarter, width)
    out_got = swap(out_own, "my", 1)

    hidden_grad_low = [
        smooth_back(hidden_pre[y], dot(down_low, weight_down[y])).astype(LOW) for y in range(pair)
    ]
    normed_part = sum(dot(hidden_grad_low[y], weight_up[y], "nt") for y in range(pair)).astype(LOW)
    up_part = jnp.stack([jnp.sum(part_low.astype(WIDE), axis=0) for part_low in hidden_grad_low])
    normed_other = swap(normed_part, "core", 1)
    ffn_parts = []
    for y in range(pair):
        ffn_parts.append(dot(normed_low, hidden_grad_low[y], "tn").astype(LOW))
        ffn_parts.append(dot(down_low, hidden_low[y], "tn").astype(LOW))
    normed_other = tie(normed_other, *ffn_parts)
    ffn_grad = jnp.concatenate(ffn_parts).reshape(pair, 2, dp_count, -1, units)
    ffn_grad = ffn_grad.transpose(0, 2, 1, 3, 4).reshape(-1, units)
    ffn_shard = lax.psum_scatter(ffn_grad, OWNERS, scatter_dimension=0, tiled=True).astype(WIDE)
    first_grad, attention_low, first_sums = row_kernel(
        first_back_kernel,
        256,
        (second_grad, normed_part, normed_other, hat_one, scale_one, norm_params),
        (((length, width), WIDE), ((length, width), LOW), ((8, width), WIDE)),
    )
    norm_part = jnp.concatenate([first_sums[:2], second_sums[:3]])
    norm_part = norm_part * (core == 0).astype(WIDE)
    head_grads = dot(attention_low, weight_out).astype(LOW)
    out_got = tie(out_got, head_grads)
    out_other = swap(out_got, "core", 1)
    grad_out = dot(attention_low, attended, "tn").astype(LOW)

    def attention_grads(stream, source, grads):
        found = []
        for y in range(pair):
            place = (stream * pair + y) * part
            own = [dot(source, grads[y], "tn").astype(LOW), grad_out[:, place : place + part]]
            found.append(jnp.concatenate(own, axis=1))
        return jnp.concatenate(found)

    def source_part(stream, grads):
        return sum(dot(grads[y], weight_in[stream][y], "nt") for y in range(pair))

    visual_back, span_visual = attend_backward(
        projected_visual, around, attended_visual, logs_visual, tie(head_grads, grad_out), 1, size
    )
    first_own = own_quarters(first_grad, quarter)
    visual_own_grad = add_both(source_part(1, visual_back), quarter)
    visual_low = (first_own + visual_own_grad).astype(LOW)
    out_other = by_side(("core", 1), out_got, tie(out_other, visual_low), 1)
    out_local = by_side(("my", 1), out_page.reshape(out_other.shape), out_other, 0)
    out_local = out_local.reshape(text.shape)
    visual_sent = (
        visual_low.reshape(pair, across, dp_count, down, width)
        .transpose(2, 0, 1, 3, 4)
        .reshape(pages, across, down, width)
    )
    visual_grad = lax.all_to_all(visual_sent, CHIPS, split_axis=0, concat_axis=0, tiled=True)
    grad_one = attention_grads(1, tie(visual_page, visual_sent), visual_back)
    sum_one = Scatter([grad_one], (("dx",), ("my",), ("dz",)), OWNERS).send()
    text_grads, span_text = attend_backward(
        projected_text, around, attended_text, logs_text, tie(head_grads, grad_one), 0, size
    )
    grad_text = attention_grads(0, text_page, text_grads)
    sum_two = Scatter([grad_text], (("my",), ("dx",), ("dz",)), OWNERS).send()
    visual_grad = sum_one.land(tie(visual_grad, grad_text))

    feature_grad = jnp.einsum("pwhd,cd->pwhc", visual_grad, weight_proj, preferred_element_type=WIDE)
    pre_grad = smooth_back(summed_pre, feature_grad)
    expanded_low = pre_grad.astype(LOW)
    conv_grad = smooth_back(
        convolved,
        jnp.einsum("pwhd,cd->pwhc", expanded_low, weight_expand, preferred_element_type=WIDE),
    ).astype(LOW)
    back_beside = extended(conv_grad, ((DP, 2),), 1)
    grad_proj = dot(
        feature_low.reshape(-1, channels), tie(visual_grad, conv_grad).reshape(-1, width), "tn"
    ).astype(LOW)
    grad_expand = dot(
        hidden_two.reshape(-1, middle), tie(expanded_low, grad_proj).reshape(-1, channels), "tn"
    )
    grad_expand = grad_expand.astype(LOW).reshape(-1, middle)
    back_beside = sum_two.land(tie(back_beside, grad_expand))
    back_padded = extended(back_beside, ((MP, 1),), 1)
    sum_side = Scatter(
        [grad_expand, grad_proj], (("core",), ("dx",), ("my",), ("dz",)), AXES, 1
    ).send()
    back_padded = sum_one.land(back_padded)
    back_taps = stacked_taps(back_padded, across, down, BACKWARD_TAPS).reshape(
        conv_grad.shape[:3] + (9, middle)
    )
    reduced_grad = smooth_back(
        reduced,
        jnp.einsum(
            "pwhko,kio->pwhi",
            back_taps,
            weight_spatial.reshape(9, middle, middle),
            preferred_element_type=WIDE,
        ),
    ).astype(LOW)
    grad_spatial = dot(
        tap_stack.reshape(-1, 9 * middle), sum_side.land(tie(conv_grad, reduced_grad)).reshape(-1, middle), "tn"
    ).astype(LOW)
    grad_reduce = dot(
        image.reshape(-1, channels),
        sum_two.land(tie(reduced_grad, grad_spatial)).reshape(-1, middle),
        "tn",
    ).astype(LOW)
    sum_last = Scatter(
        [grad_spatial, grad_reduce], (("core",), ("dx", "my"), ("dz",)), AXES
    ).send()
    reduced_grad = sum_one.land(tie(reduced_grad, grad_reduce))
    image_grad_local = pre_grad + jnp.einsum(
        "pwhd,cd->pwhc", reduced_grad, weight_reduce, preferred_element_type=WIDE
    )
    text_grads = [sum_last.land(tie(text_grads[0], image_grad_local))] + list(text_grads[1:])
    text_part = source_part(0, text_grads)
    text_own = first_own + add_both(sum_side.land(text_part), quarter)
    text_back = text_own.reshape(pair, quarter, width)
    text_sent = lax.dynamic_index_in_dim(text_back, 1 - my, 0, keepdims=False)
    text_kept = lax.dynamic_index_in_dim(text_back, my, 0, keepdims=False)
    text_grad_local = by_side(
        ("my", 1), text_kept, swap(text_sent.astype(LOW), "my", 1).astype(WIDE), 0
    )
    for tree in (sum_two, sum_one):
        while tree.rounds:
            tree.step(text_own)
        tree.take(text_own)

    up_shard, down_shard = jnp.split(ffn_shard, 2)
    one_shard, two_shard = sum_one.value(), sum_two.value()
    in_shard = jnp.stack([two_shard[:, : 3 * part], one_shard[:, : 3 * part]])
    in_shard = in_shard.reshape(2, -1, 3, part).transpose(0, 2, 1, 3)
    out_shard = jnp.stack([two_shard[:, 3 * part :], one_shard[:, 3 * part :]]).transpose(0, 2, 1)
    image_sets = (
        (reduce_weight, reduce_weight_rows, reduce_weight_cols),
        (spatial_weight, spatial_weight_rows, spatial_weight_cols),
        (expand_weight, expand_weight_rows, expand_weight_cols),
        (visual_proj, visual_proj_rows, visual_proj_cols),
    )
    layer_sets = (
        (attn_in, attn_in_rows, attn_in_cols, in_shard, dp_count, mp_count, True),
        (attn_out, attn_out_rows, attn_out_cols, out_shard, mp_count, dp_count, False),
        (ffn_up, ffn_up_rows, ffn_up_cols, up_shard, dp_count, mp_count, True),
        (ffn_down, ffn_down_rows, ffn_down_cols, down_shard.T, mp_count, dp_count, False),
    )
    row_parts = [jnp.sum(entry[3] * entry[3], axis=-1) for entry in layer_sets]
    col_parts = [jnp.sum(entry[3] * entry[3], axis=-2) for entry in layer_sets]
    over_dp = [(cols if entry[6] else rows) for rows, cols, entry in zip(row_parts, col_parts, layer_sets)]
    over_mp = [(rows if entry[6] else cols) for rows, cols, entry in zip(row_parts, col_parts, layer_sets)]
    span_sum = span_text + span_visual
    span_sum = jnp.stack([span_sum[:, :NB, :NB], span_sum[:, NB : 2 * NB, NB : 2 * NB]])
    table_part = jnp.einsum("abr,thba->trh", bucket_select, span_sum, precision=PRECISE)
    table_term = jnp.zeros(tables.shape[:2] + (pair, 2, group), WIDE)
    table_term = lax.dynamic_update_slice(
        table_term, table_part.reshape(tables.shape[:2] + (pair, 1, group)), (0, 0, 0, core, 0)
    ).reshape(tables.shape)
    up_term = lax.dynamic_update_slice(
        jnp.zeros((pair, 2, units), WIDE), up_part[:, None], (0, core, 0)
    ).reshape(up_bias.shape)
    while sum_side.rounds:
        sum_side.step()
    while sum_last.rounds:
        sum_last.step()
    sum_last.take(*row_parts)
    last_shard, side_shard = sum_last.value(), sum_side.take().value()
    spatial_rows = spatial_weight.shape[0]
    image_grads = (
        last_shard[spatial_rows:],
        last_shard[:spatial_rows],
        side_shard[:, :middle].reshape(expand_weight.shape),
        side_shard[:, middle:],
    )
    late = [jnp.sum(gradient * gradient, axis=-2) for gradient in image_grads]
    squares = [jnp.sum(rows, axis=-1) for rows in row_parts]
    over_all = [norm_part, up_term, table_term, old_sums, join(squares)] + late
    packed = pack(over_all)
    summed = total_over(jnp.concatenate([packed, pack(over_dp)]), DP)
    dp_sums = unpack(summed[packed.shape[0] :], over_dp)
    summed = total_over(jnp.concatenate([summed[: packed.shape[0]], pack(over_mp)]), MP)
    mp_sums = unpack(summed[packed.shape[0] :], over_mp)
    sums = unpack(summed, over_all)
    norm_gradient, up_gradient, table_gradient, old_sums, squares_total = sums[:5]
    image_cols = sums[5:]
    old_sums = split(old_sums, old_parts)
    weight_squares, rows_before = old_sums[:8], old_sums[8:]
    squares_total = split(squares_total, squares)

    decay_rate = 1.0 - STEP ** (-0.8)
    layer_results = []
    for number, (weight, rows_old, cols_old, gradient, row_split, col_split, flag) in enumerate(layer_sets):
        sizes = (weight.shape[-2] * row_split, weight.shape[-1] * col_split)
        rows_sum = mp_sums[number] if flag else dp_sums[number]
        cols_sum = dp_sums[number] if flag else mp_sums[number]
        mean = (
            decay_rate * rows_before[4 + number]
            + (1.0 - decay_rate) * squares_total[number] / sizes[1]
        ) / sizes[0]
        layer_results.append(
            factored_step(
                weight, gradient, rows_old, cols_old, rows_sum, cols_sum, mean,
                weight_squares[4 + number] / (sizes[0] * sizes[1]), sizes,
            )
        )
    norm_parts = moment_step(norm_params, norm_gradient, norm_moment, (1,))
    bias_parts = moment_step(up_bias, up_gradient, up_moment, (0,))
    table_parts = moment_step(tables, table_gradient, table_moment, (1, 2))

    image_results = []
    for number, (weight, rows_old, cols_old) in enumerate(image_sets):
        gradient = image_grads[number]
        sizes = (weight.shape[0] * dp_count * mp_count, weight.shape[1])
        rows_sum = jnp.sum(gradient * gradient, axis=-1)
        mean = (
            decay_rate * rows_before[number]
            + (1.0 - decay_rate) * jnp.sum(image_cols[number], axis=-1) / sizes[1]
        ) / sizes[0]
        image_results.append(
            factored_step(
                weight, gradient, rows_old, cols_old, rows_sum, image_cols[number], mean,
                weight_squares[number] / (sizes[0] * sizes[1]), sizes,
            )
        )
    flat = [value for result in image_results + layer_results for value in result]
    return (
        (out_local, text_grad_local, image_grad_local)
        + tuple(flat)
        + norm_parts
        + bias_parts
        + table_parts
    )


def solution(mesh):
    whole = mesh.shape["dp"], mesh.shape["mp"]
    devices = mesh.devices.reshape(whole[0] // 2, 2, whole[1] // 2, 2)
    flat, rows, none = P(AXES, None), P(AXES), P()
    image_weight_in = (flat, rows, none)
    image_weight_out = (flat, flat, rows, none, flat)
    in_spec, in_rows, in_cols = P(None, None, DP, MP), P(None, None, DP), P(None, None, MP)
    out_spec, out_rows, out_cols = P(None, MP, DP), P(None, MP), P(None, DP)
    up_spec, up_rows, up_cols = P(DP, MP), P(DP), P(MP)
    down_spec, down_rows, down_cols = P(MP, DP), P(MP), P(DP)
    placed = (
        (P(None, MP, DP, None), P(DP, None, None), P(DP, None, None), P(DP, None), P(DP, None, None))
        + image_weight_in * 4
        + (in_spec, in_rows, in_cols, out_spec, out_rows, out_cols)
        + (up_spec, up_rows, up_cols, down_spec, down_rows, down_cols)
        + (none,) * 6
    )
    given = (
        (P(DP, None, None), P(DP, MP, None), P(None, MP, DP, None))
        + image_weight_out * 4
        + (in_spec, in_spec, in_rows, in_cols, in_spec)
        + (out_spec, out_spec, out_rows, out_cols, out_spec)
        + (up_spec, up_spec, up_rows, up_cols, up_spec)
        + (down_spec, down_spec, down_rows, down_cols, down_spec)
        + (none,) * 9
    )
    return jax.shard_map(
        on_device, mesh=Mesh(devices, AXES), in_specs=placed, out_specs=given, check_vma=False
    )
```

```python
import functools

import jax
import jax.numpy as jnp
from jax import lax
from jax.experimental import pallas as pl
from jax.experimental.pallas import tpu as pltpu
from jax.sharding import Mesh
from jax.sharding import PartitionSpec as P

NB = 32
STEP = 5
NEGATIVE = -1000000000.0
SAFE = 2.0e8
NT = (((1,), (1,)), ((), ()))
NN = (((1,), (0,)), ((), ()))


def mm(a, b, dims=NN):
    return lax.dot_general(a, b, dims, preferred_element_type=jnp.float32)


def column(refs, head, kind, group, size):
    start = (kind * group + head % group) * size
    return refs[head // group].at[:, start : start + size]


def stage_heads(p_refs, kx_ref, tab_ref, q_scr, k_scr, heads, group, size):
    kx = kx_ref[...]
    for h in range(heads):
        mixed = mm(kx, tab_ref[h]).astype(jnp.bfloat16)
        q_scr[h, :, : 256 - size] = mixed[:, : 256 - size]
        q_scr[h, :, 256 - size :] = column(p_refs, h, 0, group, size)[...] * jnp.bfloat16(size**-0.5)
        k_scr[h, :, :128] = kx
        k_scr[h, :, 128 : 256 - size] = kx[:, : 128 - size]
        k_scr[h, :, 256 - size :] = column(p_refs, h, 1, group, size)[...]


def bound_ok(q_scr, k_scr, heads, size):
    big_q, big_k = 0.0, 0.0
    for h in range(heads):
        big_q = jnp.maximum(big_q, jnp.max(jnp.abs(q_scr[h, :, 256 - size :].astype(jnp.float32))))
        big_k = jnp.maximum(big_k, jnp.max(jnp.abs(k_scr[h, :, 256 - size :].astype(jnp.float32))))
    return big_q * big_k * size < SAFE


def window(win_ref, chunk, exact, length, tile):
    if exact:
        return 0, length // tile
    return pl.multiple_of(win_ref[0, chunk], 128), win_ref[1, chunk]


def sweep(count, tile, body, carry):
    carry = lax.fori_loop(0, count // 2, lambda t, c: body(t * 2 * tile, 2 * tile, c), carry)
    return lax.fori_loop(
        0, count % 2, lambda t, c: body(count // 2 * 2 * tile, tile, c), carry
    )


def forward_kernel(*refs, heads, group, size, chunk_rows, tile, beside):
    p_refs = refs[: heads // group]
    (
        win_ref, kx_ref, tab_ref, segc_ref, segr_ref, o_ref, lse_ref,
        q_scr, k_scr, vt_scr, s_scr, ot_scr,
    ) = refs[heads // group :]
    length = kx_ref.shape[0]
    chunks = length // chunk_rows
    stage_heads(p_refs, kx_ref, tab_ref, q_scr, k_scr, heads, group, size)
    for h in range(heads):
        values = column(p_refs, h, 2, group, size)[...]
        vt_scr[h] = values.astype(jnp.float32).T.astype(jnp.bfloat16)
    safe = bound_ok(q_scr, k_scr, heads, size)
    lse_ref[...] = jnp.zeros_like(lse_ref)

    def run(exact):
        def one_chunk(item, _):
            lead, c = (0, item) if beside == heads else (item // chunks * beside, item % chunks)
            start, count = window(win_ref, c, exact, length, tile)
            first = pl.multiple_of(c * chunk_rows, chunk_rows)
            queries = pl.ds(first, chunk_rows)

            def score(at, tile, tops):
                row = pl.multiple_of(at, 128)
                src = pl.multiple_of(start + at, 128)
                found = []
                for u in range(beside):
                    s = mm(k_scr[lead + u, pl.ds(src, tile), :], q_scr[lead + u, queries, :], NT)
                    if exact:
                        s = jnp.where(segc_ref[pl.ds(src, tile), :1] == segr_ref[:, queries], s, NEGATIVE)
                    s_scr[u, pl.ds(row, tile), :] = s
                    found.append(
                        jnp.maximum(tops[u], jnp.max(s.reshape(tile // 8, 8, chunk_rows), axis=0))
                    )
                return tuple(found)

            tops = sweep(
                count, tile, score, (jnp.full((8, chunk_rows), -3.0e38, jnp.float32),) * beside
            )
            tops = [jnp.max(top, axis=0, keepdims=True) for top in tops]
            ot_scr[pl.ds(lead, beside), :, queries] = jnp.zeros((beside, size, chunk_rows), jnp.float32)

            def mix(at, tile, totals):
                row = pl.multiple_of(at, 128)
                src = pl.multiple_of(start + at, 128)
                found = []
                for u in range(beside):
                    p = jnp.exp(s_scr[u, pl.ds(row, tile), :] - tops[u])
                    found.append(totals[u] + jnp.sum(p.reshape(tile // 8, 8, chunk_rows), axis=0))
                    ot_scr[lead + u, :, queries] += mm(
                        vt_scr[lead + u, :, pl.ds(src, tile)], p.astype(jnp.bfloat16)
                    )
                return tuple(found)

            totals = sweep(
                count, tile, mix, (jnp.zeros((8, chunk_rows), jnp.float32),) * beside
            )
            for u in range(beside):
                total = jnp.sum(totals[u], axis=0, keepdims=True)
                lse_ref[pl.ds(lead + u, 1), queries] = tops[u] + jnp.log(total)
                ot_scr[lead + u, :, queries] = ot_scr[lead + u, :, queries] / total
            return 0

        lax.fori_loop(0, heads // beside * chunks, one_chunk, 0)

    pl.when(safe)(functools.partial(run, False))
    pl.when(jnp.logical_not(safe))(functools.partial(run, True))
    for h in range(heads):
        o_ref[:, h * size : (h + 1) * size] = ot_scr[h].T.astype(jnp.bfloat16)


def backward_kernel(*refs, heads, group, size, chunk_rows, tile, offset, beside):
    groups = heads // group
    p_refs, refs = refs[:groups], refs[groups:]
    win_ref, kx_ref, tab_ref, segc_ref, segr_ref, o_ref, lse_ref, g_ref = refs[:8]
    d_refs, span_ref = refs[8 : 8 + groups], refs[8 + groups]
    q_scr, k_scr, kt_scr, v_scr, g_scr, dk_scr, dv_scr, dq_scr, dl_scr = refs[9 + groups :]
    length = kx_ref.shape[0]
    chunks = length // chunk_rows
    stage_heads(p_refs, kx_ref, tab_ref, q_scr, k_scr, heads, group, size)
    safe = bound_ok(q_scr, k_scr, heads, size)
    for h in range(heads):
        kt_scr[h] = k_scr[h, :, 128:].astype(jnp.float32).T.astype(jnp.bfloat16)
        v_scr[h] = column(p_refs, h, 2, group, size)[...]
        g = g_ref[:, offset + h * size : offset + (h + 1) * size]
        g_scr[h] = g
        o = o_ref[:, h * size : (h + 1) * size]
        mixed = g.astype(jnp.float32) * o.astype(jnp.float32)
        dl_scr[pl.ds(h, 1), :] = jnp.sum(mixed.T, axis=0, keepdims=True)
    dk_scr[...] = jnp.zeros_like(dk_scr)
    dv_scr[...] = jnp.zeros_like(dv_scr)
    dq_scr[...] = jnp.zeros_like(dq_scr)

    def run(exact):
        def one_chunk(item, _):
            lead, c = (0, item) if beside == heads else (item // chunks * beside, item % chunks)
            start, count = window(win_ref, c, exact, length, tile)
            first = pl.multiple_of(c * chunk_rows, chunk_rows)
            queries = pl.ds(first, chunk_rows)

            def step(at, tile, _):
                keys = pl.ds(pl.multiple_of(start + at, 128), tile)
                for u in range(beside):
                    h = lead + u
                    g = g_scr[h, queries, :]
                    s = mm(k_scr[h, keys, :], q_scr[h, queries, :], NT)
                    if exact:
                        s = jnp.where(segc_ref[keys, :1] == segr_ref[:, queries], s, NEGATIVE)
                    p = jnp.exp(s - lse_ref[pl.ds(h, 1), queries])
                    dp = mm(v_scr[h, keys, :], g, NT)
                    ds = (p * (dp - dl_scr[pl.ds(h, 1), queries])).astype(jnp.bfloat16)
                    dv_scr[h, keys, :] += mm(p.astype(jnp.bfloat16), g)
                    dk_scr[h, keys, :] += mm(ds, q_scr[h, queries, 256 - size :])
                    dq_scr[h, :, queries] += mm(kt_scr[h, :, keys], ds)
                return 0

            return sweep(count, tile, step, 0)

        lax.fori_loop(0, heads // beside * chunks, one_chunk, 0)

    pl.when(safe)(functools.partial(run, False))
    pl.when(jnp.logical_not(safe))(functools.partial(run, True))
    for h in range(heads):
        own, keys, values = (column(d_refs, h, kind, group, size) for kind in range(3))
        own[...] = (dq_scr[h, 128 - size :, :] * size**-0.5).T.astype(jnp.bfloat16)
        keys[...] = dk_scr[h].astype(jnp.bfloat16)
        values[...] = dv_scr[h].astype(jnp.bfloat16)
        thr = dq_scr[h, : 128 - size, :]
        upper = thr.astype(jnp.bfloat16)
        lower = (thr - upper.astype(jnp.float32)).astype(jnp.bfloat16)
        span_ref[h] = mm(upper, kx_ref[...]) + mm(lower, kx_ref[...])


CHUNK = 256
TILE = 256
VMEM = pltpu.VMEM


def attend_forward(proj, around, size):
    length, total = proj[0].shape
    group = total // (3 * size)
    heads = len(proj) * group
    full = pl.BlockSpec(memory_space=pltpu.VMEM)
    return pl.pallas_call(
        functools.partial(
            forward_kernel, heads=heads, group=group, size=size, chunk_rows=CHUNK, tile=TILE,
            beside=heads,
        ),
        in_specs=[full] * len(proj) + [pl.BlockSpec(memory_space=pltpu.SMEM)] + [full] * 4,
        out_specs=[full, full],
        out_shape=[
            jax.ShapeDtypeStruct((length, heads * size), jnp.bfloat16),
            jax.ShapeDtypeStruct((8, length), jnp.float32),
        ],
        scratch_shapes=[
            VMEM((heads, length, 256), jnp.bfloat16),
            VMEM((heads, length, 256), jnp.bfloat16),
            VMEM((heads, size, length), jnp.bfloat16),
            VMEM((heads, length, CHUNK), jnp.float32),
            VMEM((heads, size, length), jnp.float32),
        ],
        compiler_params=pltpu.CompilerParams(vmem_limit_bytes=48 * 1024 * 1024),
        cost_estimate=pl.CostEstimate(flops=0, bytes_accessed=0, transcendentals=0),
    )(*proj, *around)


def attend_backward(proj, around, out, lse, grads, stream, size):
    length, total = proj[0].shape
    group = total // (3 * size)
    heads = len(proj) * group
    full = pl.BlockSpec(memory_space=pltpu.VMEM)
    found = pl.pallas_call(
        functools.partial(
            backward_kernel, heads=heads, group=group, size=size, chunk_rows=CHUNK, tile=TILE,
            offset=stream * heads * size, beside=heads,
        ),
        in_specs=[full] * len(proj) + [pl.BlockSpec(memory_space=pltpu.SMEM)] + [full] * 7,
        out_specs=[full] * (len(proj) + 1),
        out_shape=[jax.ShapeDtypeStruct((length, total), jnp.bfloat16)] * len(proj)
        + [jax.ShapeDtypeStruct((heads, 128 - size, 128), jnp.float32)],
        scratch_shapes=[
            VMEM((heads, length, 256), jnp.bfloat16),
            VMEM((heads, length, 256), jnp.bfloat16),
            VMEM((heads, 128, length), jnp.bfloat16),
            VMEM((heads, length, size), jnp.bfloat16),
            VMEM((heads, length, size), jnp.bfloat16),
            VMEM((heads, length, size), jnp.float32),
            VMEM((heads, length, size), jnp.float32),
            VMEM((heads, 128, length), jnp.float32),
            VMEM((8, length), jnp.float32),
        ],
        compiler_params=pltpu.CompilerParams(vmem_limit_bytes=56 * 1024 * 1024),
        cost_estimate=pl.CostEstimate(flops=0, bytes_accessed=0, transcendentals=0),
    )(*proj, *around, out, lse, grads)
    return found[:-1], found[-1]


def attention_windows(segment_row, chunk_rows, tile):
    length = segment_row.shape[0]
    heads_of = segment_row[::chunk_rows]
    tails_of = segment_row[chunk_rows - 1 :: chunk_rows]
    low = jnp.sum((segment_row[None, :] < heads_of[:, None]).astype(jnp.int32), axis=1)
    high = jnp.sum((segment_row[None, :] <= tails_of[:, None]).astype(jnp.int32), axis=1)
    start = low // 128 * 128
    count = (high - start + tile - 1) // tile
    start = jnp.minimum(start, length - count * tile)
    return jnp.stack([start, count]).astype(jnp.int32)


def attention_tables(span_tables):
    _, heads, buckets, _ = span_tables.shape
    upper = lax.reduce_precision(span_tables, 8, 7)
    lower = (span_tables - upper).astype(jnp.bfloat16)
    def diag(t):
        z = jnp.zeros_like(t[0])
        return jnp.concatenate([jnp.concatenate([t[0], z], 2), jnp.concatenate([z, t[1]], 2)], 1)
    hi, lo = diag(upper.astype(jnp.bfloat16)), diag(lower)
    level = jnp.arange(64)
    away = jnp.where((level[:, None] != level[None, :]), NEGATIVE, 0.0)
    segs = jnp.where((level[:, None] < 4) & (level[None, :] < 4), away, 0.0).astype(jnp.bfloat16)
    segs = jnp.broadcast_to(segs[None], (heads, 64, 64))
    zero = jnp.zeros((heads, 64, 64), jnp.bfloat16)
    top = jnp.concatenate([hi, zero, lo, zero], 2)
    bottom = jnp.concatenate([zero, segs, zero, zero], 2)
    return jnp.concatenate([top, bottom], 1)


def token_marks(boxes_page, segment_row, buckets):
    levels = jnp.arange(buckets, dtype=jnp.int32)[None, :]
    kinds = jnp.arange(64, dtype=jnp.int32)[None, :]
    return jnp.concatenate(
        [boxes_page[0][:, None] == levels, boxes_page[1][:, None] == levels, segment_row[:, None] == kinds],
        axis=1,
    ).astype(jnp.bfloat16)


NORM_EPS = 1e-05
RELATIVE = 0.5
RATE_FLOOR = 0.001
PRECISE = lax.Precision.HIGHEST
LOW = jnp.bfloat16
WIDE = jnp.float32
AXES = ("dz", "dx", "my", "core")
DP = ("dz", "dx")
MP = ("my", "core")
CHIPS = ("dz", "dx", "my")
OWNERS = ("my", "dz", "dx")
FORWARD_TAPS = tuple((col, row) for col in range(3) for row in range(3))
BACKWARD_TAPS = tuple((2 - col, 2 - row) for col in range(3) for row in range(3))


def swap(values, axis, reach):
    count = lax.axis_size(axis)
    return lax.ppermute(values, axis, [(i, i ^ reach) for i in range(count)])


def exchange(values, flips):
    if len({axis for axis, _ in flips}) == 1:
        return swap(values, flips[0][0], sum(reach for _, reach in flips))
    (one, far), (two, near) = flips
    count = lax.axis_size(two)
    pairs = [
        (i * count + k, (i ^ far) * count + (k ^ near))
        for i in range(lax.axis_size(one))
        for k in range(count)
    ]
    return lax.ppermute(values, (one, two), pairs)


def bits_of(axis):
    reach, found = lax.axis_size(axis) // 2, []
    while reach:
        found.append((axis, reach))
        reach //= 2
    return found


def bits(axes):
    return [bit for axis in axes for bit in bits_of(axis)]


def rounds_of(order):
    found = []
    for axes in order:
        places = bits(axes)
        found += [tuple(places[n : n + 2]) for n in range(0, len(places), 2)]
    return found


def flips_of(group):
    return [(bit,) for bit in group] + ([group] if len(group) == 2 else [])


def side(bit):
    return lax.axis_index(bit[0]) // bit[1] % 2


def tie(values, *after):
    if not after:
        return values
    return lax.optimization_barrier((values,) + after)[0]


class Gather:
    def __init__(self, shard, order, owners):
        self.places = bits(owners)
        self.rounds = rounds_of(order)[::-1]
        self.sides = [side(place) for place in self.places]
        self.shape = shard.shape
        self.done = []
        self.held = shard.reshape((1,) * len(self.places) + shard.shape)
        whole = jnp.zeros((2,) * len(self.places) + shard.shape, shard.dtype)
        self.whole = lax.dynamic_update_slice(whole, self.held, self.corner())

    def corner(self, flips=()):
        return [
            0 if place in self.done else (1 - mine if place in flips else mine)
            for place, mine in zip(self.places, self.sides)
        ] + [0] * len(self.shape)

    def step(self, before=(), fill=()):
        group = self.rounds.pop()
        sent = lax.optimization_barrier((self.held,) + tuple(before))[0]
        arrived = []
        for flips in flips_of(group):
            got = tie(exchange(sent, flips), *fill)
            self.whole = lax.dynamic_update_slice(self.whole, got, self.corner(flips))
            arrived.append(got)
        self.done += group
        if self.rounds:
            sizes = [2 if place in self.done else 1 for place in self.places] + list(self.shape)
            self.held = lax.dynamic_slice(self.whole, self.corner(), sizes)
        return tuple(arrived)

    def value(self):
        return self.whole.reshape((-1,) + self.shape[1:])


class Scatter:
    def __init__(self, blocks, order, owners, axis=0):
        self.live = bits(owners)
        self.count = len(self.live)
        self.rounds = rounds_of(order)[::-1]
        self.parts = [[value.reshape((2,) * self.count + (-1,) + value.shape[1:])] for value in blocks]
        self.axis = self.count + axis
        self.busy = False

    def merged(self, other):
        self.parts = self.parts + other.parts
        self.axis = self.count
        return self

    def pick(self, group, flips):
        def cut(value):
            for bit in group:
                mine = side(bit)
                place = 1 - mine if bit in flips else mine
                value = lax.dynamic_slice_in_dim(value, place, 1, self.live.index(bit))
            return value

        found = []
        for addends in self.parts:
            if len(addends) == 1:
                found.append(cut(addends[0]))
            else:
                found.append(sum(cut(value).astype(WIDE) for value in addends).astype(LOW))
        return jnp.concatenate(found, axis=self.axis)

    def send(self, *after):
        group = self.rounds.pop()
        self.flying = tuple(
            exchange(tie(self.pick(group, flips), *after), flips) for flips in flips_of(group)
        )
        self.kept = self.pick(group, ())
        for bit in group:
            self.live[self.live.index(bit)] = None
        self.busy = True
        return self

    def take(self, *after):
        if self.busy:
            flying = lax.optimization_barrier(self.flying + after)[: len(self.flying)]
            self.parts = [[self.kept] + list(flying)]
            self.busy = False
        return self

    def step(self, *after):
        self.take(*after)
        return self.send() if self.rounds else self

    def land(self, values, go_on=True):
        found = lax.optimization_barrier((values,) + self.flying)
        self.parts = [[self.kept] + list(found[1:])]
        self.busy = False
        if self.rounds and go_on:
            self.send()
        return found[0]

    def value(self):
        total = sum(value.astype(WIDE) for value in self.parts[0])
        return total.reshape(total.shape[self.count :])


def total_over(values, axes):
    for bit in bits(axes):
        values = values + swap(values, *bit)
    return values


def by_side(bit, own, other, axis):
    return jnp.where(
        side(bit) == 0, jnp.stack([own, other], axis), jnp.stack([other, own], axis)
    )


def own_quarters(page, quarter):
    parts = page.reshape((-1, 2, quarter) + page.shape[1:])
    own = lax.dynamic_index_in_dim(parts, lax.axis_index("core"), 1, keepdims=False)
    return own.reshape((-1,) + page.shape[1:])


def add_both(partial, quarter, *after):
    parts = partial.reshape((-1, 2, quarter) + partial.shape[1:])
    core = lax.axis_index("core")
    sent = lax.dynamic_index_in_dim(parts, 1 - core, 1, keepdims=False)
    kept = lax.dynamic_index_in_dim(parts, core, 1, keepdims=False)
    got = tie(swap(sent.astype(LOW), "core", 1), *after)
    return (kept + got.astype(WIDE)).reshape((-1,) + partial.shape[1:])


def extended(cells, sides, width):
    for axis, dim in sides:
        count = lax.axis_size(axis)
        ends = count - 1
        head = lax.slice_in_dim(cells, 0, width, axis=dim)
        tail = lax.slice_in_dim(cells, cells.shape[dim] - width, cells.shape[dim], axis=dim)
        cells = jnp.concatenate(
            [
                lax.ppermute(tail, axis, [(i, i + 1) for i in range(ends)]),
                cells,
                lax.ppermute(head, axis, [(i + 1, i) for i in range(ends)]),
            ],
            axis=dim,
        )
    return cells


def smooth(values):
    return jax.nn.gelu(values, approximate=True)


def smooth_back(values, upstream):
    return jax.vjp(smooth, values)[1](upstream)[0]


def row_mean(values):
    return jnp.mean(values, axis=-1, keepdims=True)


def first_norm_kernel(text_ref, visual_ref, mine_ref, other_ref, params_ref, hat_ref, scale_ref, low_ref):
    first = text_ref[...].astype(WIDE) + visual_ref[...].astype(WIDE)
    first = first + (mine_ref[...].astype(WIDE) + other_ref[...].astype(WIDE))
    centre = first - row_mean(first)
    scale = lax.rsqrt(row_mean(centre * centre) + NORM_EPS)
    hat = centre * scale
    hat_ref[...] = hat
    scale_ref[...] = scale
    low_ref[...] = (hat * params_ref[0:1, :] + params_ref[1:2, :]).astype(LOW)


def second_norm_kernel(hat_ref, mine_ref, other_ref, upstream_ref, params_ref, out_ref, grad_ref, low_ref, sums_ref):
    normed = hat_ref[...] * params_ref[0:1, :] + params_ref[1:2, :]
    down = mine_ref[...].astype(WIDE) + other_ref[...].astype(WIDE)
    second = normed + (down + params_ref[4:5, :])
    centre = second - row_mean(second)
    scale = lax.rsqrt(row_mean(centre * centre) + NORM_EPS)
    hat = centre * scale
    out_ref[...] = (hat * params_ref[2:3, :] + params_ref[3:4, :]).astype(LOW)
    upstream = upstream_ref[...].astype(WIDE)
    inner = upstream * params_ref[2:3, :]
    grad = scale * (inner - row_mean(inner) - hat * row_mean(inner * hat))
    grad_ref[...] = grad
    low = grad.astype(LOW)
    low_ref[...] = low
    sums_ref[0:1, :] += jnp.sum(upstream * hat, axis=0, keepdims=True)
    sums_ref[1:2, :] += jnp.sum(upstream, axis=0, keepdims=True)
    sums_ref[2:3, :] += jnp.sum(low.astype(WIDE), axis=0, keepdims=True)


def first_back_kernel(grad_ref, mine_ref, other_ref, hat_ref, scale_ref, params_ref, first_ref, low_ref, sums_ref):
    upstream = grad_ref[...] + (mine_ref[...].astype(WIDE) + other_ref[...].astype(WIDE))
    hat = hat_ref[...]
    inner = upstream * params_ref[0:1, :]
    grad = scale_ref[...] * (inner - row_mean(inner) - hat * row_mean(inner * hat))
    first_ref[...] = grad
    low_ref[...] = grad.astype(LOW)
    sums_ref[0:1, :] += jnp.sum(upstream * hat, axis=0, keepdims=True)
    sums_ref[1:2, :] += jnp.sum(upstream, axis=0, keepdims=True)


def row_kernel(kernel, rows, given, made):
    length = given[0].shape[0]
    shapes = [value.shape for value in given] + [shape for shape, _ in made]

    def body(*refs):
        def block(number, _):
            here = pl.ds(pl.multiple_of(number * rows, rows), rows)
            kernel(*(ref.at[here] if shape[0] == length else ref for ref, shape in zip(refs, shapes)))
            return 0

        for ref, shape in zip(refs[len(given) :], shapes[len(given) :]):
            if shape[0] != length:
                ref[...] = jnp.zeros_like(ref)
        lax.fori_loop(0, length // rows, block, 0)

    whole = pl.BlockSpec(memory_space=pltpu.VMEM)
    return pl.pallas_call(
        body,
        in_specs=[whole] * len(given),
        out_specs=[whole] * len(made),
        out_shape=[jax.ShapeDtypeStruct(shape, kind) for shape, kind in made],
        compiler_params=pltpu.CompilerParams(vmem_limit_bytes=32 * 1024 * 1024),
        cost_estimate=pl.CostEstimate(flops=0, bytes_accessed=0, transcendentals=0),
    )(*given)


def relative_select(buckets, reach_max):
    offsets = (
        jnp.arange(buckets, dtype=jnp.int32)[None, :]
        - jnp.arange(buckets, dtype=jnp.int32)[:, None]
    )
    clipped = jnp.clip(offsets, -reach_max, reach_max) + reach_max
    return (
        clipped[:, :, None] == jnp.arange(2 * reach_max + 1, dtype=jnp.int32)[None, None, :]
    ).astype(WIDE)


def stacked_taps(padded, across, downward, anchors):
    return jnp.concatenate(
        [
            padded[:, from_col : from_col + across, from_row : from_row + downward, :]
            for from_col, from_row in anchors
        ],
        axis=-1,
    )


def dot(left, right, dims="nn"):
    first = 0 if dims[0] == "t" else 1
    second = 1 if dims[1] == "t" else 0
    return lax.dot_general(
        left, right, (((first,), (second,)), ((), ())), preferred_element_type=WIDE
    )


def factored_step(weight, gradient, rows_old, cols_old, row_piece, col_piece, row_mean, weight_mean, sizes):
    decay_rate = 1.0 - STEP ** (-0.8)
    rows_next = decay_rate * rows_old + (1.0 - decay_rate) * row_piece / sizes[1]
    cols_next = decay_rate * cols_old + (1.0 - decay_rate) * col_piece / sizes[0]
    second = rows_next[..., :, None] * cols_next[..., None, :] / row_mean[..., None, None]
    step_rate = RELATIVE * jnp.maximum(RATE_FLOOR, jnp.sqrt(weight_mean))
    weight_next = weight - step_rate[..., None, None] * (gradient * lax.rsqrt(second))
    return (gradient, weight_next, rows_next, cols_next, weight_next.astype(LOW))


def moment_step(parameter, gradient, moment, reduce_axes):
    decay_rate = 1.0 - STEP ** (-0.8)
    moment_next = decay_rate * moment + (1.0 - decay_rate) * gradient * gradient
    rms_value = jnp.sqrt(jnp.mean(parameter * parameter, axis=reduce_axes, keepdims=True))
    return (
        gradient,
        moment_next,
        parameter
        - RELATIVE * jnp.maximum(RATE_FLOOR, rms_value) * gradient * lax.rsqrt(moment_next),
    )


def pack(parts):
    flat = [part.reshape(-1) for part in parts]
    return jnp.concatenate(
        [jnp.pad(part, (0, -part.size % 1024)).reshape(-1, 8, 128) for part in flat]
    )


def unpack(packed, like):
    found, cursor = [], 0
    for part in like:
        tiles = -(-part.size // 1024)
        flat = packed[cursor : cursor + tiles].reshape(-1)
        found.append(flat[: part.size].reshape(part.shape))
        cursor += tiles
    return found


def join(parts):
    return jnp.concatenate([part.reshape(-1) for part in parts])


def split(flat, like):
    found, cursor = [], 0
    for part in like:
        found.append(flat[cursor : cursor + part.size].reshape(part.shape))
        cursor += part.size
    return found


def on_device(
    image, text, cotangent, segments, boxes,
    reduce_weight, reduce_weight_rows, reduce_weight_cols,
    spatial_weight, spatial_weight_rows, spatial_weight_cols,
    expand_weight, expand_weight_rows, expand_weight_cols,
    visual_proj, visual_proj_rows, visual_proj_cols,
    attn_in, attn_in_rows, attn_in_cols,
    attn_out, attn_out_rows, attn_out_cols,
    ffn_up, ffn_up_rows, ffn_up_cols,
    ffn_down, ffn_down_rows, ffn_down_cols,
    norm_params, norm_moment, up_bias, up_moment, tables, table_moment,
):
    dp_count = lax.axis_size(DP)
    pair = lax.axis_size("my")
    mp_count = 2 * pair
    my, core = lax.axis_index("my"), lax.axis_index("core")
    mp_index = lax.axis_index(MP)
    length, width = text.shape[1:]
    quarter = length // mp_count
    heads = tables.shape[2]
    size = width // heads
    group = heads // mp_count
    part = group * size
    units = ffn_up.shape[1]
    pages, across, down, channels = image.shape
    middle = spatial_weight.shape[1]

    flat_in = attn_in.astype(LOW).transpose(2, 0, 1, 3).reshape(attn_in.shape[2], 2, 3 * part)
    flat_out = attn_out.astype(LOW).transpose(2, 0, 1)
    layer_in = [
        jnp.concatenate([flat_in[:, stream], flat_out[:, stream]], axis=1) for stream in range(2)
    ]
    layer_ffn = jnp.concatenate([ffn_up.astype(LOW), ffn_down.astype(LOW).T], axis=1)
    base = visual_proj.shape[0]
    spatial_low = spatial_weight.astype(LOW)
    blocks, extra = divmod(spatial_low.shape[0], base)
    section_low = [spatial_low[n * base : (n + 1) * base] for n in range(blocks)]
    section_low.append(spatial_low[blocks * base :].reshape(base, -1))
    section_low.append(expand_weight.astype(LOW).reshape(base, middle))
    section_low.append(visual_proj.astype(LOW))
    section_low.append(reduce_weight.astype(LOW))
    section_low = jnp.concatenate(section_low, axis=1)
    section_whole = lax.all_gather(section_low, AXES, axis=0, tiled=True)
    ffn_whole = lax.all_gather(layer_ffn, OWNERS, axis=0, tiled=True).reshape(pair, width, -1)
    old_weights = (reduce_weight, spatial_weight, expand_weight, visual_proj, attn_in, attn_out, ffn_up, ffn_down)
    old_rows = (
        reduce_weight_rows, spatial_weight_rows, expand_weight_rows, visual_proj_rows,
        attn_in_rows, attn_out_rows, ffn_up_rows, ffn_down_rows,
    )
    copies = (1, 1, 1, 1, mp_count, dp_count, mp_count, dp_count)
    halves = [Gather(half, (("dz",), ("dx", "my")), OWNERS) for half in layer_in]
    while halves[0].rounds:
        halves[0].step()
    while len(halves[1].rounds) > 1:
        halves[1].step((halves[0].whole,))
    old_parts = [jnp.sum(weight * weight, axis=(-2, -1)) for weight in old_weights]
    old_parts += [jnp.sum(rows, axis=-1) / times for rows, times in zip(old_rows, copies)]
    old_sums = join(old_parts)

    section_whole = section_whole.reshape(dp_count * mp_count, base, -1)
    ends = [blocks * middle, extra * middle // base, middle, width, middle]
    ends = [sum(ends[: n + 1]) for n in range(len(ends))]
    weight_reduce = section_whole[:, :, ends[3] :].reshape(channels, middle)
    first_wait = (halves[0].whole, old_sums)
    reduced = jnp.einsum(
        "pwhc,cd->pwhd",
        tie(image, *first_wait),
        weight_reduce,
        preferred_element_type=WIDE,
    )
    hidden_one = smooth(reduced).astype(LOW)
    beside = extended(tie(hidden_one, halves[1].held), ((DP, 2),), 1)
    halves[1].step((beside,))
    section_whole = tie(section_whole, hidden_one)
    weight_spatial = [section_whole[:, :, n * middle : (n + 1) * middle] for n in range(blocks)]
    weight_spatial.append(
        section_whole[:, :, ends[0] : ends[1]].reshape(dp_count * mp_count, extra, middle)
    )
    weight_spatial = jnp.concatenate(weight_spatial, axis=1).reshape(-1, middle)
    weight_expand = section_whole[:, :, ends[1] : ends[2]].reshape(middle, channels)
    weight_proj = section_whole[:, :, ends[2] : ends[3]].reshape(channels, width)
    padded = extended(beside, ((MP, 1),), 1)
    tap_stack = stacked_taps(tie(padded, weight_spatial), across, down, FORWARD_TAPS)
    convolved = jnp.einsum("pwhk,kd->pwhd", tap_stack, weight_spatial, preferred_element_type=WIDE)
    hidden_two = smooth(convolved).astype(LOW)
    expanded = jnp.einsum("pwhc,cd->pwhd", hidden_two, weight_expand, preferred_element_type=WIDE)
    summed_pre = image.astype(WIDE) + expanded
    feature_low = smooth(summed_pre).astype(LOW)
    visual_rows = jnp.einsum(
        "pwhc,cd->pwhd", feature_low, weight_proj, preferred_element_type=WIDE
    ).astype(LOW)
    attn_text = halves[0].value().reshape(pair, width, 4 * part)

    bucket_select = relative_select(NB, (tables.shape[1] - 1) // 2)
    own_tables = tables.reshape(tables.shape[:2] + (pair, 2, group))
    own_tables = lax.dynamic_index_in_dim(own_tables, core, 3, keepdims=False).reshape(
        tables.shape[:2] + (pair * group,)
    )
    span_tables = jnp.einsum("abr,trh->thab", bucket_select, own_tables, precision=PRECISE)
    head_tables = attention_tables(span_tables)
    page_segments = lax.dynamic_index_in_dim(segments, my, 0, keepdims=False)
    page_boxes = lax.dynamic_index_in_dim(boxes, my, 0, keepdims=False)
    marks = token_marks(page_boxes, page_segments, NB)
    windows = attention_windows(page_segments, CHUNK, TILE)
    segment_cols = jnp.broadcast_to(page_segments[:, None], (length, 128))
    around = (windows, marks, head_tables, segment_cols, page_segments[None])
    text_page = lax.dynamic_index_in_dim(text, my, 0, keepdims=False)
    upstream_page = lax.dynamic_index_in_dim(cotangent, my, 0, keepdims=False)

    weight_up = [ffn_whole[y, :, :units] for y in range(pair)]
    weight_down = [ffn_whole[y, :, units:] for y in range(pair)]

    visual_own = lax.all_to_all(visual_rows, CHIPS, split_axis=0, concat_axis=0, tiled=True)

    text_source = tie(text_page, visual_rows, halves[1].whole)
    weight_in = [[attn_text[y, :, : 3 * part] for y in range(pair)]]
    projected_text = [dot(text_source, weight).astype(LOW) for weight in weight_in[0]]
    attended_text, logs_text = attend_forward(projected_text, around, size)
    attn_visual = halves[1].value().reshape(pair, width, 4 * part)
    weight_in.append([attn_visual[y, :, : 3 * part] for y in range(pair)])
    weight_out = jnp.concatenate(
        [whole[y, :, 3 * part :] for whole in (attn_text, attn_visual) for y in range(pair)], axis=1
    )
    visual_own = (
        tie(visual_own, attended_text)
        .reshape(dp_count, pair, across, down, width)
        .transpose(1, 2, 0, 3, 4)
        .reshape(pair, quarter, width)
    )
    visual_page = by_side(("core", 1), visual_own, swap(visual_own, "core", 1), 1)
    visual_page = visual_page.reshape(length, width)
    projected_visual = [dot(visual_page, weight).astype(LOW) for weight in weight_in[1]]
    attended_visual, logs_visual = attend_forward(projected_visual, around, size)
    attended = jnp.concatenate([attended_text, attended_visual], axis=1)
    attention = dot(attended, weight_out, "nt").astype(LOW)
    hat_one, scale_one, normed_low = row_kernel(
        first_norm_kernel,
        256,
        (text_page, visual_page, attention, swap(attention, "core", 1), norm_params),
        (((length, width), WIDE), ((length, 1), WIDE), ((length, width), LOW)),
    )
    own_bias = lax.dynamic_index_in_dim(up_bias.reshape(pair, 2, units), core, 1, keepdims=False)
    hidden_pre = [dot(normed_low, weight_up[y]) + own_bias[y] for y in range(pair)]
    hidden_low = [smooth(pre).astype(LOW) for pre in hidden_pre]
    down_part = sum(dot(hidden_low[y], weight_down[y], "nt") for y in range(pair)).astype(LOW)
    out_page, second_grad, down_low, second_sums = row_kernel(
        second_norm_kernel,
        256,
        (hat_one, down_part, swap(down_part, "core", 1), upstream_page, norm_params),
        (((length, width), LOW), ((length, width), WIDE), ((length, width), LOW), ((8, width), WIDE)),
    )

    out_own = own_quarters(out_page, quarter).reshape(pair, quarter, width)
    out_got = swap(out_own, "my", 1)

    hidden_grad_low = [
        smooth_back(hidden_pre[y], dot(down_low, weight_down[y])).astype(LOW) for y in range(pair)
    ]
    normed_part = sum(dot(hidden_grad_low[y], weight_up[y], "nt") for y in range(pair)).astype(LOW)
    up_part = jnp.stack([jnp.sum(part_low.astype(WIDE), axis=0) for part_low in hidden_grad_low])
    normed_other = swap(normed_part, "core", 1)
    ffn_parts = []
    for y in range(pair):
        ffn_parts.append(dot(normed_low, hidden_grad_low[y], "tn").astype(LOW))
        ffn_parts.append(dot(down_low, hidden_low[y], "tn").astype(LOW))
    normed_other = tie(normed_other, *ffn_parts)
    ffn_grad = jnp.concatenate(ffn_parts).reshape(pair, 2, dp_count, -1, units)
    ffn_grad = ffn_grad.transpose(0, 2, 1, 3, 4).reshape(-1, units)
    ffn_shard = lax.psum_scatter(ffn_grad, OWNERS, scatter_dimension=0, tiled=True).astype(WIDE)
    first_grad, attention_low, first_sums = row_kernel(
        first_back_kernel,
        256,
        (second_grad, normed_part, normed_other, hat_one, scale_one, norm_params),
        (((length, width), WIDE), ((length, width), LOW), ((8, width), WIDE)),
    )
    norm_part = jnp.concatenate([first_sums[:2], second_sums[:3]])
    norm_part = norm_part * (core == 0).astype(WIDE)
    head_grads = dot(attention_low, weight_out).astype(LOW)
    out_got = tie(out_got, head_grads)
    out_other = swap(out_got, "core", 1)
    grad_out = dot(attention_low, attended, "tn").astype(LOW)

    def attention_grads(stream, source, grads):
        found = []
        for y in range(pair):
            place = (stream * pair + y) * part
            own = [dot(source, grads[y], "tn").astype(LOW), grad_out[:, place : place + part]]
            found.append(jnp.concatenate(own, axis=1))
        return jnp.concatenate(found)

    def source_part(stream, grads):
        return sum(dot(grads[y], weight_in[stream][y], "nt") for y in range(pair))

    visual_back, span_visual = attend_backward(
        projected_visual, around, attended_visual, logs_visual, tie(head_grads, grad_out), 1, size
    )
    first_own = own_quarters(first_grad, quarter)
    visual_own_grad = add_both(source_part(1, visual_back), quarter)
    visual_low = (first_own + visual_own_grad).astype(LOW)
    out_other = by_side(("core", 1), out_got, tie(out_other, visual_low), 1)
    out_local = by_side(("my", 1), out_page.reshape(out_other.shape), out_other, 0)
    out_local = out_local.reshape(text.shape)
    visual_sent = (
        visual_low.reshape(pair, across, dp_count, down, width)
        .transpose(2, 0, 1, 3, 4)
        .reshape(pages, across, down, width)
    )
    visual_grad = lax.all_to_all(visual_sent, CHIPS, split_axis=0, concat_axis=0, tiled=True)
    grad_one = attention_grads(1, tie(visual_page, visual_sent), visual_back)
    sum_one = Scatter([grad_one], (("dx",), ("my",), ("dz",)), OWNERS).send()
    text_grads, span_text = attend_backward(
        projected_text, around, attended_text, logs_text, tie(head_grads, grad_one), 0, size
    )
    grad_text = attention_grads(0, text_page, text_grads)
    sum_two = Scatter([grad_text], (("my",), ("dx",), ("dz",)), OWNERS).send()
    visual_grad = sum_one.land(tie(visual_grad, grad_text))

    feature_grad = jnp.einsum("pwhd,cd->pwhc", visual_grad, weight_proj, preferred_element_type=WIDE)
    pre_grad = smooth_back(summed_pre, feature_grad)
    expanded_low = pre_grad.astype(LOW)
    conv_grad = smooth_back(
        convolved,
        jnp.einsum("pwhd,cd->pwhc", expanded_low, weight_expand, preferred_element_type=WIDE),
    ).astype(LOW)
    back_beside = extended(conv_grad, ((DP, 2),), 1)
    grad_proj = dot(
        feature_low.reshape(-1, channels), tie(visual_grad, conv_grad).reshape(-1, width), "tn"
    ).astype(LOW)
    grad_expand = dot(
        hidden_two.reshape(-1, middle), tie(expanded_low, grad_proj).reshape(-1, channels), "tn"
    )
    grad_expand = grad_expand.astype(LOW).reshape(-1, middle)
    back_beside = sum_two.land(tie(back_beside, grad_expand))
    back_padded = extended(back_beside, ((MP, 1),), 1)
    sum_side = Scatter(
        [grad_expand, grad_proj], (("core",), ("dx",), ("my",), ("dz",)), AXES, 1
    ).send()
    back_padded = sum_one.land(back_padded, False)
    back_taps = stacked_taps(back_padded, across, down, BACKWARD_TAPS).reshape(
        conv_grad.shape[:3] + (9, middle)
    )
    reduced_grad = smooth_back(
        reduced,
        jnp.einsum(
            "pwhko,kio->pwhi",
            back_taps,
            weight_spatial.reshape(9, middle, middle),
            preferred_element_type=WIDE,
        ),
    ).astype(LOW)
    grad_spatial = dot(
        tap_stack.reshape(-1, 9 * middle), sum_side.land(tie(conv_grad, reduced_grad)).reshape(-1, middle), "tn"
    ).astype(LOW)
    grad_reduce = dot(
        image.reshape(-1, channels),
        sum_two.land(tie(reduced_grad, grad_spatial), False).reshape(-1, middle),
        "tn",
    ).astype(LOW)
    sum_last = Scatter(
        [grad_spatial, grad_reduce], (("core",), ("dx", "my"), ("dz",)), AXES
    ).send()
    sum_both = sum_one.merged(sum_two).send()
    reduced_grad = tie(reduced_grad, grad_reduce)
    image_grad_local = pre_grad + jnp.einsum(
        "pwhd,cd->pwhc", reduced_grad, weight_reduce, preferred_element_type=WIDE
    )
    text_grads = [sum_last.land(tie(text_grads[0], image_grad_local))] + list(text_grads[1:])
    text_part = source_part(0, text_grads)
    text_own = first_own + add_both(sum_side.land(text_part), quarter)
    text_back = text_own.reshape(pair, quarter, width)
    text_sent = lax.dynamic_index_in_dim(text_back, 1 - my, 0, keepdims=False)
    text_kept = lax.dynamic_index_in_dim(text_back, my, 0, keepdims=False)
    text_grad_local = by_side(
        ("my", 1), text_kept, swap(text_sent.astype(LOW), "my", 1).astype(WIDE), 0
    )
    while sum_both.rounds:
        sum_both.step(text_own)
    both_shard = sum_both.take(text_own).value()

    (
        reduce_weight, spatial_weight, expand_weight, visual_proj, attn_in, attn_out, ffn_up, ffn_down,
        norm_params, norm_moment, up_bias, up_moment, tables, table_moment,
    ) = lax.optimization_barrier(
        (
            reduce_weight, spatial_weight, expand_weight, visual_proj, attn_in, attn_out, ffn_up, ffn_down,
            norm_params, norm_moment, up_bias, up_moment, tables, table_moment, grad_reduce,
        )
    )[:14]
    up_shard, down_shard = jnp.split(ffn_shard, 2)
    one_shard, two_shard = jnp.split(both_shard, 2)
    in_shard = jnp.stack([two_shard[:, : 3 * part], one_shard[:, : 3 * part]])
    in_shard = in_shard.reshape(2, -1, 3, part).transpose(0, 2, 1, 3)
    out_shard = jnp.stack([two_shard[:, 3 * part :], one_shard[:, 3 * part :]]).transpose(0, 2, 1)
    image_sets = (
        (reduce_weight, reduce_weight_rows, reduce_weight_cols),
        (spatial_weight, spatial_weight_rows, spatial_weight_cols),
        (expand_weight, expand_weight_rows, expand_weight_cols),
        (visual_proj, visual_proj_rows, visual_proj_cols),
    )
    layer_sets = (
        (attn_in, attn_in_rows, attn_in_cols, in_shard, dp_count, mp_count, True),
        (attn_out, attn_out_rows, attn_out_cols, out_shard, mp_count, dp_count, False),
        (ffn_up, ffn_up_rows, ffn_up_cols, up_shard, dp_count, mp_count, True),
        (ffn_down, ffn_down_rows, ffn_down_cols, down_shard.T, mp_count, dp_count, False),
    )
    row_parts = [jnp.sum(entry[3] * entry[3], axis=-1) for entry in layer_sets]
    col_parts = [jnp.sum(entry[3] * entry[3], axis=-2) for entry in layer_sets]
    over_dp = [(cols if entry[6] else rows) for rows, cols, entry in zip(row_parts, col_parts, layer_sets)]
    over_mp = [(rows if entry[6] else cols) for rows, cols, entry in zip(row_parts, col_parts, layer_sets)]
    span_sum = span_text + span_visual
    span_sum = jnp.stack([span_sum[:, :NB, :NB], span_sum[:, NB : 2 * NB, NB : 2 * NB]])
    table_part = jnp.einsum("abr,thba->trh", bucket_select, span_sum, precision=PRECISE)
    table_term = jnp.zeros(tables.shape[:2] + (pair, 2, group), WIDE)
    table_term = lax.dynamic_update_slice(
        table_term, table_part.reshape(tables.shape[:2] + (pair, 1, group)), (0, 0, 0, core, 0)
    ).reshape(tables.shape)
    up_term = lax.dynamic_update_slice(
        jnp.zeros((pair, 2, units), WIDE), up_part[:, None], (0, core, 0)
    ).reshape(up_bias.shape)
    while sum_side.rounds:
        sum_side.step()
    while sum_last.rounds:
        sum_last.step()
    sum_last.take(*row_parts)
    last_shard, side_shard = sum_last.value(), sum_side.take().value()
    spatial_rows = spatial_weight.shape[0]
    image_grads = (
        last_shard[spatial_rows:],
        last_shard[:spatial_rows],
        side_shard[:, :middle].reshape(expand_weight.shape),
        side_shard[:, middle:],
    )
    late = [jnp.sum(gradient * gradient, axis=-2) for gradient in image_grads]
    squares = [jnp.sum(rows, axis=-1) for rows in row_parts]
    over_all = [norm_part, up_term, table_term, old_sums, join(squares)] + late
    packed = pack(over_all)
    summed = total_over(jnp.concatenate([packed, pack(over_dp)]), DP)
    dp_sums = unpack(summed[packed.shape[0] :], over_dp)
    summed = total_over(jnp.concatenate([summed[: packed.shape[0]], pack(over_mp)]), MP)
    mp_sums = unpack(summed[packed.shape[0] :], over_mp)
    sums = unpack(summed, over_all)
    norm_gradient, up_gradient, table_gradient, old_sums, squares_total = sums[:5]
    image_cols = sums[5:]
    old_sums = split(old_sums, old_parts)
    weight_squares, rows_before = old_sums[:8], old_sums[8:]
    squares_total = split(squares_total, squares)

    decay_rate = 1.0 - STEP ** (-0.8)
    layer_results = []
    for number, (weight, rows_old, cols_old, gradient, row_split, col_split, flag) in enumerate(layer_sets):
        sizes = (weight.shape[-2] * row_split, weight.shape[-1] * col_split)
        rows_sum = mp_sums[number] if flag else dp_sums[number]
        cols_sum = dp_sums[number] if flag else mp_sums[number]
        mean = (
            decay_rate * rows_before[4 + number]
            + (1.0 - decay_rate) * squares_total[number] / sizes[1]
        ) / sizes[0]
        layer_results.append(
            factored_step(
                weight, gradient, rows_old, cols_old, rows_sum, cols_sum, mean,
                weight_squares[4 + number] / (sizes[0] * sizes[1]), sizes,
            )
        )
    norm_parts = moment_step(norm_params, norm_gradient, norm_moment, (1,))
    bias_parts = moment_step(up_bias, up_gradient, up_moment, (0,))
    table_parts = moment_step(tables, table_gradient, table_moment, (1, 2))

    image_results = []
    for number, (weight, rows_old, cols_old) in enumerate(image_sets):
        gradient = image_grads[number]
        sizes = (weight.shape[0] * dp_count * mp_count, weight.shape[1])
        rows_sum = jnp.sum(gradient * gradient, axis=-1)
        mean = (
            decay_rate * rows_before[number]
            + (1.0 - decay_rate) * jnp.sum(image_cols[number], axis=-1) / sizes[1]
        ) / sizes[0]
        image_results.append(
            factored_step(
                weight, gradient, rows_old, cols_old, rows_sum, image_cols[number], mean,
                weight_squares[number] / (sizes[0] * sizes[1]), sizes,
            )
        )
    flat = [value for result in image_results + layer_results for value in result]
    return (
        (out_local, text_grad_local, image_grad_local)
        + tuple(flat)
        + norm_parts
        + bias_parts
        + table_parts
    )


def solution(mesh):
    whole = mesh.shape["dp"], mesh.shape["mp"]
    devices = mesh.devices.reshape(whole[0] // 2, 2, whole[1] // 2, 2)
    flat, rows, none = P(AXES, None), P(AXES), P()
    image_weight_in = (flat, rows, none)
    image_weight_out = (flat, flat, rows, none, flat)
    in_spec, in_rows, in_cols = P(None, None, DP, MP), P(None, None, DP), P(None, None, MP)
    out_spec, out_rows, out_cols = P(None, MP, DP), P(None, MP), P(None, DP)
    up_spec, up_rows, up_cols = P(DP, MP), P(DP), P(MP)
    down_spec, down_rows, down_cols = P(MP, DP), P(MP), P(DP)
    placed = (
        (P(None, MP, DP, None), P(DP, None, None), P(DP, None, None), P(DP, None), P(DP, None, None))
        + image_weight_in * 4
        + (in_spec, in_rows, in_cols, out_spec, out_rows, out_cols)
        + (up_spec, up_rows, up_cols, down_spec, down_rows, down_cols)
        + (none,) * 6
    )
    given = (
        (P(DP, None, None), P(DP, MP, None), P(None, MP, DP, None))
        + image_weight_out * 4
        + (in_spec, in_spec, in_rows, in_cols, in_spec)
        + (out_spec, out_spec, out_rows, out_cols, out_spec)
        + (up_spec, up_spec, up_rows, up_cols, up_spec)
        + (down_spec, down_spec, down_rows, down_cols, down_spec)
        + (none,) * 9
    )
    return jax.shard_map(
        on_device, mesh=Mesh(devices, AXES), in_specs=placed, out_specs=given, check_vma=False
    )
```

```python
import functools

import jax
import jax.numpy as jnp
from jax import lax
from jax.experimental import pallas as pl
from jax.experimental.pallas import tpu as pltpu
from jax.sharding import Mesh
from jax.sharding import PartitionSpec as P

NB = 32
STEP = 5
NEGATIVE = -1000000000.0
SAFE = 2.0e8
NT = (((1,), (1,)), ((), ()))
NN = (((1,), (0,)), ((), ()))


def mm(a, b, dims=NN):
    return lax.dot_general(a, b, dims, preferred_element_type=jnp.float32)


def column(refs, head, kind, group, size):
    start = (kind * group + head % group) * size
    return refs[head // group].at[:, start : start + size]


def stage_heads(p_refs, kx_ref, tab_ref, q_scr, k_scr, heads, group, size):
    kx = kx_ref[...]
    for h in range(heads):
        mixed = mm(kx, tab_ref[h]).astype(jnp.bfloat16)
        q_scr[h, :, : 256 - size] = mixed[:, : 256 - size]
        q_scr[h, :, 256 - size :] = column(p_refs, h, 0, group, size)[...] * jnp.bfloat16(size**-0.5)
        k_scr[h, :, :128] = kx
        k_scr[h, :, 128 : 256 - size] = kx[:, : 128 - size]
        k_scr[h, :, 256 - size :] = column(p_refs, h, 1, group, size)[...]


def bound_ok(q_scr, k_scr, heads, size):
    big_q, big_k = 0.0, 0.0
    for h in range(heads):
        big_q = jnp.maximum(big_q, jnp.max(jnp.abs(q_scr[h, :, 256 - size :].astype(jnp.float32))))
        big_k = jnp.maximum(big_k, jnp.max(jnp.abs(k_scr[h, :, 256 - size :].astype(jnp.float32))))
    return big_q * big_k * size < SAFE


def window(win_ref, chunk, exact, length, tile):
    if exact:
        return 0, length // tile
    return pl.multiple_of(win_ref[0, chunk], 128), win_ref[1, chunk]


def sweep(count, tile, body, carry):
    carry = lax.fori_loop(0, count // 2, lambda t, c: body(t * 2 * tile, 2 * tile, c), carry)
    return lax.fori_loop(
        0, count % 2, lambda t, c: body(count // 2 * 2 * tile, tile, c), carry
    )


def forward_kernel(*refs, heads, group, size, chunk_rows, tile, beside):
    p_refs = refs[: heads // group]
    (
        win_ref, kx_ref, tab_ref, segc_ref, segr_ref, o_ref, lse_ref,
        q_scr, k_scr, vt_scr, s_scr, ot_scr,
    ) = refs[heads // group :]
    length = kx_ref.shape[0]
    chunks = length // chunk_rows
    stage_heads(p_refs, kx_ref, tab_ref, q_scr, k_scr, heads, group, size)
    for h in range(heads):
        values = column(p_refs, h, 2, group, size)[...]
        vt_scr[h] = values.astype(jnp.float32).T.astype(jnp.bfloat16)
    safe = bound_ok(q_scr, k_scr, heads, size)
    lse_ref[...] = jnp.zeros_like(lse_ref)

    def run(exact):
        def one_chunk(item, _):
            lead, c = (0, item) if beside == heads else (item // chunks * beside, item % chunks)
            start, count = window(win_ref, c, exact, length, tile)
            first = pl.multiple_of(c * chunk_rows, chunk_rows)
            queries = pl.ds(first, chunk_rows)

            def score(at, tile, tops):
                row = pl.multiple_of(at, 128)
                src = pl.multiple_of(start + at, 128)
                found = []
                for u in range(beside):
                    s = mm(k_scr[lead + u, pl.ds(src, tile), :], q_scr[lead + u, queries, :], NT)
                    if exact:
                        s = jnp.where(segc_ref[pl.ds(src, tile), :1] == segr_ref[:, queries], s, NEGATIVE)
                    s_scr[u, pl.ds(row, tile), :] = s
                    found.append(
                        jnp.maximum(tops[u], jnp.max(s.reshape(tile // 8, 8, chunk_rows), axis=0))
                    )
                return tuple(found)

            tops = sweep(
                count, tile, score, (jnp.full((8, chunk_rows), -3.0e38, jnp.float32),) * beside
            )
            tops = [jnp.max(top, axis=0, keepdims=True) for top in tops]
            ot_scr[pl.ds(lead, beside), :, queries] = jnp.zeros((beside, size, chunk_rows), jnp.float32)

            def mix(at, tile, totals):
                row = pl.multiple_of(at, 128)
                src = pl.multiple_of(start + at, 128)
                found = []
                for u in range(beside):
                    p = jnp.exp(s_scr[u, pl.ds(row, tile), :] - tops[u])
                    found.append(totals[u] + jnp.sum(p.reshape(tile // 8, 8, chunk_rows), axis=0))
                    ot_scr[lead + u, :, queries] += mm(
                        vt_scr[lead + u, :, pl.ds(src, tile)], p.astype(jnp.bfloat16)
                    )
                return tuple(found)

            totals = sweep(
                count, tile, mix, (jnp.zeros((8, chunk_rows), jnp.float32),) * beside
            )
            for u in range(beside):
                total = jnp.sum(totals[u], axis=0, keepdims=True)
                lse_ref[pl.ds(lead + u, 1), queries] = tops[u] + jnp.log(total)
                ot_scr[lead + u, :, queries] = ot_scr[lead + u, :, queries] / total
            return 0

        lax.fori_loop(0, heads // beside * chunks, one_chunk, 0)

    pl.when(safe)(functools.partial(run, False))
    pl.when(jnp.logical_not(safe))(functools.partial(run, True))
    for h in range(heads):
        o_ref[:, h * size : (h + 1) * size] = ot_scr[h].T.astype(jnp.bfloat16)


def backward_kernel(*refs, heads, group, size, chunk_rows, tile, offset, beside):
    groups = heads // group
    p_refs, refs = refs[:groups], refs[groups:]
    win_ref, kx_ref, tab_ref, segc_ref, segr_ref, o_ref, lse_ref, g_ref = refs[:8]
    d_refs, span_ref = refs[8 : 8 + groups], refs[8 + groups]
    q_scr, k_scr, kt_scr, v_scr, g_scr, dk_scr, dv_scr, dq_scr, dl_scr = refs[9 + groups :]
    length = kx_ref.shape[0]
    chunks = length // chunk_rows
    stage_heads(p_refs, kx_ref, tab_ref, q_scr, k_scr, heads, group, size)
    safe = bound_ok(q_scr, k_scr, heads, size)
    for h in range(heads):
        kt_scr[h] = k_scr[h, :, 128:].astype(jnp.float32).T.astype(jnp.bfloat16)
        v_scr[h] = column(p_refs, h, 2, group, size)[...]
        g = g_ref[:, offset + h * size : offset + (h + 1) * size]
        g_scr[h] = g
        o = o_ref[:, h * size : (h + 1) * size]
        mixed = g.astype(jnp.float32) * o.astype(jnp.float32)
        dl_scr[pl.ds(h, 1), :] = jnp.sum(mixed.T, axis=0, keepdims=True)
    dk_scr[...] = jnp.zeros_like(dk_scr)
    dv_scr[...] = jnp.zeros_like(dv_scr)
    dq_scr[...] = jnp.zeros_like(dq_scr)

    def run(exact):
        def one_chunk(item, _):
            lead, c = (0, item) if beside == heads else (item // chunks * beside, item % chunks)
            start, count = window(win_ref, c, exact, length, tile)
            first = pl.multiple_of(c * chunk_rows, chunk_rows)
            queries = pl.ds(first, chunk_rows)

            def step(at, tile, _):
                keys = pl.ds(pl.multiple_of(start + at, 128), tile)
                for u in range(beside):
                    h = lead + u
                    g = g_scr[h, queries, :]
                    s = mm(k_scr[h, keys, :], q_scr[h, queries, :], NT)
                    if exact:
                        s = jnp.where(segc_ref[keys, :1] == segr_ref[:, queries], s, NEGATIVE)
                    p = jnp.exp(s - lse_ref[pl.ds(h, 1), queries])
                    dp = mm(v_scr[h, keys, :], g, NT)
                    ds = (p * (dp - dl_scr[pl.ds(h, 1), queries])).astype(jnp.bfloat16)
                    dv_scr[h, keys, :] += mm(p.astype(jnp.bfloat16), g)
                    dk_scr[h, keys, :] += mm(ds, q_scr[h, queries, 256 - size :])
                    dq_scr[h, :, queries] += mm(kt_scr[h, :, keys], ds)
                return 0

            return sweep(count, tile, step, 0)

        lax.fori_loop(0, heads // beside * chunks, one_chunk, 0)

    pl.when(safe)(functools.partial(run, False))
    pl.when(jnp.logical_not(safe))(functools.partial(run, True))
    for h in range(heads):
        own, keys, values = (column(d_refs, h, kind, group, size) for kind in range(3))
        own[...] = (dq_scr[h, 128 - size :, :] * size**-0.5).T.astype(jnp.bfloat16)
        keys[...] = dk_scr[h].astype(jnp.bfloat16)
        values[...] = dv_scr[h].astype(jnp.bfloat16)
        thr = dq_scr[h, : 128 - size, :]
        upper = thr.astype(jnp.bfloat16)
        lower = (thr - upper.astype(jnp.float32)).astype(jnp.bfloat16)
        span_ref[h] = mm(upper, kx_ref[...]) + mm(lower, kx_ref[...])


CHUNK = 256
TILE = 256
VMEM = pltpu.VMEM


def attend_forward(proj, around, size):
    length, total = proj[0].shape
    group = total // (3 * size)
    heads = len(proj) * group
    full = pl.BlockSpec(memory_space=pltpu.VMEM)
    return pl.pallas_call(
        functools.partial(
            forward_kernel, heads=heads, group=group, size=size, chunk_rows=CHUNK, tile=TILE,
            beside=heads,
        ),
        in_specs=[full] * len(proj) + [pl.BlockSpec(memory_space=pltpu.SMEM)] + [full] * 4,
        out_specs=[full, full],
        out_shape=[
            jax.ShapeDtypeStruct((length, heads * size), jnp.bfloat16),
            jax.ShapeDtypeStruct((8, length), jnp.float32),
        ],
        scratch_shapes=[
            VMEM((heads, length, 256), jnp.bfloat16),
            VMEM((heads, length, 256), jnp.bfloat16),
            VMEM((heads, size, length), jnp.bfloat16),
            VMEM((heads, length, CHUNK), jnp.float32),
            VMEM((heads, size, length), jnp.float32),
        ],
        compiler_params=pltpu.CompilerParams(vmem_limit_bytes=48 * 1024 * 1024),
        cost_estimate=pl.CostEstimate(flops=0, bytes_accessed=0, transcendentals=0),
    )(*proj, *around)


def attend_backward(proj, around, out, lse, grads, stream, size):
    length, total = proj[0].shape
    group = total // (3 * size)
    heads = len(proj) * group
    full = pl.BlockSpec(memory_space=pltpu.VMEM)
    found = pl.pallas_call(
        functools.partial(
            backward_kernel, heads=heads, group=group, size=size, chunk_rows=CHUNK, tile=TILE,
            offset=stream * heads * size, beside=heads,
        ),
        in_specs=[full] * len(proj) + [pl.BlockSpec(memory_space=pltpu.SMEM)] + [full] * 7,
        out_specs=[full] * (len(proj) + 1),
        out_shape=[jax.ShapeDtypeStruct((length, total), jnp.bfloat16)] * len(proj)
        + [jax.ShapeDtypeStruct((heads, 128 - size, 128), jnp.float32)],
        scratch_shapes=[
            VMEM((heads, length, 256), jnp.bfloat16),
            VMEM((heads, length, 256), jnp.bfloat16),
            VMEM((heads, 128, length), jnp.bfloat16),
            VMEM((heads, length, size), jnp.bfloat16),
            VMEM((heads, length, size), jnp.bfloat16),
            VMEM((heads, length, size), jnp.float32),
            VMEM((heads, length, size), jnp.float32),
            VMEM((heads, 128, length), jnp.float32),
            VMEM((8, length), jnp.float32),
        ],
        compiler_params=pltpu.CompilerParams(vmem_limit_bytes=56 * 1024 * 1024),
        cost_estimate=pl.CostEstimate(flops=0, bytes_accessed=0, transcendentals=0),
    )(*proj, *around, out, lse, grads)
    return found[:-1], found[-1]


def attention_windows(segment_row, chunk_rows, tile):
    length = segment_row.shape[0]
    heads_of = segment_row[::chunk_rows]
    tails_of = segment_row[chunk_rows - 1 :: chunk_rows]
    low = jnp.sum((segment_row[None, :] < heads_of[:, None]).astype(jnp.int32), axis=1)
    high = jnp.sum((segment_row[None, :] <= tails_of[:, None]).astype(jnp.int32), axis=1)
    start = low // 128 * 128
    count = (high - start + tile - 1) // tile
    start = jnp.minimum(start, length - count * tile)
    return jnp.stack([start, count]).astype(jnp.int32)


def attention_tables(span_tables):
    _, heads, buckets, _ = span_tables.shape
    upper = lax.reduce_precision(span_tables, 8, 7)
    lower = (span_tables - upper).astype(jnp.bfloat16)
    def diag(t):
        z = jnp.zeros_like(t[0])
        return jnp.concatenate([jnp.concatenate([t[0], z], 2), jnp.concatenate([z, t[1]], 2)], 1)
    hi, lo = diag(upper.astype(jnp.bfloat16)), diag(lower)
    level = jnp.arange(64)
    away = jnp.where((level[:, None] != level[None, :]), NEGATIVE, 0.0)
    segs = jnp.where((level[:, None] < 4) & (level[None, :] < 4), away, 0.0).astype(jnp.bfloat16)
    segs = jnp.broadcast_to(segs[None], (heads, 64, 64))
    zero = jnp.zeros((heads, 64, 64), jnp.bfloat16)
    top = jnp.concatenate([hi, zero, lo, zero], 2)
    bottom = jnp.concatenate([zero, segs, zero, zero], 2)
    return jnp.concatenate([top, bottom], 1)


def token_marks(boxes_page, segment_row, buckets):
    levels = jnp.arange(buckets, dtype=jnp.int32)[None, :]
    kinds = jnp.arange(64, dtype=jnp.int32)[None, :]
    return jnp.concatenate(
        [boxes_page[0][:, None] == levels, boxes_page[1][:, None] == levels, segment_row[:, None] == kinds],
        axis=1,
    ).astype(jnp.bfloat16)


NORM_EPS = 1e-05
RELATIVE = 0.5
RATE_FLOOR = 0.001
PRECISE = lax.Precision.HIGHEST
LOW = jnp.bfloat16
WIDE = jnp.float32
AXES = ("dz", "dx", "my", "core")
DP = ("dz", "dx")
MP = ("my", "core")
CHIPS = ("dz", "dx", "my")
OWNERS = ("my", "dz", "dx")
FORWARD_TAPS = tuple((col, row) for col in range(3) for row in range(3))
BACKWARD_TAPS = tuple((2 - col, 2 - row) for col in range(3) for row in range(3))


def swap(values, axis, reach):
    count = lax.axis_size(axis)
    return lax.ppermute(values, axis, [(i, i ^ reach) for i in range(count)])


def exchange(values, flips):
    if len({axis for axis, _ in flips}) == 1:
        return swap(values, flips[0][0], sum(reach for _, reach in flips))
    (one, far), (two, near) = flips
    count = lax.axis_size(two)
    pairs = [
        (i * count + k, (i ^ far) * count + (k ^ near))
        for i in range(lax.axis_size(one))
        for k in range(count)
    ]
    return lax.ppermute(values, (one, two), pairs)


def bits_of(axis):
    reach, found = lax.axis_size(axis) // 2, []
    while reach:
        found.append((axis, reach))
        reach //= 2
    return found


def bits(axes):
    return [bit for axis in axes for bit in bits_of(axis)]


def rounds_of(order):
    found = []
    for axes in order:
        places = bits(axes)
        found += [tuple(places[n : n + 2]) for n in range(0, len(places), 2)]
    return found


def flips_of(group):
    return [(bit,) for bit in group] + ([group] if len(group) == 2 else [])


def side(bit):
    return lax.axis_index(bit[0]) // bit[1] % 2


def tie(values, *after):
    if not after:
        return values
    return lax.optimization_barrier((values,) + after)[0]


class Gather:
    def __init__(self, shard, order, owners):
        self.places = bits(owners)
        self.rounds = rounds_of(order)[::-1]
        self.sides = [side(place) for place in self.places]
        self.shape = shard.shape
        self.done = []
        self.held = shard.reshape((1,) * len(self.places) + shard.shape)
        whole = jnp.zeros((2,) * len(self.places) + shard.shape, shard.dtype)
        self.whole = lax.dynamic_update_slice(whole, self.held, self.corner())

    def corner(self, flips=()):
        return [
            0 if place in self.done else (1 - mine if place in flips else mine)
            for place, mine in zip(self.places, self.sides)
        ] + [0] * len(self.shape)

    def step(self, before=(), fill=()):
        group = self.rounds.pop()
        sent = lax.optimization_barrier((self.held,) + tuple(before))[0]
        arrived = []
        for flips in flips_of(group):
            got = tie(exchange(sent, flips), *fill)
            self.whole = lax.dynamic_update_slice(self.whole, got, self.corner(flips))
            arrived.append(got)
        self.done += group
        if self.rounds:
            sizes = [2 if place in self.done else 1 for place in self.places] + list(self.shape)
            self.held = lax.dynamic_slice(self.whole, self.corner(), sizes)
        return tuple(arrived)

    def value(self):
        return self.whole.reshape((-1,) + self.shape[1:])


class Scatter:
    def __init__(self, blocks, order, owners, axis=0):
        self.live = bits(owners)
        self.count = len(self.live)
        self.rounds = rounds_of(order)[::-1]
        self.parts = [[value.reshape((2,) * self.count + (-1,) + value.shape[1:])] for value in blocks]
        self.axis = self.count + axis
        self.busy = False

    def merged(self, other):
        self.parts = self.parts + other.parts
        self.axis = self.count
        return self

    def pick(self, group, flips):
        def cut(value):
            for bit in group:
                mine = side(bit)
                place = 1 - mine if bit in flips else mine
                value = lax.dynamic_slice_in_dim(value, place, 1, self.live.index(bit))
            return value

        found = []
        for addends in self.parts:
            if len(addends) == 1:
                found.append(cut(addends[0]))
            else:
                found.append(sum(cut(value).astype(WIDE) for value in addends).astype(LOW))
        return jnp.concatenate(found, axis=self.axis)

    def send(self, *after):
        group = self.rounds.pop()
        self.flying = tuple(
            exchange(tie(self.pick(group, flips), *after), flips) for flips in flips_of(group)
        )
        self.kept = self.pick(group, ())
        for bit in group:
            self.live[self.live.index(bit)] = None
        self.busy = True
        return self

    def take(self, *after):
        if self.busy:
            flying = lax.optimization_barrier(self.flying + after)[: len(self.flying)]
            self.parts = [[self.kept] + list(flying)]
            self.busy = False
        return self

    def step(self, *after):
        self.take(*after)
        return self.send() if self.rounds else self

    def land(self, values, go_on=True):
        found = lax.optimization_barrier((values,) + self.flying)
        self.parts = [[self.kept] + list(found[1:])]
        self.busy = False
        if self.rounds and go_on:
            self.send()
        return found[0]

    def value(self):
        total = sum(value.astype(WIDE) for value in self.parts[0])
        return total.reshape(total.shape[self.count :])


def total_over(values, axes):
    for bit in bits(axes):
        values = values + swap(values, *bit)
    return values


def by_side(bit, own, other, axis):
    return jnp.where(
        side(bit) == 0, jnp.stack([own, other], axis), jnp.stack([other, own], axis)
    )


def own_quarters(page, quarter):
    parts = page.reshape((-1, 2, quarter) + page.shape[1:])
    own = lax.dynamic_index_in_dim(parts, lax.axis_index("core"), 1, keepdims=False)
    return own.reshape((-1,) + page.shape[1:])


def add_both(partial, quarter, *after):
    parts = partial.reshape((-1, 2, quarter) + partial.shape[1:])
    core = lax.axis_index("core")
    sent = lax.dynamic_index_in_dim(parts, 1 - core, 1, keepdims=False)
    kept = lax.dynamic_index_in_dim(parts, core, 1, keepdims=False)
    got = tie(swap(sent.astype(LOW), "core", 1), *after)
    return (kept + got.astype(WIDE)).reshape((-1,) + partial.shape[1:])


def extended(cells, sides, width):
    for axis, dim in sides:
        count = lax.axis_size(axis)
        ends = count - 1
        head = lax.slice_in_dim(cells, 0, width, axis=dim)
        tail = lax.slice_in_dim(cells, cells.shape[dim] - width, cells.shape[dim], axis=dim)
        cells = jnp.concatenate(
            [
                lax.ppermute(tail, axis, [(i, i + 1) for i in range(ends)]),
                cells,
                lax.ppermute(head, axis, [(i + 1, i) for i in range(ends)]),
            ],
            axis=dim,
        )
    return cells


def smooth(values):
    return jax.nn.gelu(values, approximate=True)


def smooth_back(values, upstream):
    return jax.vjp(smooth, values)[1](upstream)[0]


def row_mean(values):
    return jnp.mean(values, axis=-1, keepdims=True)


def first_norm_kernel(text_ref, visual_ref, mine_ref, other_ref, params_ref, hat_ref, scale_ref, low_ref):
    first = text_ref[...].astype(WIDE) + visual_ref[...].astype(WIDE)
    first = first + (mine_ref[...].astype(WIDE) + other_ref[...].astype(WIDE))
    centre = first - row_mean(first)
    scale = lax.rsqrt(row_mean(centre * centre) + NORM_EPS)
    hat = centre * scale
    hat_ref[...] = hat
    scale_ref[...] = scale
    low_ref[...] = (hat * params_ref[0:1, :] + params_ref[1:2, :]).astype(LOW)


def second_norm_kernel(hat_ref, mine_ref, other_ref, upstream_ref, params_ref, out_ref, grad_ref, low_ref, sums_ref):
    normed = hat_ref[...] * params_ref[0:1, :] + params_ref[1:2, :]
    down = mine_ref[...].astype(WIDE) + other_ref[...].astype(WIDE)
    second = normed + (down + params_ref[4:5, :])
    centre = second - row_mean(second)
    scale = lax.rsqrt(row_mean(centre * centre) + NORM_EPS)
    hat = centre * scale
    out_ref[...] = (hat * params_ref[2:3, :] + params_ref[3:4, :]).astype(LOW)
    upstream = upstream_ref[...].astype(WIDE)
    inner = upstream * params_ref[2:3, :]
    grad = scale * (inner - row_mean(inner) - hat * row_mean(inner * hat))
    grad_ref[...] = grad
    low = grad.astype(LOW)
    low_ref[...] = low
    sums_ref[0:1, :] += jnp.sum(upstream * hat, axis=0, keepdims=True)
    sums_ref[1:2, :] += jnp.sum(upstream, axis=0, keepdims=True)
    sums_ref[2:3, :] += jnp.sum(low.astype(WIDE), axis=0, keepdims=True)


def first_back_kernel(grad_ref, mine_ref, other_ref, hat_ref, scale_ref, params_ref, first_ref, low_ref, sums_ref):
    upstream = grad_ref[...] + (mine_ref[...].astype(WIDE) + other_ref[...].astype(WIDE))
    hat = hat_ref[...]
    inner = upstream * params_ref[0:1, :]
    grad = scale_ref[...] * (inner - row_mean(inner) - hat * row_mean(inner * hat))
    first_ref[...] = grad
    low_ref[...] = grad.astype(LOW)
    sums_ref[0:1, :] += jnp.sum(upstream * hat, axis=0, keepdims=True)
    sums_ref[1:2, :] += jnp.sum(upstream, axis=0, keepdims=True)


def row_kernel(kernel, rows, given, made):
    length = given[0].shape[0]
    shapes = [value.shape for value in given] + [shape for shape, _ in made]

    def body(*refs):
        def block(number, _):
            here = pl.ds(pl.multiple_of(number * rows, rows), rows)
            kernel(*(ref.at[here] if shape[0] == length else ref for ref, shape in zip(refs, shapes)))
            return 0

        for ref, shape in zip(refs[len(given) :], shapes[len(given) :]):
            if shape[0] != length:
                ref[...] = jnp.zeros_like(ref)
        lax.fori_loop(0, length // rows, block, 0)

    whole = pl.BlockSpec(memory_space=pltpu.VMEM)
    return pl.pallas_call(
        body,
        in_specs=[whole] * len(given),
        out_specs=[whole] * len(made),
        out_shape=[jax.ShapeDtypeStruct(shape, kind) for shape, kind in made],
        compiler_params=pltpu.CompilerParams(vmem_limit_bytes=32 * 1024 * 1024),
        cost_estimate=pl.CostEstimate(flops=0, bytes_accessed=0, transcendentals=0),
    )(*given)


def relative_select(buckets, reach_max):
    offsets = (
        jnp.arange(buckets, dtype=jnp.int32)[None, :]
        - jnp.arange(buckets, dtype=jnp.int32)[:, None]
    )
    clipped = jnp.clip(offsets, -reach_max, reach_max) + reach_max
    return (
        clipped[:, :, None] == jnp.arange(2 * reach_max + 1, dtype=jnp.int32)[None, None, :]
    ).astype(WIDE)


def stacked_taps(padded, across, downward, anchors):
    return jnp.concatenate(
        [
            padded[:, from_col : from_col + across, from_row : from_row + downward, :]
            for from_col, from_row in anchors
        ],
        axis=-1,
    )


def dot(left, right, dims="nn"):
    first = 0 if dims[0] == "t" else 1
    second = 1 if dims[1] == "t" else 0
    return lax.dot_general(
        left, right, (((first,), (second,)), ((), ())), preferred_element_type=WIDE
    )


def factored_step(weight, gradient, rows_old, cols_old, row_piece, col_piece, row_mean, weight_mean, sizes):
    decay_rate = 1.0 - STEP ** (-0.8)
    rows_next = decay_rate * rows_old + (1.0 - decay_rate) * row_piece / sizes[1]
    cols_next = decay_rate * cols_old + (1.0 - decay_rate) * col_piece / sizes[0]
    second = rows_next[..., :, None] * cols_next[..., None, :] / row_mean[..., None, None]
    step_rate = RELATIVE * jnp.maximum(RATE_FLOOR, jnp.sqrt(weight_mean))
    weight_next = weight - step_rate[..., None, None] * (gradient * lax.rsqrt(second))
    return (gradient, weight_next, rows_next, cols_next, weight_next.astype(LOW))


def moment_step(parameter, gradient, moment, reduce_axes):
    decay_rate = 1.0 - STEP ** (-0.8)
    moment_next = decay_rate * moment + (1.0 - decay_rate) * gradient * gradient
    rms_value = jnp.sqrt(jnp.mean(parameter * parameter, axis=reduce_axes, keepdims=True))
    return (
        gradient,
        moment_next,
        parameter
        - RELATIVE * jnp.maximum(RATE_FLOOR, rms_value) * gradient * lax.rsqrt(moment_next),
    )


def pack(parts):
    flat = [part.reshape(-1) for part in parts]
    return jnp.concatenate(
        [jnp.pad(part, (0, -part.size % 1024)).reshape(-1, 8, 128) for part in flat]
    )


def unpack(packed, like):
    found, cursor = [], 0
    for part in like:
        tiles = -(-part.size // 1024)
        flat = packed[cursor : cursor + tiles].reshape(-1)
        found.append(flat[: part.size].reshape(part.shape))
        cursor += tiles
    return found


def join(parts):
    return jnp.concatenate([part.reshape(-1) for part in parts])


def split(flat, like):
    found, cursor = [], 0
    for part in like:
        found.append(flat[cursor : cursor + part.size].reshape(part.shape))
        cursor += part.size
    return found


def on_device(
    image, text, cotangent, segments, boxes,
    reduce_weight, reduce_weight_rows, reduce_weight_cols,
    spatial_weight, spatial_weight_rows, spatial_weight_cols,
    expand_weight, expand_weight_rows, expand_weight_cols,
    visual_proj, visual_proj_rows, visual_proj_cols,
    attn_in, attn_in_rows, attn_in_cols,
    attn_out, attn_out_rows, attn_out_cols,
    ffn_up, ffn_up_rows, ffn_up_cols,
    ffn_down, ffn_down_rows, ffn_down_cols,
    norm_params, norm_moment, up_bias, up_moment, tables, table_moment,
):
    dp_count = lax.axis_size(DP)
    pair = lax.axis_size("my")
    mp_count = 2 * pair
    my, core = lax.axis_index("my"), lax.axis_index("core")
    mp_index = lax.axis_index(MP)
    length, width = text.shape[1:]
    quarter = length // mp_count
    heads = tables.shape[2]
    size = width // heads
    group = heads // mp_count
    part = group * size
    units = ffn_up.shape[1]
    pages, across, down, channels = image.shape
    middle = spatial_weight.shape[1]

    flat_in = attn_in.astype(LOW).transpose(2, 0, 1, 3).reshape(attn_in.shape[2], 2, 3 * part)
    flat_out = attn_out.astype(LOW).transpose(2, 0, 1)
    layer_in = [
        jnp.concatenate([flat_in[:, stream], flat_out[:, stream]], axis=1) for stream in range(2)
    ]
    layer_ffn = jnp.concatenate([ffn_up.astype(LOW), ffn_down.astype(LOW).T], axis=1)
    base = visual_proj.shape[0]
    spatial_low = spatial_weight.astype(LOW)
    blocks, extra = divmod(spatial_low.shape[0], base)
    section_low = [spatial_low[n * base : (n + 1) * base] for n in range(blocks)]
    section_low.append(spatial_low[blocks * base :].reshape(base, -1))
    section_low.append(expand_weight.astype(LOW).reshape(base, middle))
    section_low.append(visual_proj.astype(LOW))
    section_low.append(reduce_weight.astype(LOW))
    section_low = jnp.concatenate(section_low, axis=1)
    section_whole = lax.all_gather(section_low, AXES, axis=0, tiled=True)
    ffn_whole = lax.all_gather(layer_ffn, OWNERS, axis=0, tiled=True).reshape(pair, width, -1)
    old_weights = (reduce_weight, spatial_weight, expand_weight, visual_proj, attn_in, attn_out, ffn_up, ffn_down)
    old_rows = (
        reduce_weight_rows, spatial_weight_rows, expand_weight_rows, visual_proj_rows,
        attn_in_rows, attn_out_rows, ffn_up_rows, ffn_down_rows,
    )
    copies = (1, 1, 1, 1, mp_count, dp_count, mp_count, dp_count)
    halves = [Gather(half, (("dz",), ("dx", "my")), OWNERS) for half in layer_in]
    while halves[0].rounds:
        halves[0].step()
    while len(halves[1].rounds) > 1:
        halves[1].step((halves[0].whole,))
    old_parts = [jnp.sum(weight * weight, axis=(-2, -1)) for weight in old_weights]
    old_parts += [jnp.sum(rows, axis=-1) / times for rows, times in zip(old_rows, copies)]
    old_sums = join(old_parts)

    section_whole = section_whole.reshape(dp_count * mp_count, base, -1)
    ends = [blocks * middle, extra * middle // base, middle, width, middle]
    ends = [sum(ends[: n + 1]) for n in range(len(ends))]
    weight_reduce = section_whole[:, :, ends[3] :].reshape(channels, middle)
    first_wait = (halves[0].whole, old_sums)
    reduced = jnp.einsum(
        "pwhc,cd->pwhd",
        tie(image, *first_wait),
        weight_reduce,
        preferred_element_type=WIDE,
    )
    hidden_one = smooth(reduced).astype(LOW)
    beside = extended(tie(hidden_one, halves[1].held), ((DP, 2),), 1)
    halves[1].step((beside,))
    section_whole = tie(section_whole, hidden_one)
    weight_spatial = [section_whole[:, :, n * middle : (n + 1) * middle] for n in range(blocks)]
    weight_spatial.append(
        section_whole[:, :, ends[0] : ends[1]].reshape(dp_count * mp_count, extra, middle)
    )
    weight_spatial = jnp.concatenate(weight_spatial, axis=1).reshape(-1, middle)
    weight_expand = section_whole[:, :, ends[1] : ends[2]].reshape(middle, channels)
    weight_proj = section_whole[:, :, ends[2] : ends[3]].reshape(channels, width)
    padded = extended(beside, ((MP, 1),), 1)
    tap_stack = stacked_taps(tie(padded, weight_spatial), across, down, FORWARD_TAPS)
    convolved = jnp.einsum("pwhk,kd->pwhd", tap_stack, weight_spatial, preferred_element_type=WIDE)
    hidden_two = smooth(convolved).astype(LOW)
    expanded = jnp.einsum("pwhc,cd->pwhd", hidden_two, weight_expand, preferred_element_type=WIDE)
    summed_pre = image.astype(WIDE) + expanded
    feature_low = smooth(summed_pre).astype(LOW)
    visual_rows = jnp.einsum(
        "pwhc,cd->pwhd", feature_low, weight_proj, preferred_element_type=WIDE
    ).astype(LOW)
    attn_text = halves[0].value().reshape(pair, width, 4 * part)

    bucket_select = relative_select(NB, (tables.shape[1] - 1) // 2)
    own_tables = tables.reshape(tables.shape[:2] + (pair, 2, group))
    own_tables = lax.dynamic_index_in_dim(own_tables, core, 3, keepdims=False).reshape(
        tables.shape[:2] + (pair * group,)
    )
    span_tables = jnp.einsum("abr,trh->thab", bucket_select, own_tables, precision=PRECISE)
    head_tables = attention_tables(span_tables)
    page_segments = lax.dynamic_index_in_dim(segments, my, 0, keepdims=False)
    page_boxes = lax.dynamic_index_in_dim(boxes, my, 0, keepdims=False)
    marks = token_marks(page_boxes, page_segments, NB)
    windows = attention_windows(page_segments, CHUNK, TILE)
    segment_cols = jnp.broadcast_to(page_segments[:, None], (length, 128))
    around = (windows, marks, head_tables, segment_cols, page_segments[None])
    text_page = lax.dynamic_index_in_dim(text, my, 0, keepdims=False)
    upstream_page = lax.dynamic_index_in_dim(cotangent, my, 0, keepdims=False)

    weight_up = [ffn_whole[y, :, :units] for y in range(pair)]
    weight_down = [ffn_whole[y, :, units:] for y in range(pair)]

    visual_own = lax.all_to_all(visual_rows, CHIPS, split_axis=0, concat_axis=0, tiled=True)

    text_source = tie(text_page, visual_rows, halves[1].whole)
    weight_in = [[attn_text[y, :, : 3 * part] for y in range(pair)]]
    projected_text = [dot(text_source, weight).astype(LOW) for weight in weight_in[0]]
    attended_text, logs_text = attend_forward(projected_text, around, size)
    attn_visual = halves[1].value().reshape(pair, width, 4 * part)
    weight_in.append([attn_visual[y, :, : 3 * part] for y in range(pair)])
    weight_out = jnp.concatenate(
        [whole[y, :, 3 * part :] for whole in (attn_text, attn_visual) for y in range(pair)], axis=1
    )
    visual_own = (
        tie(visual_own, attended_text)
        .reshape(dp_count, pair, across, down, width)
        .transpose(1, 2, 0, 3, 4)
        .reshape(pair, quarter, width)
    )
    visual_page = by_side(("core", 1), visual_own, swap(visual_own, "core", 1), 1)
    visual_page = visual_page.reshape(length, width)
    projected_visual = [dot(visual_page, weight).astype(LOW) for weight in weight_in[1]]
    attended_visual, logs_visual = attend_forward(projected_visual, around, size)
    attended = jnp.concatenate([attended_text, attended_visual], axis=1)
    attention = dot(attended, weight_out, "nt").astype(LOW)
    hat_one, scale_one, normed_low = row_kernel(
        first_norm_kernel,
        256,
        (text_page, visual_page, attention, swap(attention, "core", 1), norm_params),
        (((length, width), WIDE), ((length, 1), WIDE), ((length, width), LOW)),
    )
    own_bias = lax.dynamic_index_in_dim(up_bias.reshape(pair, 2, units), core, 1, keepdims=False)
    hidden_pre = [dot(normed_low, weight_up[y]) + own_bias[y] for y in range(pair)]
    hidden_low = [smooth(pre).astype(LOW) for pre in hidden_pre]
    down_part = sum(dot(hidden_low[y], weight_down[y], "nt") for y in range(pair)).astype(LOW)
    out_page, second_grad, down_low, second_sums = row_kernel(
        second_norm_kernel,
        256,
        (hat_one, down_part, swap(down_part, "core", 1), upstream_page, norm_params),
        (((length, width), LOW), ((length, width), WIDE), ((length, width), LOW), ((8, width), WIDE)),
    )

    out_own = own_quarters(out_page, quarter).reshape(pair, quarter, width)
    out_got = swap(out_own, "my", 1)

    hidden_grad_low = [
        smooth_back(hidden_pre[y], dot(down_low, weight_down[y])).astype(LOW) for y in range(pair)
    ]
    normed_part = sum(dot(hidden_grad_low[y], weight_up[y], "nt") for y in range(pair)).astype(LOW)
    up_part = jnp.stack([jnp.sum(part_low.astype(WIDE), axis=0) for part_low in hidden_grad_low])
    normed_other = swap(normed_part, "core", 1)
    ffn_parts = []
    for y in range(pair):
        ffn_parts.append(dot(normed_low, hidden_grad_low[y], "tn").astype(LOW))
        ffn_parts.append(dot(down_low, hidden_low[y], "tn").astype(LOW))
    normed_other = tie(normed_other, *ffn_parts)
    ffn_grad = jnp.concatenate(ffn_parts).reshape(pair, 2, dp_count, -1, units)
    ffn_grad = ffn_grad.transpose(0, 2, 1, 3, 4).reshape(-1, units)
    ffn_shard = lax.psum_scatter(ffn_grad, OWNERS, scatter_dimension=0, tiled=True).astype(WIDE)
    first_grad, attention_low, first_sums = row_kernel(
        first_back_kernel,
        256,
        (second_grad, normed_part, normed_other, hat_one, scale_one, norm_params),
        (((length, width), WIDE), ((length, width), LOW), ((8, width), WIDE)),
    )
    norm_part = jnp.concatenate([first_sums[:2], second_sums[:3]])
    norm_part = norm_part * (core == 0).astype(WIDE)
    head_grads = dot(attention_low, weight_out).astype(LOW)
    out_got = tie(out_got, head_grads)
    out_other = swap(out_got, "core", 1)
    grad_out = dot(attention_low, attended, "tn").astype(LOW)

    def attention_grads(stream, source, grads):
        found = []
        for y in range(pair):
            place = (stream * pair + y) * part
            own = [dot(source, grads[y], "tn").astype(LOW), grad_out[:, place : place + part]]
            found.append(jnp.concatenate(own, axis=1))
        return jnp.concatenate(found)

    def source_part(stream, grads):
        return sum(dot(grads[y], weight_in[stream][y], "nt") for y in range(pair))

    visual_back, span_visual = attend_backward(
        projected_visual, around, attended_visual, logs_visual, tie(head_grads, grad_out), 1, size
    )
    first_own = own_quarters(first_grad, quarter)
    visual_own_grad = add_both(source_part(1, visual_back), quarter)
    visual_low = (first_own + visual_own_grad).astype(LOW)
    out_other = by_side(("core", 1), out_got, tie(out_other, visual_low), 1)
    out_local = by_side(("my", 1), out_page.reshape(out_other.shape), out_other, 0)
    out_local = out_local.reshape(text.shape)
    visual_sent = (
        visual_low.reshape(pair, across, dp_count, down, width)
        .transpose(2, 0, 1, 3, 4)
        .reshape(pages, across, down, width)
    )
    visual_grad = lax.all_to_all(visual_sent, CHIPS, split_axis=0, concat_axis=0, tiled=True)
    grad_one = attention_grads(1, tie(visual_page, visual_sent), visual_back)
    sum_one = Scatter([grad_one], (("dx",), ("my",), ("dz",)), OWNERS).send()
    text_grads, span_text = attend_backward(
        projected_text, around, attended_text, logs_text, tie(head_grads, grad_one), 0, size
    )
    grad_text = attention_grads(0, text_page, text_grads)
    sum_two = Scatter([grad_text], (("my",), ("dx",), ("dz",)), OWNERS).send()
    visual_grad = sum_one.land(tie(visual_grad, grad_text))

    feature_grad = jnp.einsum("pwhd,cd->pwhc", visual_grad, weight_proj, preferred_element_type=WIDE)
    pre_grad = smooth_back(summed_pre, feature_grad)
    expanded_low = pre_grad.astype(LOW)
    conv_grad = smooth_back(
        convolved,
        jnp.einsum("pwhd,cd->pwhc", expanded_low, weight_expand, preferred_element_type=WIDE),
    ).astype(LOW)
    back_beside = extended(conv_grad, ((DP, 2),), 1)
    grad_proj = dot(
        feature_low.reshape(-1, channels), tie(visual_grad, conv_grad).reshape(-1, width), "tn"
    ).astype(LOW)
    grad_expand = dot(
        hidden_two.reshape(-1, middle), tie(expanded_low, grad_proj).reshape(-1, channels), "tn"
    )
    grad_expand = grad_expand.astype(LOW).reshape(-1, middle)
    back_beside = sum_two.land(tie(back_beside, grad_expand))
    back_padded = extended(back_beside, ((MP, 1),), 1)
    sum_side = Scatter(
        [grad_expand, grad_proj], (("core",), ("dx",), ("my",), ("dz",)), AXES, 1
    ).send()
    back_padded = sum_one.land(back_padded, False)
    back_taps = stacked_taps(back_padded, across, down, BACKWARD_TAPS).reshape(
        conv_grad.shape[:3] + (9, middle)
    )
    reduced_grad = smooth_back(
        reduced,
        jnp.einsum(
            "pwhko,kio->pwhi",
            back_taps,
            weight_spatial.reshape(9, middle, middle),
            preferred_element_type=WIDE,
        ),
    ).astype(LOW)
    grad_spatial = dot(
        tap_stack.reshape(-1, 9 * middle), sum_side.land(tie(conv_grad, reduced_grad)).reshape(-1, middle), "tn"
    ).astype(LOW)
    grad_reduce = dot(
        image.reshape(-1, channels),
        sum_two.land(tie(reduced_grad, grad_spatial), False).reshape(-1, middle),
        "tn",
    ).astype(LOW)
    sum_last = Scatter(
        [grad_spatial, grad_reduce], (("core",), ("dx", "my"), ("dz",)), AXES
    ).send()
    sum_both = sum_one.merged(sum_two).send()
    reduced_grad = tie(reduced_grad, grad_reduce)
    image_grad_local = pre_grad + jnp.einsum(
        "pwhd,cd->pwhc", reduced_grad, weight_reduce, preferred_element_type=WIDE
    )
    text_grads = [sum_last.land(tie(text_grads[0], image_grad_local))] + list(text_grads[1:])
    text_part = source_part(0, text_grads)
    text_own = first_own + add_both(sum_side.land(text_part), quarter)
    text_back = text_own.reshape(pair, quarter, width)
    text_sent = lax.dynamic_index_in_dim(text_back, 1 - my, 0, keepdims=False)
    text_kept = lax.dynamic_index_in_dim(text_back, my, 0, keepdims=False)
    text_grad_local = by_side(
        ("my", 1), text_kept, swap(text_sent.astype(LOW), "my", 1).astype(WIDE), 0
    )
    while sum_both.rounds:
        sum_both.step(text_own)
    both_shard = sum_both.take(text_own, *sum_last.flying).value()

    (
        reduce_weight, spatial_weight, expand_weight, visual_proj, attn_in, attn_out, ffn_up, ffn_down,
        norm_params, norm_moment, up_bias, up_moment, tables, table_moment,
    ) = lax.optimization_barrier(
        (
            reduce_weight, spatial_weight, expand_weight, visual_proj, attn_in, attn_out, ffn_up, ffn_down,
            norm_params, norm_moment, up_bias, up_moment, tables, table_moment, grad_reduce,
        )
    )[:14]
    up_shard, down_shard = jnp.split(ffn_shard, 2)
    one_shard, two_shard = jnp.split(both_shard, 2)
    in_shard = jnp.stack([two_shard[:, : 3 * part], one_shard[:, : 3 * part]])
    in_shard = in_shard.reshape(2, -1, 3, part).transpose(0, 2, 1, 3)
    out_shard = jnp.stack([two_shard[:, 3 * part :], one_shard[:, 3 * part :]]).transpose(0, 2, 1)
    image_sets = (
        (reduce_weight, reduce_weight_rows, reduce_weight_cols),
        (spatial_weight, spatial_weight_rows, spatial_weight_cols),
        (expand_weight, expand_weight_rows, expand_weight_cols),
        (visual_proj, visual_proj_rows, visual_proj_cols),
    )
    layer_sets = (
        (attn_in, attn_in_rows, attn_in_cols, in_shard, dp_count, mp_count, True),
        (attn_out, attn_out_rows, attn_out_cols, out_shard, mp_count, dp_count, False),
        (ffn_up, ffn_up_rows, ffn_up_cols, up_shard, dp_count, mp_count, True),
        (ffn_down, ffn_down_rows, ffn_down_cols, down_shard.T, mp_count, dp_count, False),
    )
    row_parts = [jnp.sum(entry[3] * entry[3], axis=-1) for entry in layer_sets]
    col_parts = [jnp.sum(entry[3] * entry[3], axis=-2) for entry in layer_sets]
    over_dp = [(cols if entry[6] else rows) for rows, cols, entry in zip(row_parts, col_parts, layer_sets)]
    over_mp = [(rows if entry[6] else cols) for rows, cols, entry in zip(row_parts, col_parts, layer_sets)]
    span_sum = span_text + span_visual
    span_sum = jnp.stack([span_sum[:, :NB, :NB], span_sum[:, NB : 2 * NB, NB : 2 * NB]])
    table_part = jnp.einsum("abr,thba->trh", bucket_select, span_sum, precision=PRECISE)
    table_term = jnp.zeros(tables.shape[:2] + (pair, 2, group), WIDE)
    table_term = lax.dynamic_update_slice(
        table_term, table_part.reshape(tables.shape[:2] + (pair, 1, group)), (0, 0, 0, core, 0)
    ).reshape(tables.shape)
    up_term = lax.dynamic_update_slice(
        jnp.zeros((pair, 2, units), WIDE), up_part[:, None], (0, core, 0)
    ).reshape(up_bias.shape)
    while sum_side.rounds:
        sum_side.step()
    while sum_last.rounds:
        sum_last.step()
    sum_last.take(*row_parts)
    last_shard, side_shard = sum_last.value(), sum_side.take().value()
    spatial_rows = spatial_weight.shape[0]
    image_grads = (
        last_shard[spatial_rows:],
        last_shard[:spatial_rows],
        side_shard[:, :middle].reshape(expand_weight.shape),
        side_shard[:, middle:],
    )
    late = [jnp.sum(gradient * gradient, axis=-2) for gradient in image_grads]
    squares = [jnp.sum(rows, axis=-1) for rows in row_parts]
    over_all = [norm_part, up_term, table_term, old_sums, join(squares)] + late
    packed = pack(over_all)
    summed = total_over(jnp.concatenate([packed, pack(over_dp)]), DP)
    dp_sums = unpack(summed[packed.shape[0] :], over_dp)
    summed = total_over(jnp.concatenate([summed[: packed.shape[0]], pack(over_mp)]), MP)
    mp_sums = unpack(summed[packed.shape[0] :], over_mp)
    sums = unpack(summed, over_all)
    norm_gradient, up_gradient, table_gradient, old_sums, squares_total = sums[:5]
    image_cols = sums[5:]
    old_sums = split(old_sums, old_parts)
    weight_squares, rows_before = old_sums[:8], old_sums[8:]
    squares_total = split(squares_total, squares)

    decay_rate = 1.0 - STEP ** (-0.8)
    layer_results = []
    for number, (weight, rows_old, cols_old, gradient, row_split, col_split, flag) in enumerate(layer_sets):
        sizes = (weight.shape[-2] * row_split, weight.shape[-1] * col_split)
        rows_sum = mp_sums[number] if flag else dp_sums[number]
        cols_sum = dp_sums[number] if flag else mp_sums[number]
        mean = (
            decay_rate * rows_before[4 + number]
            + (1.0 - decay_rate) * squares_total[number] / sizes[1]
        ) / sizes[0]
        layer_results.append(
            factored_step(
                weight, gradient, rows_old, cols_old, rows_sum, cols_sum, mean,
                weight_squares[4 + number] / (sizes[0] * sizes[1]), sizes,
            )
        )
    norm_parts = moment_step(norm_params, norm_gradient, norm_moment, (1,))
    bias_parts = moment_step(up_bias, up_gradient, up_moment, (0,))
    table_parts = moment_step(tables, table_gradient, table_moment, (1, 2))

    image_results = []
    for number, (weight, rows_old, cols_old) in enumerate(image_sets):
        gradient = image_grads[number]
        sizes = (weight.shape[0] * dp_count * mp_count, weight.shape[1])
        rows_sum = jnp.sum(gradient * gradient, axis=-1)
        mean = (
            decay_rate * rows_before[number]
            + (1.0 - decay_rate) * jnp.sum(image_cols[number], axis=-1) / sizes[1]
        ) / sizes[0]
        image_results.append(
            factored_step(
                weight, gradient, rows_old, cols_old, rows_sum, image_cols[number], mean,
                weight_squares[number] / (sizes[0] * sizes[1]), sizes,
            )
        )
    flat = [value for result in image_results + layer_results for value in result]
    return (
        (out_local, text_grad_local, image_grad_local)
        + tuple(flat)
        + norm_parts
        + bias_parts
        + table_parts
    )


def solution(mesh):
    whole = mesh.shape["dp"], mesh.shape["mp"]
    devices = mesh.devices.reshape(whole[0] // 2, 2, whole[1] // 2, 2)
    flat, rows, none = P(AXES, None), P(AXES), P()
    image_weight_in = (flat, rows, none)
    image_weight_out = (flat, flat, rows, none, flat)
    in_spec, in_rows, in_cols = P(None, None, DP, MP), P(None, None, DP), P(None, None, MP)
    out_spec, out_rows, out_cols = P(None, MP, DP), P(None, MP), P(None, DP)
    up_spec, up_rows, up_cols = P(DP, MP), P(DP), P(MP)
    down_spec, down_rows, down_cols = P(MP, DP), P(MP), P(DP)
    placed = (
        (P(None, MP, DP, None), P(DP, None, None), P(DP, None, None), P(DP, None), P(DP, None, None))
        + image_weight_in * 4
        + (in_spec, in_rows, in_cols, out_spec, out_rows, out_cols)
        + (up_spec, up_rows, up_cols, down_spec, down_rows, down_cols)
        + (none,) * 6
    )
    given = (
        (P(DP, None, None), P(DP, MP, None), P(None, MP, DP, None))
        + image_weight_out * 4
        + (in_spec, in_spec, in_rows, in_cols, in_spec)
        + (out_spec, out_spec, out_rows, out_cols, out_spec)
        + (up_spec, up_spec, up_rows, up_cols, up_spec)
        + (down_spec, down_spec, down_rows, down_cols, down_spec)
        + (none,) * 9
    )
    return jax.shard_map(
        on_device, mesh=Mesh(devices, AXES), in_specs=placed, out_specs=given, check_vma=False
    )
```
